32 devices in a mesh: lat: 4 (over x, core), lon: 8 (over z, y).
Axes of the slice: x: 2, y: 2, z: 4, core: 2. Of those that a mesh axis runs over, the one named last changes fastest.
Arguments:
- air_temp: float32 [128, 2880, 128], P('lat', 'lon'), may hold values from -6 to 6
- sea_temp: float32 [128, 2880], P(('lat', 'lon')), may hold values from -6 to 6
- land_sea: int32 [128, 2880], P('lat', 'lon'), may hold values 0 or 1
- courant: float32 [128], replicated, may hold values from -0.4 to 0.4
- vertical_mix: float32 [128, 128], replicated, may hold values from -0.25 to 0.25
- cutoffs: int32 [32], replicated, may hold values from 1 to 127, as said below
Outputs:
- air_final: float32 [128, 2880, 128], P('lat', 'lon')
- sea_final: float32 [128, 2880], P(('lat', 'lon'))
The draws below stay inside these ranges and needn't reach their ends.
Inputs may be any that keep to these rules, and one draw needn't show every extreme that they name: cutoffs holds the rows in the order of the filtered rows; some row keeps exactly 127.
All inputs are finite; a program needn't handle non-finite values. No bound on the sum of `land_sea` on one device may be relied on, other than what follows from the above.
Results may differ from the reference program's by a relative error of at most 0.0001.
Values sent between devices are 32-bit elements; how exact they have to be, the bound alone decides.
No kernel may reach another device: no remote copies, remote signals or barrier semaphores. Data moves between devices by JAX's collectives and lax.ppermute only.
A program may use at most 128 MiB of HBM per device.

```python
import math
import jax
import jax.numpy as jnp
from jax import lax

NLON = 2880
LEVELS = 128
NPOLE = 16
KMAX = 127
STEPS = 6
NLAT = 128


def draw_cutoffs(key, part):
    values = jax.random.randint(jax.random.fold_in(key, 7), (2 * NPOLE,), 1, KMAX + 1)
    return values.at[NPOLE - 1].set(KMAX).astype(jnp.int32)


def plant(result, stream_key, low, high):
    index_at = [jax.random.randint(jax.random.fold_in(stream_key, axis), (), 0, length) for axis, length in enumerate(result.shape)]
    main_axis = result.shape.index(max(result.shape))
    next_to = index_at[:main_axis] + [(index_at[main_axis] + 1) % result.shape[main_axis]] + index_at[main_axis + 1:]
    return result.at[tuple(index_at)].set(low).at[tuple(next_to)].set(high)


def steps_of(own_key, extent, shards, smallest, top_value):
    gain = 1.0
    for position, shards_of in shards:
        draws = jax.random.uniform(jax.random.fold_in(jax.random.fold_in(own_key, 6), position), (shards_of,), jnp.float32, smallest / len(shards), top_value / len(shards))
        gain = gain * jnp.repeat(jnp.exp(draws), extent[position] // shards_of).reshape((-1,) + (1,) * (len(extent) - 1 - position))
    return gain


def noise(own_key, extent, width, most, shards=(), kind=jnp.bfloat16):
    gain = steps_of(own_key, extent, shards, -0.22, 0.18) if shards else 1.0
    result = jax.random.normal(own_key, extent, jnp.float32) * width * gain
    return jnp.minimum(jnp.maximum(result, -most), most).astype(kind)


def setup_inputs(seed: int = 0) -> dict:
    arg_keys = jax.random.split(jax.random.key(seed), 7)
    return {
        "air_temp": noise(arg_keys[0], (NLAT, NLON, LEVELS), 1.0, 6.0, ((0, 4), (1, 8)), jnp.float32),
        "sea_temp": noise(arg_keys[1], (NLAT, NLON), 1.0, 6.0, ((0, 32),), jnp.float32),
        "land_sea": plant((jax.random.randint(arg_keys[2], (NLAT, NLON), 0, 3) < 2).astype(jnp.int32), jax.random.fold_in(arg_keys[2], 1), 0, 1),
        "courant": jnp.clip(jax.random.uniform(arg_keys[3], (LEVELS,), jnp.float32, -0.4, 0.4), -0.4, 0.4),
        "vertical_mix": noise(arg_keys[4], (LEVELS, LEVELS), (4 * LEVELS) ** -0.5, 0.25, (), jnp.float32),
        "cutoffs": draw_cutoffs(jax.random.fold_in(arg_keys[6], 71), 0),
    }


diffusion_rate = 0.1
air_gain = 0.5
ocean_gain = 0.3
ocean_diffusion = 0.2
sea_coef = 0.5
land_coef = 0.15


def horizontal(air_temp, courant):
    zero_row = jnp.zeros_like(air_temp[:1])
    north_cell = jnp.concatenate([zero_row, air_temp[:-1]], 0)
    south_cell = jnp.concatenate([air_temp[1:], zero_row], 0)
    east_cell = jnp.roll(air_temp, -1, axis=1)
    west_cell = jnp.roll(air_temp, 1, axis=1)
    laplace = north_cell + south_cell + east_cell + west_cell - 4.0 * air_temp
    return air_temp + diffusion_rate * laplace - 0.5 * courant * (east_cell - west_cell)


def polar_filter(polar_rows, cutoff):
    wavenum = jnp.arange(KMAX + 1, dtype=jnp.int32)
    columns = jnp.arange(NLON, dtype=jnp.int32)
    phase = ((columns[:, None] * wavenum[None, :]) % NLON).astype(jnp.float32) * (2.0 * math.pi / NLON)
    cosine = jnp.cos(phase)
    sine_table = jnp.sin(phase)
    real_part = jnp.einsum('pcl,ck->pkl', polar_rows, cosine, precision=lax.Precision.HIGHEST)
    imag_part = jnp.einsum('pcl,ck->pkl', polar_rows, sine_table, precision=lax.Precision.HIGHEST)
    weights = jnp.where(wavenum[None, :] <= cutoff[:, None], jnp.where(wavenum[None, :] == 0, 1.0, 2.0), 0.0) / NLON
    weights = weights[:, :, None]
    return (jnp.einsum('pkl,ck->pcl', real_part * weights, cosine, precision=lax.Precision.HIGHEST)
            + jnp.einsum('pkl,ck->pcl', imag_part * weights, sine_table, precision=lax.Precision.HIGHEST))


def reference(air_temp, sea_temp, land_sea, courant, vertical_mix, cutoffs):
    exchange_coef = jnp.where(land_sea == 1, sea_coef, land_coef)
    for step_index in range(STEPS):
        advanced = horizontal(air_temp, courant)
        polar_rows = jnp.concatenate([advanced[:NPOLE], advanced[NLAT - NPOLE:]], 0)
        filtered = polar_filter(polar_rows, cutoffs)
        advanced = advanced.at[:NPOLE].set(filtered[:NPOLE]).at[NLAT - NPOLE:].set(filtered[NPOLE:])
        mixed = jnp.dot(advanced.reshape(-1, LEVELS), vertical_mix, precision=lax.Precision.HIGHEST)
        air_next = advanced + mixed.reshape(advanced.shape)
        heat_flux = exchange_coef * (sea_temp - air_next[:, :, 0])
        air_temp = air_next.at[:, :, 0].add(air_gain * heat_flux)
        zero_row = jnp.zeros_like(sea_temp[:1])
        laplace = (jnp.concatenate([zero_row, sea_temp[:-1]], 0) + jnp.concatenate([sea_temp[1:], zero_row], 0)
                   + jnp.roll(sea_temp, 1, axis=1) + jnp.roll(sea_temp, -1, axis=1) - 4.0 * sea_temp)
        sea_temp = sea_temp - ocean_gain * heat_flux + ocean_diffusion * laplace
    return air_temp, sea_temp
```

```python
import functools
import math

import jax
import jax.numpy as jnp
import ml_dtypes
import numpy as np
from jax import lax
from jax.experimental import pallas as pl
from jax.experimental.pallas import tpu as pltpu
from jax.sharding import PartitionSpec as P

NPOLE = 16
KMAX = 127
STEPS = 6
NK = 2 * (KMAX + 1)
CAP = NPOLE + STEPS
HALO = 8
ROW0 = STEPS
WEDGE = STEPS - 1

diffusion_rate = 0.1
air_gain = 0.5
ocean_gain = 0.3
ocean_diffusion = 0.2
sea_coef = 0.5
land_coef = 0.15

F32 = jnp.float32
BF16 = jnp.bfloat16
VMEM_LIMIT = 56 * 1024 * 1024


def round_up(value, unit):
    return -(-value // unit) * unit


def two_parts(x):
    high = x.astype(BF16)
    return high, (x - high.astype(F32)).astype(BF16)


def dot(a, b):
    return jnp.dot(a, b, preferred_element_type=F32)


def dot_nt(a, b):
    return lax.dot_general(a, b, (((1,), (1,)), ((), ())), preferred_element_type=F32)


def table_dot(high, low, x):
    x_high, x_low = two_parts(x)
    both = dot(high, jnp.concatenate([x_high, x_low], axis=1))
    return both[:, :128] + both[:, 128:] + dot(low, x_high)


def numpy_parts(table):
    high = table.astype(ml_dtypes.bfloat16)
    low = (table - high.astype(np.float64)).astype(ml_dtypes.bfloat16)
    return high, low


@functools.lru_cache(maxsize=None)
def tables(blocks, count, width, depth):
    nlon = blocks * count
    wavenum = np.arange(KMAX + 1)
    weight = np.where(wavenum == 0, 1.0, 2.0) / nlon

    def table(columns):
        phase = (columns[:, None] * wavenum[None, :]) % nlon * (2.0 * math.pi / nlon)
        return np.concatenate([np.cos(phase), np.sin(phase)], 1)

    window = np.concatenate(
        [table((j * count - HALO + np.arange(width)) % nlon) for j in range(blocks)], 0
    )
    forward = np.zeros((blocks, NK, depth))
    for j in range(blocks):
        own = table(j * count + np.arange(count)) * np.tile(weight, 2)
        forward[j, :, :count] = own.T
    return numpy_parts(window), numpy_parts(forward), np.tile(weight, 2)


def lane_iota(shape):
    return lax.broadcasted_iota(jnp.int32, shape, len(shape) - 1)


def spectra_kernel(count, scal, air, high, low, out, padded):
    @pl.when(pl.program_id(0) == 0)
    def _():
        padded[...] = jnp.zeros_like(padded)

    @pl.when(scal[1] == 1)
    def _():
        padded[0:count, :] = air[0]
        out[0] = table_dot(high[...], low[...], padded[...])


def start_spectra(scal, air_temp, high, low):
    rows, count, levels = air_temp.shape
    depth = high.shape[1]

    def place(q, scal):
        return (jnp.where(scal[0] == 1, rows - 1 - q, q), 0, 0)

    return pl.pallas_call(
        functools.partial(spectra_kernel, count),
        out_shape=jax.ShapeDtypeStruct((CAP, NK, levels), F32),
        grid_spec=pltpu.PrefetchScalarGridSpec(
            num_scalar_prefetch=1,
            grid=(CAP,),
            in_specs=[
                pl.BlockSpec((1, count, levels), place),
                pl.BlockSpec((NK, depth), lambda q, scal: (0, 0)),
                pl.BlockSpec((NK, depth), lambda q, scal: (0, 0)),
            ],
            out_specs=pl.BlockSpec((1, NK, levels), lambda q, scal: (q, 0, 0)),
            scratch_shapes=[pltpu.VMEM((depth, levels), F32)],
        ),
        compiler_params=pltpu.CompilerParams(vmem_limit_bytes=VMEM_LIMIT),
        name="start_spectra",
    )(scal, air_temp, high, low)


def advance_row(width, buf, base, north_ref, north, south_ref, south, cour, vcat, adv, xcat, prev):
    c_east, c_west = cour[0:1, :], cour[1:2, :]
    for o in range(0, width, 128):
        here = buf[pl.ds(base + o, 128), :]
        east = buf[pl.ds(base + o + 1, 128), :]
        west = buf[pl.ds(base + o - 1, 128), :]
        around = north_ref[pl.ds(north + o, 128), :] + south_ref[pl.ds(south + o, 128), :]
        x = (
            (1.0 - 4.0 * diffusion_rate) * here
            + diffusion_rate * around
            + c_east * east
            + c_west * west
        )
        high, low = two_parts(x)
        prev[pl.ds(o, 128), :] = here
        adv[pl.ds(o, 128), :] = x
        xcat[pl.ds(o, 128), 0:128] = high
        xcat[pl.ds(o, 128), 128:256] = low
    mixed = dot(xcat[...], vcat[...])
    return adv[...] + mixed[:, :128] + mixed[:, 128:]


def exchange(y, lane, sea, coef):
    back = (128 - lane) % 128
    flux = pltpu.roll(coef, back, 1) * (pltpu.roll(sea, back, 1) - y)
    return jnp.where(lane_iota(y.shape) == 0, flux, 0.0)


def sea_next(width, polar, rows, sea, flux, pad):
    pad[pl.ds(8, width), :] = sea
    east = pad[pl.ds(9, width), :]
    west = pad[pl.ds(7, width), :]
    around = east + west + pltpu.roll(sea, 1, 1) + pltpu.roll(sea, 127, 1)
    new = sea - ocean_gain * flux + ocean_diffusion * (around - 4.0 * sea)
    lane = lane_iota(sea.shape)
    first = jnp.where(polar == 1, ROW0, 0)
    return jnp.where((lane >= first) & (lane < rows + 2 * ROW0), new, 0.0)


def outside_kernel(
    rows, count, width, fast,
    scal, air, west, east, north, south, sea_in, coef, cour, vcat,
    air_out, wedge, side, sea_hist, flux_hist,
    buf, prev, adv, xcat, sea, flux, pad, sems,
):
    flip, polar = scal[0], scal[1]
    total = rows + 2 * ROW0
    inner = count + 2 * HALO

    def base_of(q):
        return pl.multiple_of(8 + (q + ROW0) * width, 8)

    def q_of(r):
        return jnp.where(flip == 1, rows - 1 - r, r)

    buf[0:8, :] = jnp.zeros((8, 128), F32)
    buf[pl.ds(8 + total * width, 8), :] = jnp.zeros((8, 128), F32)
    pad[...] = jnp.zeros_like(pad)

    if fast:
        @pl.loop(0, rows)
        def _(r):
            base = base_of(q_of(r))
            pltpu.make_async_copy(west.at[r], buf.at[pl.ds(base, HALO)], sems.at[0]).start()
            pltpu.make_async_copy(air.at[r], buf.at[pl.ds(base + HALO, count)], sems.at[0]).start()
            pltpu.make_async_copy(
                east.at[r], buf.at[pl.ds(base + HALO + count, HALO)], sems.at[0]
            ).start()

        @pl.loop(0, ROW0)
        def _(r):
            pltpu.make_async_copy(
                north.at[r], buf.at[pl.ds(base_of(q_of(r - ROW0)), inner)], sems.at[0]
            ).start()
            pltpu.make_async_copy(
                south.at[r], buf.at[pl.ds(base_of(q_of(r + rows)), inner)], sems.at[0]
            ).start()

        if inner < width:
            @pl.loop(0, total)
            def _(e):
                buf[pl.ds(base_of(e - ROW0) + inner, width - inner), :] = jnp.zeros(
                    (width - inner, 128), F32
                )

        everything = buf.at[pl.ds(0, total * inner)]
    else:
        @pl.loop(0, total)
        def _(e):
            pltpu.make_async_copy(
                air.at[e], buf.at[pl.ds(base_of(q_of(e - ROW0)), width)], sems.at[0]
            ).start()

        everything = buf.at[pl.ds(0, total * width)]
    pltpu.make_async_copy(everything, everything, sems.at[0]).wait()

    sea[...] = sea_in[...]
    for step in range(1, STEPS + 1):
        lo = jnp.where(polar == 1, NPOLE + step - 1, step - STEPS)
        hi = rows - 1 + STEPS - step
        flux[...] = jnp.zeros_like(flux)
        prev[...] = buf[pl.ds(base_of(lo - 1), width), :]
        if step >= 2:
            side[step - 2] = buf[pl.ds(base_of(lo), width), :]

        @pl.loop(lo, hi + 1)
        def _(q):
            base = base_of(q)
            y = advance_row(
                width, buf, base, prev, 0, buf, base + width, cour, vcat, adv, xcat, prev
            )
            out = exchange(y, q + ROW0, sea[...], coef[...])
            buf[pl.ds(base, width), :] = y + air_gain * out
            flux[...] += pltpu.roll(out, q + ROW0, 1)

        new_sea = sea_next(width, polar, rows, sea[...], flux[...], pad)
        sea[...] = new_sea
        sea_hist[step - 1] = new_sea
        flux_hist[step - 1] = flux[...]

    for j in range(WEDGE):
        wedge[j] = buf[pl.ds(base_of(NPOLE + j), width), :]
    first = jnp.where(polar == 1, NPOLE + WEDGE, 0)
    start, extent = (HALO, count) if fast else (0, width)

    def back(q):
        return pltpu.make_async_copy(
            buf.at[pl.ds(base_of(q) + start, extent)], air_out.at[q_of(q)], sems.at[1]
        )

    @pl.loop(first, rows)
    def _(q):
        back(q).start()

    @pl.when(polar == 1)
    def _():
        whole = buf.at[pl.ds(0, (rows - NPOLE - WEDGE) * extent)]
        pltpu.make_async_copy(whole, whole, sems.at[1]).wait()

    @pl.when(polar == 0)
    def _():
        whole = buf.at[pl.ds(0, rows * extent)]
        pltpu.make_async_copy(whole, whole, sems.at[1]).wait()


def outside_steps(rows, count, width, fast, scal, air, halos, sea, coef, cour, vcat):
    levels = 128
    any_spec = pl.BlockSpec(memory_space=pl.ANY)
    vmem = pl.BlockSpec(memory_space=pltpu.VMEM)
    total = rows + 2 * ROW0
    shape = jax.ShapeDtypeStruct
    return pl.pallas_call(
        functools.partial(outside_kernel, rows, count, width, fast),
        out_shape=[
            shape((rows, count if fast else width, levels), F32),
            shape((WEDGE, width, levels), F32),
            shape((WEDGE, width, levels), F32),
            shape((STEPS, width, 128), F32),
            shape((STEPS, width, 128), F32),
        ],
        in_specs=[pl.BlockSpec(memory_space=pltpu.SMEM)] + [any_spec] * 5 + [vmem] * 4,
        out_specs=[any_spec] + [vmem] * 4,
        scratch_shapes=[
            pltpu.VMEM((total * width + 16, levels), F32),
            pltpu.VMEM((width, levels), F32),
            pltpu.VMEM((width, levels), F32),
            pltpu.VMEM((width, 2 * levels), BF16),
            pltpu.VMEM((width, 128), F32),
            pltpu.VMEM((width, 128), F32),
            pltpu.VMEM((width + 16, 128), F32),
            pltpu.SemaphoreType.DMA((2,)),
        ],
        compiler_params=pltpu.CompilerParams(vmem_limit_bytes=VMEM_LIMIT),
        cost_estimate=pl.CostEstimate(
            flops=STEPS * rows * width * levels * levels * 4,
            bytes_accessed=rows * width * levels * 10,
            transcendentals=0,
        ),
        name="outside_steps",
    )(scal, air, *halos, sea, coef, cour, vcat)


def cap_kernel(
    rows, count, width, blocks, fast, steps,
    scal, spec_in, t_high, t_low, stencil, weight, cour, vcat,
    wedge_in, side, sea_hist, flux_hist, coef, sea_in, flux_in,
    sea_ring_in, coef_ring, ring_flux_in, gathered, air_in,
    *outs_and_scratch,
):
    last = steps[-1] == STEPS
    if last:
        (air_out, sea_out, spec_a, spec_b, cur, prev, adv, xcat, kcat, point, sea, flux, pad, ring,
         sea_ring, shares, back, sems) = outs_and_scratch
    else:
        (spec_out, wedge_out, sea_out, flux_out, sea_ring_out, ring_out, gather_out,
         spec_a, spec_b, cur, prev, adv, xcat, kcat, point, sea, flux, pad, ring,
         sea_ring, shares) = outs_and_scratch
    flip, polar, block = scal[0], scal[1], scal[2]
    lanes = lane_iota((width, 128))
    own = pl.ds(pl.multiple_of(block * width, 128), width)

    def own_dot(x):
        return table_dot(t_high[own, :], t_low[own, :], x)

    def wedge_step(step):
        pending = flux_hist[step - 1]
        for j in range(step - 1):
            base = 8 + j * width
            if j == step - 2:
                south_ref, south = side.at[step - 2], 0
            else:
                south_ref, south = cur, base + width
            y = advance_row(
                width, cur, base, prev, 0, south_ref, south, cour, vcat, adv, xcat, prev
            )
            lane = NPOLE + j + ROW0
            out = exchange(y, lane, sea[...], coef[...])
            cur[pl.ds(base, width), :] = y + air_gain * out
            pending += pltpu.roll(out, lane, 1)
        return pending

    def cap_step(step, src, dst, slot):
        count_rows = CAP - step
        if step > 1:
            for j in range(blocks):
                ring[pl.ds(NPOLE, 8), pl.ds(j * width, width)] = gathered[
                    j, pl.ds(8 * slot, 8), :
                ]
            old, at = sea_ring[...], ring[...]
            place = lax.broadcasted_iota(jnp.int32, old.shape, 0)
            up = jnp.where(place == 0, 0.0, pltpu.roll(old, 1, 0))
            down = pltpu.roll(old, old.shape[0] - 1, 0)
            ring_width = blocks * width
            around = up + down + pltpu.roll(old, 1, 1) + pltpu.roll(old, ring_width - 1, 1)
            sea_ring[...] = old - ocean_gain * at + ocean_diffusion * (around - 4.0 * old)
            spot = lane_iota(at.shape) % width
            at = jnp.where((spot >= HALO) & (spot < HALO + count), at, 0.0)
            high, low = two_parts(at)
            both = dot(jnp.concatenate([high, low], axis=0), t_high[...])
            sums = both[:24] + both[24:] + dot(high, t_low[...])
            sums = sums * (air_gain * weight[0:1, :])
            sums = jnp.concatenate([sums, jnp.zeros((104, NK), F32)], axis=0)
            shares[...] = jnp.transpose(sums)

            @pl.loop(0, count_rows + 1)
            def _(q):
                moved = pltpu.roll(shares[...], lax.rem(128 - q, 128), 1)
                first = lane_iota((NK, 128)) == 0
                src[q + 1] += jnp.where(first, moved, 0.0)

        point[...] = jnp.zeros_like(point)

        @pl.loop(0, count_rows)
        def _(q):
            cut = scal[3 + q]
            for o, other in ((0, 128), (128, 0)):
                here = src[q + 1, pl.ds(o, 128), :]
                swapped = src[q + 1, pl.ds(other, 128), :]
                around = src[q, pl.ds(o, 128), :] + src[q + 2, pl.ds(o, 128), :]
                x = (
                    stencil[0, pl.ds(o, 128), :] * here
                    + diffusion_rate * around
                    + stencil[1, pl.ds(o, 128), :] * swapped
                )
                x = jnp.where(lax.broadcasted_iota(jnp.int32, x.shape, 0) <= cut, x, 0.0)
                high, low = two_parts(x)
                dst[q + 1, pl.ds(o, 128), :] = x
                kcat[pl.ds(o, 128), 0:128] = high
                kcat[pl.ds(o, 128), 128:256] = low
            mixed = dot(kcat[...], vcat[...])
            y = dst[q + 1] + mixed[:, :128] + mixed[:, 128:]
            dst[q + 1] = y
            first = lane_iota((NK, 128)) == 0
            point[...] += pltpu.roll(jnp.where(first, y, 0.0), q, 1)

        at_rows = jnp.transpose(point[...])[:NPOLE]
        high, low = two_parts(at_rows)
        both = dot_nt(jnp.concatenate([high, low], axis=0), t_high[...])
        surface = both[:NPOLE] + both[NPOLE:] + dot_nt(high, t_low[...])
        ring[0:NPOLE, :] = coef_ring[...] * (sea_ring[0:NPOLE, :] - surface)

        here = pltpu.roll(own_dot(point[...]), ROW0, 1)
        in_cap = (lanes >= ROW0) & (lanes < ROW0 + NPOLE)
        total = jnp.where(in_cap, coef[...] * (sea[...] - here), flux[...])
        flux[...] = total
        if step < STEPS:
            edge = pltpu.roll(total, 128 - (ROW0 + NPOLE - 1), 1)
            prev[...] = own_dot(dst[NPOLE]) + air_gain * jnp.where(lanes == 0, edge, 0.0)
        new = sea_next(width, polar, rows, sea[...], total, pad)
        sea[...] = jnp.where(lanes >= ROW0 + NPOLE + step - 1, sea_hist[step - 1], new)

    @pl.when(polar == 1)
    def _():
        spec_a[0] = jnp.zeros((NK, 128), F32)
        spec_b[0] = jnp.zeros((NK, 128), F32)
        spec_a[pl.ds(1, CAP)] = spec_in[...]
        cur[0:8, :] = jnp.zeros((8, 128), F32)
        for j in range(WEDGE):
            cur[pl.ds(8 + j * width, width), :] = wedge_in[j]
        cur[pl.ds(8 + WEDGE * width, 8), :] = jnp.zeros((8, 128), F32)
        pad[...] = jnp.zeros_like(pad)
        sea[...] = sea_in[...]
        flux[...] = flux_in[...]
        ring[0:NPOLE, :] = ring_flux_in[...]
        sea_ring[...] = sea_ring_in[...]
        src, dst = spec_a, spec_b
        for n, step in enumerate(steps):
            cap_step(step, src, dst, n)
            src, dst = dst, src
            if step < STEPS:
                pending = wedge_step(step + 1)
                flux[...] = pending
                if not last:
                    gather_out[pl.ds(8 * n, 8), :] = jnp.transpose(pending)[
                        NPOLE + ROW0 : NPOLE + ROW0 + 8
                    ]
        if last:
            start, extent = (HALO, count) if fast else (0, width)

            def send(ref, offset, q):
                r = jnp.where(flip == 1, rows - 1 - q, q)
                return pltpu.make_async_copy(
                    ref.at[pl.ds(offset + start, extent)], air_out.at[r], sems.at[q]
                )

            for j in range(WEDGE):
                send(cur, 8 + j * width, NPOLE + j).start()

            @pl.loop(0, NPOLE)
            def _(q):
                y = own_dot(src[q + 1])
                edge = pltpu.roll(flux[...], lax.rem(128 - ROW0 - q, 128), 1)
                back[q] = y + air_gain * jnp.where(lanes == 0, edge, 0.0)
                send(back.at[q], 0, q).start()

            @pl.loop(0, NPOLE)
            def _(q):
                send(back.at[q], 0, q).wait()

            for j in range(WEDGE):
                send(cur, 8 + j * width, NPOLE + j).wait()
            sea_out[...] = sea[...]
        else:
            spec_out[...] = src[pl.ds(1, CAP)]
            for j in range(WEDGE):
                wedge_out[j] = cur[pl.ds(8 + j * width, width), :]
            sea_out[...] = sea[...]
            flux_out[...] = flux[...]
            sea_ring_out[...] = sea_ring[...]
            ring_out[...] = ring[0:NPOLE, :]

    if last:
        @pl.when(polar == 0)
        def _():
            sea_out[...] = sea_hist[STEPS - 1]


def cap_steps(rows, count, width, blocks, fast, steps, operands):
    levels = 128
    ring_width = blocks * width
    last = steps[-1] == STEPS
    any_spec = pl.BlockSpec(memory_space=pl.ANY)
    vmem = pl.BlockSpec(memory_space=pltpu.VMEM)
    shape = jax.ShapeDtypeStruct
    if last:
        out_shape = [
            shape((rows, count if fast else width, levels), F32),
            shape((width, 128), F32),
        ]
        out_specs = [any_spec, vmem]
        extra = [pltpu.VMEM((NPOLE, width, levels), F32), pltpu.SemaphoreType.DMA((NPOLE + WEDGE,))]
        aliases = {len(operands) - 1: 0}
    else:
        out_shape = [
            shape((CAP, NK, levels), F32),
            shape((WEDGE, width, levels), F32),
            shape((width, 128), F32),
            shape((width, 128), F32),
            shape((24, ring_width), F32),
            shape((NPOLE, ring_width), F32),
            shape((16, width), F32),
        ]
        out_specs = [vmem] * 7
        extra = []
        aliases = {}
    return pl.pallas_call(
        functools.partial(cap_kernel, rows, count, width, blocks, fast, steps),
        out_shape=out_shape,
        in_specs=[pl.BlockSpec(memory_space=pltpu.SMEM)]
        + [vmem] * (len(operands) - 2)
        + [any_spec],
        out_specs=out_specs,
        scratch_shapes=[
            pltpu.VMEM((CAP + 2, NK, levels), F32),
            pltpu.VMEM((CAP + 2, NK, levels), F32),
            pltpu.VMEM((WEDGE * width + 16, levels), F32),
            pltpu.VMEM((width, levels), F32),
            pltpu.VMEM((width, levels), F32),
            pltpu.VMEM((width, 2 * levels), BF16),
            pltpu.VMEM((NK, 2 * levels), BF16),
            pltpu.VMEM((NK, 128), F32),
            pltpu.VMEM((width, 128), F32),
            pltpu.VMEM((width, 128), F32),
            pltpu.VMEM((width + 16, 128), F32),
            pltpu.VMEM((24, ring_width), F32),
            pltpu.VMEM((24, ring_width), F32),
            pltpu.VMEM((NK, 128), F32),
        ]
        + extra,
        input_output_aliases=aliases,
        compiler_params=pltpu.CompilerParams(vmem_limit_bytes=VMEM_LIMIT),
        cost_estimate=pl.CostEstimate(
            flops=len(steps) * CAP * NK * levels * levels * 4,
            bytes_accessed=20_000_000,
            transcendentals=0,
        ),
        name="cap_steps",
    )(*operands)


def shift(x, axis, by, wrap):
    size = lax.axis_size(axis)
    pairs = [(i, (i + by) % size) for i in range(size) if wrap or 0 <= i + by < size]
    return lax.ppermute(x, axis, pairs)


def to_all(x, blocks):
    copies = jnp.broadcast_to(x[None], (blocks,) + x.shape)
    return lax.all_to_all(copies, "lon", split_axis=0, concat_axis=0, tiled=True)


def local(air_temp, sea_temp, land_sea, courant, vertical_mix, cutoffs):
    rows, count, levels = air_temp.shape
    blocks, bands = lax.axis_size("lon"), lax.axis_size("lat")
    nlon = blocks * count
    width = round_up(count + 2 * HALO, 128)
    depth = round_up(count, 128)
    fast = count % 8 == 0
    band, block = lax.axis_index("lat"), lax.axis_index("lon")
    flip = band == bands - 1
    polar = (band == 0) | flip

    cut = jnp.where(flip, cutoffs[::-1][:NPOLE], cutoffs[:NPOLE])
    head = jnp.stack([flip, polar, block]).astype(jnp.int32)
    scal = jnp.concatenate([head, cut, jnp.full((STEPS + 1,), KMAX, jnp.int32)])
    window, forward, weight = tables(blocks, count, width, depth)
    t_high, t_low = (jnp.asarray(part) for part in window)
    own_high, own_low = (
        lax.dynamic_index_in_dim(jnp.asarray(part), block, 0, keepdims=False) for part in forward
    )
    theta = np.arange(KMAX + 1) * (2.0 * math.pi / nlon)
    cosine = np.tile(np.cos(theta), 2).astype(np.float32)
    sine = np.concatenate([-np.sin(theta), np.sin(theta)]).astype(np.float32)
    stay = 1.0 - 4.0 * diffusion_rate + 2.0 * diffusion_rate * jnp.asarray(cosine)
    stencil = jnp.stack(
        [
            jnp.broadcast_to(stay[:, None], (NK, levels)),
            (2.0 * 0.5) * jnp.asarray(sine)[:, None] * courant[None, :],
        ]
    )
    weights = jnp.broadcast_to(jnp.asarray(weight.astype(np.float32))[None], (8, NK))
    cour = jnp.stack([diffusion_rate - 0.5 * courant, diffusion_rate + 0.5 * courant])
    cour = jnp.concatenate([cour, jnp.zeros((6, levels), F32)], 0)
    v_round = lax.reduce_precision(vertical_mix, 8, 7)
    v_high, v_low = v_round.astype(BF16), (vertical_mix - v_round).astype(BF16)
    vcat = jnp.concatenate(
        [
            jnp.concatenate([v_high, v_low], 1),
            jnp.concatenate([v_high, jnp.zeros_like(v_low)], 1),
        ],
        0,
    )

    spec = start_spectra(scal, air_temp, own_high, own_low)
    spec = lax.psum(spec, "lon")

    west = shift(air_temp[:, count - HALO :], "lon", 1, True)
    east = shift(air_temp[:, :HALO], "lon", -1, True)

    def edge(part):
        return jnp.concatenate([west[part], air_temp[part], east[part]], 1)

    north = shift(edge(slice(rows - ROW0, rows)), "lat", 1, False)
    south = shift(edge(slice(0, ROW0)), "lat", -1, False)

    exchange_coef = jnp.where(land_sea == 1, sea_coef, land_coef).astype(F32)
    sea_band = lax.all_gather(sea_temp, "lon", axis=0, tiled=True)
    coef_band = lax.all_gather(exchange_coef, "lon", axis=1, tiled=True)
    pair = jnp.stack([sea_band, coef_band])
    above = shift(pair[:, rows - ROW0 :], "lat", 1, False)
    below = shift(pair[:, :ROW0], "lat", -1, False)
    pair = jnp.concatenate([above, pair, below], 1)
    pair = jnp.where(flip, pair[:, ::-1], pair)
    around = jnp.concatenate([pair[:, :, nlon - HALO :], pair, pair[:, :, : width]], 2)
    ring = jnp.concatenate(
        [around[:, ROW0 : ROW0 + 24, j * count : j * count + width] for j in range(blocks)], 2
    )
    mine = lax.dynamic_slice_in_dim(around, block * count, width, 2)
    mine = jnp.pad(mine.transpose(0, 2, 1), ((0, 0), (0, 0), (0, 128 - rows - 2 * ROW0)))
    sea, coef = mine[0], mine[1]
    sea_ring, coef_ring = ring[0], ring[1, :NPOLE]

    if fast:
        air = air_temp
    else:
        middle = jnp.concatenate([west, air_temp, east], 1)
        air = jnp.concatenate([north, middle, south], 0)
        air = jnp.pad(air, ((0, 0), (0, width - count - 2 * HALO), (0, 0)))
    halos = (west, east, north, south)
    air, wedge, side, sea_hist, flux_hist = outside_steps(
        rows, count, width, fast, scal, air, halos, sea, coef, cour, vcat
    )

    flux = flux_hist[0]
    first = NPOLE + ROW0
    gathered = jnp.zeros((16, width), F32).at[8:].set(flux[:, first : first + 8].T)
    gathered = lax.all_gather(gathered, "lon", axis=0, tiled=False)
    ring_flux = jnp.zeros((NPOLE, blocks * width), F32)
    for steps in ((1, 2), (3, 4), (5, 6)):
        operands = (
            scal, spec, t_high, t_low, stencil, weights, cour, vcat,
            wedge, side, sea_hist, flux_hist, coef, sea, flux,
            sea_ring, coef_ring, ring_flux, gathered, air,
        )
        outs = cap_steps(rows, count, width, blocks, fast, steps, operands)
        if steps[-1] < STEPS:
            spec, wedge, sea, flux, sea_ring, ring_flux, mine = outs
            gathered = to_all(mine, blocks).reshape(blocks, 16, width)
    air, sea = outs
    if not fast:
        air = air[:, HALO : HALO + count]
    sea = sea[HALO : HALO + count, ROW0 : ROW0 + rows].T
    sea = jnp.where(flip, sea[::-1], sea)
    sea = lax.all_to_all(sea, "lon", split_axis=0, concat_axis=1, tiled=True)
    return air, sea


def solution(mesh):
    placed = (P("lat", "lon", None), P(("lat", "lon"), None), P("lat", "lon"), P(), P(), P())
    return jax.shard_map(
        local,
        mesh=mesh,
        in_specs=placed,
        out_specs=(P("lat", "lon", None), P(("lat", "lon"), None)),
        check_vma=False,
    )
```

```python
import functools
import math

import jax
import jax.numpy as jnp
import ml_dtypes
import numpy as np
from jax import lax
from jax.experimental import pallas as pl
from jax.experimental.pallas import tpu as pltpu
from jax.sharding import PartitionSpec as P

NPOLE = 16
KMAX = 127
STEPS = 6
NK = 2 * (KMAX + 1)
CAP = NPOLE + STEPS
HALO = 8
ROW0 = STEPS
WEDGE = STEPS - 1

diffusion_rate = 0.1
air_gain = 0.5
ocean_gain = 0.3
ocean_diffusion = 0.2
sea_coef = 0.5
land_coef = 0.15

F32 = jnp.float32
BF16 = jnp.bfloat16
VMEM_LIMIT = 56 * 1024 * 1024


def round_up(value, unit):
    return -(-value // unit) * unit


def two_parts(x):
    high = x.astype(BF16)
    return high, (x - high.astype(F32)).astype(BF16)


def dot(a, b):
    return jnp.dot(a, b, preferred_element_type=F32)


def dot_nt(a, b):
    return lax.dot_general(a, b, (((1,), (1,)), ((), ())), preferred_element_type=F32)


def table_dot(high, low, x):
    x_high, x_low = two_parts(x)
    both = dot(high, jnp.concatenate([x_high, x_low], axis=1))
    return both[:, :128] + both[:, 128:] + dot(low, x_high)


def numpy_parts(table):
    high = table.astype(ml_dtypes.bfloat16)
    low = (table - high.astype(np.float64)).astype(ml_dtypes.bfloat16)
    return high, low


@functools.lru_cache(maxsize=None)
def tables(blocks, count, width, depth):
    nlon = blocks * count
    wavenum = np.arange(KMAX + 1)
    weight = np.where(wavenum == 0, 1.0, 2.0) / nlon

    def table(columns):
        phase = (columns[:, None] * wavenum[None, :]) % nlon * (2.0 * math.pi / nlon)
        return np.concatenate([np.cos(phase), np.sin(phase)], 1)

    window = np.concatenate(
        [table((j * count - HALO + np.arange(width)) % nlon) for j in range(blocks)], 0
    )
    forward = np.zeros((blocks, NK, depth))
    for j in range(blocks):
        own = table(j * count + np.arange(count)) * np.tile(weight, 2)
        forward[j, :, :count] = own.T
    high, low = numpy_parts(forward)
    return numpy_parts(window), np.concatenate([high, high, low], 2), np.tile(weight, 2)


def lane_iota(shape):
    return lax.broadcasted_iota(jnp.int32, shape, len(shape) - 1)


def spectra_kernel(count, blocks, scal, air, table, keep, send, stacked, sums):
    depth = stacked.shape[0] // 3
    half, part = blocks // 2, NK // blocks
    flip, block = scal[0], scal[2]
    side, place = lax.rem(block, 2), block // 2

    @pl.when(pl.program_id(0) == 0)
    def _():
        stacked[...] = jnp.zeros_like(stacked)

    @pl.when(scal[1] == 1)
    def _():
        for n in range(2):
            high, low = two_parts(air[n])
            lanes = slice(128 * n, 128 * n + 128)
            stacked[0:count, lanes] = high
            stacked[depth : depth + count, lanes] = low
            stacked[2 * depth : 2 * depth + count, lanes] = high
        sums[...] = dot(table[...], stacked[...])
        for n in range(2):
            to = jnp.where(flip == 1, 1 - n, n)
            lanes = slice(128 * n, 128 * n + 128)
            for z in range(half):
                at = jnp.bitwise_xor(place, z)
                mine = pl.multiple_of((side * half + z) * part, part)
                other = pl.multiple_of(((1 - side) * half + z) * part, part)
                keep[at, to] = sums[pl.ds(mine, part), lanes]
                send[at, to] = sums[pl.ds(other, part), lanes]


def start_spectra(blocks, scal, air_temp, table):
    rows, count, levels = air_temp.shape
    half, part = blocks // 2, NK // blocks
    depth = table.shape[1] // 3

    def place(p, scal):
        return (jnp.where(scal[0] == 1, rows // 2 - 1 - p, p), 0, 0)

    out = jax.ShapeDtypeStruct((half, CAP, part, levels), F32)
    out_spec = pl.BlockSpec((half, 2, part, levels), lambda p, scal: (0, p, 0, 0))
    return pl.pallas_call(
        functools.partial(spectra_kernel, count, blocks),
        out_shape=[out, out],
        grid_spec=pltpu.PrefetchScalarGridSpec(
            num_scalar_prefetch=1,
            grid=(CAP // 2,),
            in_specs=[
                pl.BlockSpec((2, count, levels), place),
                pl.BlockSpec((NK, 3 * depth), lambda p, scal: (0, 0)),
            ],
            out_specs=[out_spec, out_spec],
            scratch_shapes=[
                pltpu.VMEM((3 * depth, 2 * levels), BF16),
                pltpu.VMEM((NK, 2 * levels), F32),
            ],
        ),
        compiler_params=pltpu.CompilerParams(vmem_limit_bytes=VMEM_LIMIT // 2),
        name="start_spectra",
    )(scal, air_temp, table)


def advance(
    width, here_ref, base, north_ref, north, south_ref, south, cour, adv, xcat, more=None
):
    c_east, c_west = cour[0:1, :], cour[1:2, :]
    for o in range(0, width, 128):
        around = north_ref[pl.ds(north + o, 128), :] + south_ref[pl.ds(south + o, 128), :]
        x = (
            (1.0 - 4.0 * diffusion_rate) * here_ref[pl.ds(base + o, 128), :]
            + diffusion_rate * around
            + c_east * here_ref[pl.ds(base + o + 1, 128), :]
            + c_west * here_ref[pl.ds(base + o - 1, 128), :]
        )
        if more is not None:
            moved = pltpu.roll(more[0][pl.ds(o, 128), :], more[1], 1)
            x += jnp.where(lane_iota(x.shape) == 0, moved, 0.0)
        high, low = two_parts(x)
        adv[pl.ds(o, 128), :] = x
        xcat[pl.ds(o, 128), 0:128] = high
        xcat[pl.ds(o, 128), 128:256] = low


def two_at_a_time(first, pairs, load, finish):
    load(first, 0)

    @pl.loop(0, pairs)
    def _(n):
        q = first + 2 * n
        finish(q, 0, lambda: load(q + 1, 1))
        finish(q + 1, 1, lambda: load(q + 2, 0))


def exchange(y, lane, sea, coef):
    back = (128 - lane) % 128
    flux = pltpu.roll(coef, back, 1) * (pltpu.roll(sea, back, 1) - y)
    return jnp.where(lane_iota(y.shape) == 0, flux, 0.0)


def sea_next(width, polar, rows, sea, flux, pad):
    pad[pl.ds(8, width), :] = sea
    east = pad[pl.ds(9, width), :]
    west = pad[pl.ds(7, width), :]
    around = east + west + pltpu.roll(sea, 1, 1) + pltpu.roll(sea, 127, 1)
    new = sea - ocean_gain * flux + ocean_diffusion * (around - 4.0 * sea)
    lane = lane_iota(sea.shape)
    first = jnp.where(polar == 1, ROW0, 0)
    return jnp.where((lane >= first) & (lane < rows + 2 * ROW0), new, 0.0)


def windows_kernel(rows, count, width, blocks, scal, got, own, ring_sea, ring_coef, wide):
    per = rows // blocks
    for j in range(blocks):
        columns = slice(j * width + HALO, j * width + HALO + count)
        for i in range(blocks):
            wide[0, per * i : per * (i + 1), columns] = got[i, per * j : per * (j + 1), :]
        wide[1, :, columns] = got[j, rows:, :]
    rest = width - HALO - count
    for j in range(blocks):
        before = ((j - 1) % blocks) * width + count
        after = ((j + 1) % blocks) * width + HALO
        end = j * width + HALO + count
        wide[:, :, j * width : j * width + HALO] = wide[:, :, before : before + HALO]
        wide[:, :, end : end + rest] = wide[:, :, after : after + rest]
    own[...] = wide[:, :, pl.ds(pl.multiple_of(scal[2] * width, 128), width)]

    @pl.when(scal[1] == 1)
    def _():
        @pl.loop(0, 24)
        def _(q):
            r = jnp.where(scal[0] == 1, rows - 1 - q, q)
            ring_sea[pl.ds(q, 1), :] = wide[0, pl.ds(r, 1), :]

        @pl.loop(0, NPOLE)
        def _(q):
            r = jnp.where(scal[0] == 1, rows - 1 - q, q)
            ring_coef[pl.ds(q, 1), :] = wide[1, pl.ds(r, 1), :]


def windows(rows, count, width, blocks, scal, got):
    vmem = pl.BlockSpec(memory_space=pltpu.VMEM)
    shape = jax.ShapeDtypeStruct
    return pl.pallas_call(
        functools.partial(windows_kernel, rows, count, width, blocks),
        out_shape=[
            shape((2, rows, width), F32),
            shape((24, blocks * width), F32),
            shape((NPOLE, blocks * width), F32),
        ],
        in_specs=[pl.BlockSpec(memory_space=pltpu.SMEM), vmem],
        out_specs=[vmem] * 3,
        scratch_shapes=[pltpu.VMEM((2, rows, blocks * width), F32)],
        compiler_params=pltpu.CompilerParams(vmem_limit_bytes=VMEM_LIMIT // 2),
        name="windows",
    )(scal, got)


def outside_kernel(rows, count, width, fast, steps, scal, *refs):
    first, last = steps[0] == 1, steps[-1] == STEPS
    if first:
        (air, west, east, north, south, own, above, below, cour, vcat), refs = refs[:10], refs[10:]
        (state, wedge, side, sea_hist, flux_hist, sea_start, coef, gather_out), refs = (
            refs[:8], refs[8:])
    else:
        (state, sea_hist_in, flux_hist_in, coef, cour, vcat), refs = refs[:6], refs[6:]
        (air_out, wedge, side, sea_hist, flux_hist), refs = refs[:5], refs[5:]
    (buf_a, buf_b, adv_a, adv_b, xcat_a, xcat_b, sea, flux, point, more, turn, pad, sems) = refs
    flip, polar = scal[0], scal[1]
    total = rows + 2 * ROW0
    inner = count + 2 * HALO
    lanes = lane_iota((width, 128))

    def base_of(q):
        return pl.multiple_of(8 + (q + ROW0) * width, 8)

    def q_of(r):
        return jnp.where(flip == 1, rows - 1 - r, r)

    def low_row(step):
        return jnp.where(polar == 1, NPOLE + step - 1, step - STEPS)

    def row_range(body, step, *sizes):
        hi = rows - 1 + STEPS - step
        ref, extent, sem = sizes

        @pl.loop(low_row(step), hi + 1)
        def _(q):
            body(q).start()

        for kind, count_rows in ((1, hi + 1 - NPOLE - step + 1), (0, hi + 1 + STEPS - step)):
            @pl.when(polar == kind)
            def _(count_rows=count_rows):
                whole = ref.at[pl.ds(0, count_rows * extent)]
                pltpu.make_async_copy(whole, whole, sem).wait()

    def begin():
        beyond = 8 + total * width
        for ref in (buf_a, buf_b):
            ref[0:8, :] = jnp.zeros((8, 128), F32)
            ref[pl.ds(beyond, 3 * width + 8), :] = jnp.zeros((3 * width + 8, 128), F32)
        pad[...] = jnp.zeros_like(pad)

    if first:
        if fast:
            @pl.loop(0, rows)
            def _(r):
                base = base_of(q_of(r))
                for ref, offset, size in (
                    (west, 0, HALO), (air, HALO, count), (east, HALO + count, HALO)
                ):
                    pltpu.make_async_copy(
                        ref.at[r], buf_a.at[pl.ds(base + offset, size)], sems.at[0]
                    ).start()

            @pl.loop(0, ROW0)
            def _(r):
                for ref, at in ((north, r - ROW0), (south, r + rows)):
                    pltpu.make_async_copy(
                        ref.at[r], buf_a.at[pl.ds(base_of(q_of(at)), inner)], sems.at[0]
                    ).start()

            if inner < width:
                @pl.loop(0, total)
                def _(e):
                    buf_a[pl.ds(base_of(e - ROW0) + inner, width - inner), :] = jnp.zeros(
                        (width - inner, 128), F32
                    )

            everything = buf_a.at[pl.ds(0, total * inner)]
        else:
            @pl.loop(0, total)
            def _(e):
                pltpu.make_async_copy(
                    air.at[e], buf_a.at[pl.ds(base_of(q_of(e - ROW0)), width)], sems.at[0]
                ).start()

            everything = buf_a.at[pl.ds(0, total * width)]
        begin()
        for n, ref in ((0, sea), (1, coef)):
            turn[...] = jnp.zeros_like(turn)
            for source, size, at in ((above, ROW0, -ROW0), (own, rows, 0), (below, ROW0, rows)):
                @pl.loop(0, size)
                def _(r, source=source, at=at):
                    turn[pl.ds(q_of(r + at) + ROW0, 1), :] = source[n, pl.ds(r, 1), :]

            ref[...] = jnp.transpose(turn[...])
        sea_start[...] = sea[...]
        pltpu.make_async_copy(everything, everything, sems.at[0]).wait()
    else:
        begin()
        sea[...] = sea_hist_in[steps[0] - 2]
        flux[...] = flux_hist_in[steps[0] - 2]
        row_range(
            lambda q: pltpu.make_async_copy(
                state.at[q + ROW0], buf_a.at[pl.ds(base_of(q), width)], sems.at[0]
            ),
            steps[0] - 1, buf_a, width, sems.at[0],
        )

    def with_flux(y, q):
        gain = air_gain * pltpu.roll(flux[...], 128 - (q + ROW0), 1)
        return y + jnp.where(lanes == 0, gain, 0.0)

    advs, xcats = (adv_a, adv_b), (xcat_a, xcat_b)
    src, dst = buf_a, buf_b
    for n, step in enumerate(steps):
        lo = low_row(step)
        hi = rows - 1 + STEPS - step
        pairs = jnp.where(polar == 1, (hi - NPOLE - step + 3) // 2, (hi + 1 + STEPS - step) // 2)
        if step > 1:
            gain = air_gain * flux[...]
            pad[pl.ds(8, width), :] = gain
            more[...] = (
                (1.0 - 4.0 * diffusion_rate) * gain
                + diffusion_rate * (pltpu.roll(gain, 1, 1) + pltpu.roll(gain, 127, 1))
                + cour[2:3, :] * pad[pl.ds(9, width), :]
                + cour[3:4, :] * pad[pl.ds(7, width), :]
            )
        point[...] = jnp.zeros_like(point)

        def load(q, slot, src=src, step=step):
            base = base_of(q)
            advance(width, src, base, src, base - width, src, base + width, cour,
                    advs[slot], xcats[slot], (more, 128 - (q + ROW0)) if step > 1 else None)

        def finish(q, slot, between, dst=dst):
            mixed = dot(xcats[slot][...], vcat[...])
            between()
            y = advs[slot][...] + mixed[:, :128] + mixed[:, 128:]
            dst[pl.ds(base_of(q), width), :] = y
            point[...] += pltpu.roll(jnp.where(lanes == 0, y, 0.0), q + ROW0, 1)

        two_at_a_time(lo, pairs, load, finish)

        total_flux = jnp.where(lanes >= lo + ROW0, coef[...] * (sea[...] - point[...]), 0.0)
        flux[...] = total_flux
        new_sea = sea_next(width, polar, rows, sea[...], total_flux, pad)
        sea[...] = new_sea
        sea_hist[n] = new_sea
        flux_hist[n] = total_flux
        if step <= WEDGE:
            @pl.when(polar == 1)
            def _(dst=dst, step=step, n=n):
                for ref, q in ((wedge, NPOLE + step - 1), (side, NPOLE + step)):
                    ref[n] = with_flux(dst[pl.ds(base_of(q), width), :], q)
        src, dst = dst, src

    if first:
        state_rows = row_range(
            lambda q: pltpu.make_async_copy(
                src.at[pl.ds(base_of(q), width)], state.at[q + ROW0], sems.at[1]
            ),
            steps[-1], src, width, sems.at[1],
        )
        turned = jnp.transpose(flux_hist[0])[NPOLE + ROW0 : NPOLE + ROW0 + 8]
        gather_out[...] = jnp.concatenate([jnp.zeros_like(turned), turned], axis=0)
    else:
        start, extent = (HALO, count) if fast else (0, width)
        first_row = jnp.where(polar == 1, NPOLE + WEDGE, 0)

        @pl.loop(first_row, rows)
        def _(q):
            row = pl.ds(base_of(q), width)
            src[row, :] = with_flux(src[row, :], q)
            pltpu.make_async_copy(
                src.at[pl.ds(base_of(q) + start, extent)], air_out.at[q_of(q)], sems.at[1]
            ).start()

        for kind, count_rows in ((1, rows - NPOLE - WEDGE), (0, rows)):
            @pl.when(polar == kind)
            def _(count_rows=count_rows):
                whole = src.at[pl.ds(0, count_rows * extent)]
                pltpu.make_async_copy(whole, whole, sems.at[1]).wait()


def outside_steps(rows, count, width, fast, steps, scal, big, small):
    levels = 128
    any_spec = pl.BlockSpec(memory_space=pl.ANY)
    vmem = pl.BlockSpec(memory_space=pltpu.VMEM)
    total = rows + 2 * ROW0
    shape = jax.ShapeDtypeStruct
    square = shape((width, 128), F32)
    hist = [shape((len(steps), width, 128), F32)] * 4
    if steps[0] == 1:
        out_shape = [shape((total, width, levels), F32)] + hist + [square, square]
        out_shape.append(shape((16, width), F32))
    else:
        out_shape = [shape((rows, count if fast else width, levels), F32)] + hist
    return pl.pallas_call(
        functools.partial(outside_kernel, rows, count, width, fast, steps),
        out_shape=out_shape,
        in_specs=[pl.BlockSpec(memory_space=pltpu.SMEM)]
        + [any_spec] * len(big)
        + [vmem] * len(small),
        out_specs=[any_spec] + [vmem] * (len(out_shape) - 1),
        scratch_shapes=[
            pltpu.VMEM(((total + 3) * width + 16, levels), F32),
            pltpu.VMEM(((total + 3) * width + 16, levels), F32),
            pltpu.VMEM((width, levels), F32),
            pltpu.VMEM((width, levels), F32),
            pltpu.VMEM((width, 2 * levels), BF16),
            pltpu.VMEM((width, 2 * levels), BF16),
            pltpu.VMEM((width, 128), F32),
            pltpu.VMEM((width, 128), F32),
            pltpu.VMEM((width, 128), F32),
            pltpu.VMEM((width, 128), F32),
            pltpu.VMEM((128, width), F32),
            pltpu.VMEM((width + 16, 128), F32),
            pltpu.SemaphoreType.DMA((2,)),
        ],
        compiler_params=pltpu.CompilerParams(vmem_limit_bytes=VMEM_LIMIT),
        cost_estimate=pl.CostEstimate(
            flops=len(steps) * rows * width * levels * levels * 4,
            bytes_accessed=rows * width * levels * 10,
            transcendentals=0,
        ),
        name="outside_steps",
    )(scal, *big, *small)


def cap_kernel(rows, count, width, blocks, fast, steps, parts, scal, *refs):
    last = steps[-1] == STEPS
    wedge_steps = [step + 1 for step in steps if step < STEPS]
    spec_in, refs = refs[:parts], refs[parts:]
    hists, refs = refs[: 4 * len(cap_hists(steps))], refs[4 * len(cap_hists(steps)) :]
    names = ["t_high", "t_low", "stencil", "coef", "sea", "sea_ring", "coef_ring", "gathered"]
    if steps[0] > 1:
        names += ["flux", "ring_flux", "wedge"]
    loads = dict(zip(names, refs[: len(names)]))
    refs = refs[len(names) :]
    weight, cour, vcat = refs[:3]
    refs = refs[3:]
    if last:
        refs = refs[1:]
        (air_out, sea_out), refs = refs[:2], refs[2:]
    else:
        (spec_out, wedge_out, sea_out, flux_out, sea_ring_out, ring_out, gather_out), refs = (
            refs[:7], refs[7:])
    (spec_a, spec_b, cur, prev, adv, xcat, kcat_a, kcat_b, kadv_a, kadv_b, point, sea, flux, pad,
     ring, sea_ring, shares, t_high, t_low, stencil, coef, coef_ring, gathered, sea_hist,
     flux_hist, side, turn, load_sems) = refs[:28]
    if last:
        back, sems = refs[28:]
    flip, polar, block = scal[0], scal[1], scal[2]
    lanes = lane_iota((width, 128))
    own = pl.ds(pl.multiple_of(block * width, 128), width)

    def hist(kind, step):
        at = cap_hists(steps).index(0 if step <= 3 else 1)
        return hists[4 * at + kind].at[(step - 1) % 3]

    def own_dot(x):
        return table_dot(t_high[own, :], t_low[own, :], x)

    def wedge_step(step):
        at = wedge_steps.index(step)
        pending = flux_hist[at]
        for j in range(step - 1):
            base = 8 + j * width
            if j == step - 2:
                south_ref, south = side.at[at], 0
            else:
                south_ref, south = cur, base + width
            advance(width, cur, base, prev, 0, south_ref, south, cour, adv, xcat)
            prev[...] = cur[pl.ds(base, width), :]
            mixed = dot(xcat[...], vcat[...])
            y = adv[...] + mixed[:, :128] + mixed[:, 128:]
            lane = NPOLE + j + ROW0
            out = exchange(y, lane, sea[...], coef[...])
            cur[pl.ds(base, width), :] = y + air_gain * out
            pending += pltpu.roll(out, lane, 1)
        return pending

    def cap_step(step, src, dst, slot):
        count_rows = CAP - step
        if step > 1:
            ready("gathered", "t_high", "t_low", "stencil", "sea_ring", "ring_flux")
        if step > 1:
            for j in range(blocks):
                ring[pl.ds(NPOLE, 8), pl.ds(j * width, width)] = gathered[
                    j, pl.ds(8 * slot, 8), :
                ]
            old, at = sea_ring[...], ring[...]
            place = lax.broadcasted_iota(jnp.int32, old.shape, 0)
            up = jnp.where(place == 0, 0.0, pltpu.roll(old, 1, 0))
            down = pltpu.roll(old, old.shape[0] - 1, 0)
            ring_width = blocks * width
            around = up + down + pltpu.roll(old, 1, 1) + pltpu.roll(old, ring_width - 1, 1)
            sea_ring[...] = old - ocean_gain * at + ocean_diffusion * (around - 4.0 * old)
            spot = lane_iota(at.shape) % width
            at = jnp.where((spot >= HALO) & (spot < HALO + count), at, 0.0)
            high, low = two_parts(at)
            both = dot(jnp.concatenate([high, low], axis=0), t_high[...])
            sums = both[:24] + both[24:] + dot(high, t_low[...])
            sums = sums * (air_gain * weight[0:1, :])
            sums = jnp.concatenate([sums, jnp.zeros((104, NK), F32)], axis=0)
            moved = jnp.transpose(sums)
            swapped = jnp.concatenate([moved[128:], moved[:128]], axis=0)
            beside = pltpu.roll(moved, 1, 1) + pltpu.roll(moved, 127, 1)
            shares[...] = stencil[0] * moved + diffusion_rate * beside + stencil[2] * swapped

        ready("spec", "stencil")
        point[...] = jnp.zeros_like(point)
        kcats, kadvs = (kcat_a, kcat_b), (kadv_a, kadv_b)
        first = lane_iota((128, 128)) == 0

        def load(q, slot):
            cut = scal[3 + q]
            for o, other in ((0, 128), (128, 0)):
                here = src[q + 1, pl.ds(o, 128), :]
                swapped = src[q + 1, pl.ds(other, 128), :]
                around = src[q, pl.ds(o, 128), :] + src[q + 2, pl.ds(o, 128), :]
                x = (
                    stencil[0, pl.ds(o, 128), :] * here
                    + diffusion_rate * around
                    + stencil[1, pl.ds(o, 128), :] * swapped
                )
                if step > 1:
                    more = pltpu.roll(shares[pl.ds(o, 128), :], lax.rem(128 - q, 128), 1)
                    x += jnp.where(first, more, 0.0)
                x = jnp.where(lax.broadcasted_iota(jnp.int32, x.shape, 0) <= cut, x, 0.0)
                high, low = two_parts(x)
                kadvs[slot][pl.ds(o, 128), :] = x
                kcats[slot][pl.ds(o, 128), 0:128] = high
                kcats[slot][pl.ds(o, 128), 128:256] = low

        def finish(q, slot, between):
            mixed = dot(kcats[slot][...], vcat[...])
            between()
            y = kadvs[slot][...] + mixed[:, :128] + mixed[:, 128:]
            dst[q + 1] = y
            point[...] += pltpu.roll(jnp.where(lane_iota(y.shape) == 0, y, 0.0), q, 1)

        two_at_a_time(0, (count_rows + 1) // 2, load, finish)

        ready("t_high", "t_low", "sea_ring", "coef_ring", "coef", "sea", "flux", "hist")
        at_rows = jnp.transpose(point[...])[:NPOLE]
        high, low = two_parts(at_rows)
        both = dot_nt(jnp.concatenate([high, low], axis=0), t_high[...])
        surface = both[:NPOLE] + both[NPOLE:] + dot_nt(high, t_low[...])
        ring[0:NPOLE, :] = coef_ring[...] * (sea_ring[0:NPOLE, :] - surface)

        here = pltpu.roll(own_dot(point[...]), ROW0, 1)
        in_cap = (lanes >= ROW0) & (lanes < ROW0 + NPOLE)
        total = jnp.where(in_cap, coef[...] * (sea[...] - here), flux[...])
        flux[...] = total
        if step < STEPS:
            edge = pltpu.roll(total, 128 - (ROW0 + NPOLE - 1), 1)
            prev[...] = own_dot(dst[NPOLE]) + air_gain * jnp.where(lanes == 0, edge, 0.0)
        new = sea_next(width, polar, rows, sea[...], total, pad)
        sea[...] = jnp.where(lanes >= ROW0 + NPOLE + step - 1, sea_hist[slot], new)

    copies = {}
    order = []

    def fetch(name, source, target):
        copy = pltpu.make_async_copy(source, target, load_sems.at[len(order)])
        order.append(copy)
        copies.setdefault(name, []).append(copy)
        copy.start()

    def ready(*wanted):
        for name in wanted:
            for copy in copies.pop(name, ()):
                copy.wait()

    @pl.when(polar == 1)
    def _():
        if steps[0] == 1:
            half, part = blocks // 2, NK // blocks
            y, z = lax.rem(block, 2), block // 2
            for n, ref in enumerate(spec_in):
                at = jnp.bitwise_xor(z, n % half) + half * (y if n < half else 1 - y)
                at = pl.ds(pl.multiple_of(at * part, part), part)
                fetch("spec", ref, spec_a.at[pl.ds(1, CAP), at])
        else:
            fetch("spec", spec_in[0], spec_a.at[pl.ds(1, CAP)])
        fetch("stencil", loads["stencil"], stencil)
        if steps[0] > 1:
            fetch("gathered", loads["gathered"], gathered)
            fetch("sea_ring", loads["sea_ring"], sea_ring)
            fetch("ring_flux", loads["ring_flux"], ring.at[pl.ds(0, NPOLE)])
        fetch("t_high", loads["t_high"], t_high)
        fetch("t_low", loads["t_low"], t_low)
        if steps[0] == 1:
            fetch("sea_ring", loads["sea_ring"], sea_ring)
            fetch("gathered", loads["gathered"], gathered)
        fetch("coef_ring", loads["coef_ring"], coef_ring)
        fetch("coef", loads["coef"], coef)
        fetch("sea", loads["sea"], sea)
        fetch("flux", loads["flux"] if steps[0] > 1 else hist(3, 1), flux)
        for n, step in enumerate(steps):
            fetch("hist", hist(2, step), sea_hist.at[n])
        for n, step in enumerate(wedge_steps):
            fetch("hist", hist(3, step), flux_hist.at[n])
            fetch("hist", hist(1, step - 1), side.at[n])
            row = pl.ds(8 + (step - 2) * width, width)
            fetch("hist", hist(0, step - 1), cur.at[row])
        kept = steps[0] - 1
        for j in range(kept):
            fetch("hist", loads["wedge"].at[j], cur.at[pl.ds(8 + j * width, width)])
        for ref in (spec_a, spec_b):
            ref[0] = jnp.zeros((NK, 128), F32)
            for beyond in range(CAP + 1, CAP + 4):
                ref[beyond] = jnp.zeros((NK, 128), F32)
        cur[0:8, :] = jnp.zeros((8, 128), F32)
        pad[...] = jnp.zeros_like(pad)

        src, dst = spec_a, spec_b
        for n, step in enumerate(steps):
            cap_step(step, src, dst, n)
            src, dst = dst, src
            if step < STEPS:
                pending = wedge_step(step + 1)
                flux[...] = pending
                if not last:
                    gather_out[pl.ds(8 * n, 8), :] = jnp.transpose(pending)[
                        NPOLE + ROW0 : NPOLE + ROW0 + 8
                    ]
        ready(*list(copies))
        if last:
            start, extent = (HALO, count) if fast else (0, width)

            def send(ref, offset, q):
                r = jnp.where(flip == 1, rows - 1 - q, q)
                return pltpu.make_async_copy(
                    ref.at[pl.ds(offset + start, extent)], air_out.at[r], sems.at[q]
                )

            for j in range(WEDGE):
                send(cur, 8 + j * width, NPOLE + j).start()

            @pl.loop(0, NPOLE)
            def _(q):
                y = own_dot(src[q + 1])
                edge = pltpu.roll(flux[...], lax.rem(128 - ROW0 - q, 128), 1)
                back[q] = y + air_gain * jnp.where(lanes == 0, edge, 0.0)
                send(back.at[q], 0, q).start()

            @pl.loop(0, NPOLE)
            def _(q):
                send(back.at[q], 0, q).wait()

            for j in range(WEDGE):
                send(cur, 8 + j * width, NPOLE + j).wait()
        else:
            stores = [pltpu.make_async_copy(src.at[pl.ds(1, CAP)], spec_out, load_sems.at[0])]
            for j in range(len(wedge_steps) + kept):
                stores.append(
                    pltpu.make_async_copy(
                        cur.at[pl.ds(8 + j * width, width)], wedge_out.at[j], load_sems.at[1 + j]
                    )
                )
            for copy in stores:
                copy.start()
            sea_out[...] = sea[...]
            flux_out[...] = flux[...]
            sea_ring_out[...] = sea_ring[...]
            ring_out[...] = ring[0:NPOLE, :]
            for copy in stores:
                copy.wait()

    if last:
        @pl.when(polar == 0)
        def _():
            copy = pltpu.make_async_copy(hist(2, STEPS), sea, load_sems.at[0])
            copy.start()
            copy.wait()

        turn[...] = jnp.transpose(sea[...])

        @pl.loop(0, rows)
        def _(q):
            r = jnp.where(flip == 1, rows - 1 - q, q)
            sea_out[pl.ds(r, 1), :] = turn[pl.ds(q + ROW0, 1), :]


def cap_hists(steps):
    return [0] if steps[-1] < 3 else [0, 1] if steps[0] < 5 else [1]


def cap_steps(rows, count, width, blocks, fast, steps, scal, spec, big, small, air):
    levels = 128
    ring_width = blocks * width
    last = steps[-1] == STEPS
    any_spec = pl.BlockSpec(memory_space=pl.ANY)
    vmem = pl.BlockSpec(memory_space=pltpu.VMEM)
    shape = jax.ShapeDtypeStruct
    square = pltpu.VMEM((width, 128), F32)
    aliases = {}
    extra = []
    if last:
        out_shape = [
            shape((rows, count if fast else width, levels), F32),
            shape((rows, width), F32),
        ]
        out_specs = [any_spec, vmem]
        extra = [pltpu.VMEM((NPOLE, width, levels), F32), pltpu.SemaphoreType.DMA((NPOLE + WEDGE,))]
        aliases = {1 + len(spec) + len(big) + len(small): 0}
    else:
        out_shape = [
            shape((CAP, NK, levels), F32),
            shape((steps[-1], width, levels), F32),
            shape((width, 128), F32),
            shape((width, 128), F32),
            shape((24, ring_width), F32),
            shape((NPOLE, ring_width), F32),
            shape((16, width), F32),
        ]
        out_specs = [any_spec] * 2 + [vmem] * 5
    return pl.pallas_call(
        functools.partial(cap_kernel, rows, count, width, blocks, fast, steps, len(spec)),
        out_shape=out_shape,
        in_specs=[pl.BlockSpec(memory_space=pltpu.SMEM)]
        + [any_spec] * (len(spec) + len(big))
        + [vmem] * len(small)
        + [any_spec] * len(air),
        out_specs=out_specs,
        scratch_shapes=[
            pltpu.VMEM((CAP + 4, NK, levels), F32),
            pltpu.VMEM((CAP + 4, NK, levels), F32),
            pltpu.VMEM((WEDGE * width + 16, levels), F32),
            square,
            square,
            pltpu.VMEM((width, 2 * levels), BF16),
            pltpu.VMEM((NK, 2 * levels), BF16),
            pltpu.VMEM((NK, 2 * levels), BF16),
            pltpu.VMEM((NK, 128), F32),
            pltpu.VMEM((NK, 128), F32),
            pltpu.VMEM((NK, 128), F32),
            square,
            square,
            pltpu.VMEM((width + 16, 128), F32),
            pltpu.VMEM((24, ring_width), F32),
            pltpu.VMEM((24, ring_width), F32),
            pltpu.VMEM((NK, 128), F32),
            pltpu.VMEM((ring_width, NK), BF16),
            pltpu.VMEM((ring_width, NK), BF16),
            pltpu.VMEM((3, NK, levels), F32),
            square,
            pltpu.VMEM((NPOLE, ring_width), F32),
            pltpu.VMEM((blocks, 16, width), F32),
            pltpu.VMEM((2, width, 128), F32),
            pltpu.VMEM((2, width, 128), F32),
            pltpu.VMEM((2, width, 128), F32),
            pltpu.VMEM((128, width), F32),
            pltpu.SemaphoreType.DMA((blocks + 32,)),
        ]
        + extra,
        input_output_aliases=aliases,
        compiler_params=pltpu.CompilerParams(vmem_limit_bytes=VMEM_LIMIT),
        cost_estimate=pl.CostEstimate(
            flops=len(steps) * CAP * NK * levels * levels * 4,
            bytes_accessed=20_000_000,
            transcendentals=0,
        ),
        name="cap_steps",
    )(scal, *spec, *big, *small, *air)


def shift(x, axis, by, wrap):
    size = lax.axis_size(axis)
    pairs = [(i, (i + by) % size) for i in range(size) if wrap or 0 <= i + by < size]
    return lax.ppermute(x, axis, pairs)


def between_caps(x, by):
    size, bands = lax.axis_size("lon"), lax.axis_size("lat")
    pairs = [(b * size + i, b * size + (i ^ by)) for b in (0, bands - 1) for i in range(size)]
    return lax.ppermute(x, ("lat", "lon"), pairs)


def to_all(x, blocks):
    copies = jnp.broadcast_to(x[None], (blocks,) + x.shape)
    return lax.all_to_all(copies, "lon", split_axis=0, concat_axis=0, tiled=True)


def local(air_temp, sea_temp, land_sea, courant, vertical_mix, cutoffs):
    rows, count, levels = air_temp.shape
    blocks, bands = lax.axis_size("lon"), lax.axis_size("lat")
    nlon = blocks * count
    width = round_up(count + 2 * HALO, 128)
    depth = round_up(count, 128)
    fast = count % 8 == 0
    band, block = lax.axis_index("lat"), lax.axis_index("lon")
    flip = band == bands - 1
    polar = (band == 0) | flip

    cut = jnp.where(flip, cutoffs[::-1][:NPOLE], cutoffs[:NPOLE])
    head = jnp.stack([flip, polar, block]).astype(jnp.int32)
    scal = jnp.concatenate([head, cut, jnp.full((STEPS + 4,), KMAX, jnp.int32)])
    window, forward, weight = tables(blocks, count, width, depth)
    t_high, t_low = (jnp.asarray(part) for part in window)
    own_table = lax.dynamic_index_in_dim(jnp.asarray(forward), block, 0, keepdims=False)
    theta = np.arange(KMAX + 1) * (2.0 * math.pi / nlon)
    cosine = np.tile(np.cos(theta), 2).astype(np.float32)
    sine = np.concatenate([-np.sin(theta), np.sin(theta)]).astype(np.float32)
    stay = 1.0 - 4.0 * diffusion_rate + 2.0 * diffusion_rate * jnp.asarray(cosine)
    stencil = jnp.stack(
        [
            jnp.broadcast_to(stay[:, None], (NK, levels)),
            jnp.asarray(sine)[:, None] * courant[None, :],
            jnp.asarray(sine)[:, None] * jnp.broadcast_to(courant[:1], (levels,))[None, :],
        ]
    )
    weights = jnp.broadcast_to(jnp.asarray(weight.astype(np.float32))[None], (8, NK))
    cour = jnp.stack([diffusion_rate - 0.5 * courant, diffusion_rate + 0.5 * courant])
    surface = jnp.broadcast_to(cour[:, :1], cour.shape)
    cour = jnp.concatenate([cour, surface, jnp.zeros((4, levels), F32)], 0)
    v_round = lax.reduce_precision(vertical_mix, 8, 7)
    v_high, v_low = v_round.astype(BF16), (vertical_mix - v_round).astype(BF16)
    vcat = jnp.concatenate(
        [
            jnp.concatenate([v_high, v_low], 1),
            jnp.concatenate([v_high, jnp.zeros_like(v_low)], 1),
        ],
        0,
    )

    west = shift(air_temp[:, count - HALO :], "lon", 1, True)
    east = shift(air_temp[:, :HALO], "lon", -1, True)

    half = blocks // 2
    keep, send = start_spectra(blocks, scal, air_temp, own_table)
    send, sea_temp, land_sea, west, east = lax.optimization_barrier(
        (send, sea_temp, land_sea, west, east)
    )
    half_sum = keep + between_caps(send, 1)

    exchange_coef = jnp.where(land_sea == 1, sea_coef, land_coef).astype(F32)
    sea_blocks = sea_temp.reshape(-1, blocks, count).transpose(1, 0, 2).reshape(rows, count)
    got = to_all(jnp.concatenate([sea_blocks, exchange_coef], 0), blocks)
    own_window, sea_ring, coef_ring = windows(
        rows, count, width, blocks, scal, got.reshape(blocks, 2 * rows, count)
    )
    above = shift(own_window[:, rows - ROW0 :], "lat", 1, False)
    below = shift(own_window[:, :ROW0], "lat", -1, False)

    def edge(part):
        return jnp.concatenate([west[part], air_temp[part], east[part]], 1)

    north = shift(edge(slice(rows - ROW0, rows)), "lat", 1, False)
    south = shift(edge(slice(0, ROW0)), "lat", -1, False)

    if fast:
        air = air_temp
    else:
        middle = jnp.concatenate([west, air_temp, east], 1)
        air = jnp.concatenate([north, middle, south], 0)
        air = jnp.pad(air, ((0, 0), (0, width - count - 2 * HALO), (0, 0)))
    half_sum, own_window = lax.optimization_barrier((half_sum, own_window))
    parts = [between_caps(half_sum[j], 2 * j) for j in range(1, half)]
    outs = outside_steps(
        rows, count, width, fast, (1, 2, 3), scal, (air, west, east, north, south),
        (own_window, above, below, cour, vcat),
    )
    state, early, sea, coef, gathered = outs[0], tuple(outs[1:5]), outs[5], outs[6], outs[7]
    own = functools.reduce(jnp.add, parts, half_sum[0])
    own, state = lax.optimization_barrier((own, state))
    near = [own] + [between_caps(own, 2 * j) for j in range(1, half)]
    gathered = to_all(gathered, blocks).reshape(blocks, 16, width)
    near, gathered = lax.optimization_barrier((near, gathered))
    outs = outside_steps(
        rows, count, width, fast, (4, 5, 6), scal, (state,),
        (early[2], early[3], coef, cour, vcat),
    )
    air, late = outs[0], tuple(outs[1:5])
    far = between_caps(jnp.stack(near), 1)
    spec = tuple(near) + tuple(far[j] for j in range(half))
    spec, air, late = lax.optimization_barrier((spec, air, late))

    more = ()
    for steps in ((1, 2), (3, 4), (5, 6)):
        hists = sum(((early, late)[h] for h in cap_hists(steps)), ())
        big = hists + (t_high, t_low, stencil, coef, sea, sea_ring, coef_ring, gathered) + more
        outs = cap_steps(
            rows, count, width, blocks, fast, steps, scal, spec, big,
            (weights, cour, vcat), (air,) if steps[-1] == STEPS else (),
        )
        if steps[-1] < STEPS:
            spec, wedge, sea, flux, sea_ring, ring_flux, mine = outs
            spec, more = (spec,), (flux, ring_flux, wedge)
            gathered = to_all(mine, blocks).reshape(blocks, 16, width)
    air, sea = outs
    if not fast:
        air = air[:, HALO : HALO + count]
    sea = sea[:, HALO : HALO + count]
    sea = lax.all_to_all(sea, "lon", split_axis=0, concat_axis=1, tiled=True)
    return air, sea


def solution(mesh):
    placed = (P("lat", "lon", None), P(("lat", "lon"), None), P("lat", "lon"), P(), P(), P())
    return jax.shard_map(
        local,
        mesh=mesh,
        in_specs=placed,
        out_specs=(P("lat", "lon", None), P(("lat", "lon"), None)),
        check_vma=False,
    )
```

```python
import functools
import math

import jax
import jax.numpy as jnp
import ml_dtypes
import numpy as np
from jax import lax
from jax.experimental import pallas as pl
from jax.experimental.pallas import tpu as pltpu
from jax.sharding import PartitionSpec as P

NPOLE = 16
KMAX = 127
STEPS = 6
NK = 2 * (KMAX + 1)
CAP = NPOLE + STEPS
HALO = 8
ROW0 = STEPS
WEDGE = STEPS - 1

diffusion_rate = 0.1
air_gain = 0.5
ocean_gain = 0.3
ocean_diffusion = 0.2
sea_coef = 0.5
land_coef = 0.15

F32 = jnp.float32
BF16 = jnp.bfloat16
VMEM_LIMIT = 56 * 1024 * 1024


def round_up(value, unit):
    return -(-value // unit) * unit


def two_parts(x):
    high = x.astype(BF16)
    return high, (x - high.astype(F32)).astype(BF16)


def dot(a, b):
    return jnp.dot(a, b, preferred_element_type=F32)


def dot_nt(a, b):
    return lax.dot_general(a, b, (((1,), (1,)), ((), ())), preferred_element_type=F32)


def table_dot(high, low, x):
    x_high, x_low = two_parts(x)
    both = dot(high, jnp.concatenate([x_high, x_low], axis=1))
    return both[:, :128] + both[:, 128:] + dot(low, x_high)


def numpy_parts(table):
    high = table.astype(ml_dtypes.bfloat16)
    low = (table - high.astype(np.float64)).astype(ml_dtypes.bfloat16)
    return high, low


def owner_order(blocks):
    k = np.arange(KMAX + 1).reshape(blocks, -1)
    return np.concatenate([k, k + KMAX + 1], 1).reshape(-1)


@functools.lru_cache(maxsize=None)
def tables(blocks, count, width, depth):
    nlon = blocks * count
    wavenum = np.arange(KMAX + 1)
    weight = np.where(wavenum == 0, 1.0, 2.0) / nlon

    def table(columns):
        phase = (columns[:, None] * wavenum[None, :]) % nlon * (2.0 * math.pi / nlon)
        return np.concatenate([np.cos(phase), np.sin(phase)], 1)

    window = np.concatenate(
        [table((j * count - HALO + np.arange(width)) % nlon) for j in range(blocks)], 0
    )
    forward = np.zeros((blocks, NK, depth))
    for j in range(blocks):
        own = table(j * count + np.arange(count)) * np.tile(weight, 2)
        forward[j, :, :count] = own.T[owner_order(blocks)]
    high, low = numpy_parts(forward)
    return numpy_parts(window), np.concatenate([high, high, low], 2), np.tile(weight, 2)


@functools.lru_cache(maxsize=None)
def rotations(nlon):
    theta = np.arange(KMAX + 1) * (2.0 * math.pi / nlon)
    stay = 1.0 - 4.0 * diffusion_rate + 2.0 * diffusion_rate * np.tile(np.cos(theta), 2)
    turn = np.concatenate([-np.sin(theta), np.sin(theta)])
    both = np.stack([stay, turn]).astype(np.float32)
    return np.ascontiguousarray(np.broadcast_to(both[:, :, None], (2, NK, 128)))


def mixing(mix, vcat):
    high, low = two_parts(mix[...])
    vcat[0:128, 0:128] = high
    vcat[128:256, 0:128] = high
    vcat[0:128, 128:256] = low
    vcat[128:256, 128:256] = jnp.zeros_like(low)


def winds(courant):
    c = courant[0:1, :]
    top = jnp.broadcast_to(c[:, 0:1], c.shape)
    return [diffusion_rate + sign * 0.5 * x for x in (c, top) for sign in (-1.0, 1.0)]


def lane_iota(shape):
    return lax.broadcasted_iota(jnp.int32, shape, len(shape) - 1)


def spectra_kernel(count, blocks, scal, air, table, keep, send, stacked, sums):
    depth = stacked.shape[0] // 3
    half, part = blocks // 2, NK // blocks
    flip, block = scal[0], scal[2]
    side, place = lax.rem(block, 2), block // 2

    @pl.when(pl.program_id(0) == 0)
    def _():
        stacked[...] = jnp.zeros_like(stacked)

    @pl.when(scal[1] == 1)
    def _():
        for n in range(2):
            high, low = two_parts(air[n])
            lanes = slice(128 * n, 128 * n + 128)
            stacked[0:count, lanes] = high
            stacked[depth : depth + count, lanes] = low
            stacked[2 * depth : 2 * depth + count, lanes] = high
        sums[...] = dot(table[0], stacked[...])
        for n in range(2):
            to = jnp.where(flip == 1, 1 - n, n)
            lanes = slice(128 * n, 128 * n + 128)
            for z in range(half):
                at = jnp.bitwise_xor(place, z)
                mine = pl.multiple_of((side * half + z) * part, part)
                other = pl.multiple_of(((1 - side) * half + z) * part, part)
                keep[at, to] = sums[pl.ds(mine, part), lanes]
                send[at, to] = sums[pl.ds(other, part), lanes]


def start_spectra(blocks, scal, air_temp, table):
    rows, count, levels = air_temp.shape
    half, part = blocks // 2, NK // blocks
    depth = table.shape[2] // 3

    def place(p, scal):
        return (jnp.where(scal[0] == 1, rows // 2 - 1 - p, p), 0, 0)

    out = jax.ShapeDtypeStruct((half, CAP, part, levels), F32)
    out_spec = pl.BlockSpec((half, 2, part, levels), lambda p, scal: (0, p, 0, 0))
    return pl.pallas_call(
        functools.partial(spectra_kernel, count, blocks),
        out_shape=[out, out],
        grid_spec=pltpu.PrefetchScalarGridSpec(
            num_scalar_prefetch=1,
            grid=(CAP // 2,),
            in_specs=[
                pl.BlockSpec((2, count, levels), place),
                pl.BlockSpec((1, NK, 3 * depth), lambda p, scal: (scal[2], 0, 0)),
            ],
            out_specs=[out_spec, out_spec],
            scratch_shapes=[
                pltpu.VMEM((3 * depth, 2 * levels), BF16),
                pltpu.VMEM((NK, 2 * levels), F32),
            ],
        ),
        compiler_params=pltpu.CompilerParams(vmem_limit_bytes=VMEM_LIMIT),
        name="start_spectra",
    )(scal, air_temp, table)


def free_kernel(blocks, parts, scal, *refs):
    sums, refs = refs[:parts], refs[parts:]
    rotate, courant, mix, edge, early, late, state, mask, adv, xcat, vcat = refs
    part = NK // blocks
    some = part // 2
    owner = lax.rem(scal[2], 2) * (blocks // 2) + scal[2] // 2

    @pl.when(scal[1] == 1)
    def _():
        mixing(mix, vcat)
        state[0] = jnp.zeros((part, 128), F32)
        state[1 : CAP + 1] = functools.reduce(jnp.add, [ref[...] for ref in sums])
        at = pl.ds(pl.multiple_of(owner * part, part), part)
        stay, turn = rotate[0, at, :], rotate[1, at, :] * courant[0:1, :]
        wavenum = lax.broadcasted_iota(jnp.int32, (part, 128), 0) % some + owner * some
        for q in range(CAP):
            mask[q] = jnp.where(wavenum <= scal[3 + q], 1.0, 0.0)
        first = lane_iota((part, 128)) == 0
        top = jnp.zeros((part, 128), F32)
        for step in range(1, STEPS + 1):
            size = CAP - step
            here = state[1 : size + 1]
            swapped = jnp.concatenate([here[:, some:], here[:, :some]], axis=1)
            x = stay * here + diffusion_rate * (state[0:size] + state[2 : size + 2])
            x = (x + turn * swapped) * mask[0:size]
            x = x.reshape(size * part, 128)
            high, low = two_parts(x)
            adv[0 : size * part, :] = x
            xcat[0 : size * part, 0:128] = high
            xcat[0 : size * part, 128:256] = low
            mixed = dot(xcat[0 : size * part, :], vcat[...])
            y = adv[0 : size * part, :] + mixed[:, :128] + mixed[:, 128:]
            state[1 : size + 1] = y.reshape(size, part, 128)
            for q in range(NPOLE):
                lane = NPOLE * (step - 1) + q
                top += pltpu.roll(jnp.where(first, state[q + 1], 0.0), lane, 1)
            if step < STEPS:
                for to in range(blocks):
                    early[to, part * step : part * (step + 1), :] = state[NPOLE]
            else:
                late[...] = state[1 : NPOLE + 1]
        for to in range(blocks):
            early[to, 0:part, :] = top
            early[to, STEPS * part :, :] = edge[...]


def free_steps(blocks, scal, sums, rotate, courant, mix, edge):
    part = NK // blocks
    vmem = pl.BlockSpec(memory_space=pltpu.VMEM)
    shape = jax.ShapeDtypeStruct
    return pl.pallas_call(
        functools.partial(free_kernel, blocks, len(sums)),
        out_shape=[
            shape((blocks, STEPS * part + edge.shape[0], 128), F32),
            shape((NPOLE, part, 128), F32),
        ],
        in_specs=[pl.BlockSpec(memory_space=pltpu.SMEM)] + [vmem] * (len(sums) + 4),
        out_specs=[vmem] * 2,
        scratch_shapes=[
            pltpu.VMEM((CAP + 2, part, 128), F32),
            pltpu.VMEM((CAP, part, 128), F32),
            pltpu.VMEM((CAP * part, 128), F32),
            pltpu.VMEM((CAP * part, 256), BF16),
            pltpu.VMEM((256, 256), BF16),
        ],
        compiler_params=pltpu.CompilerParams(vmem_limit_bytes=VMEM_LIMIT),
        name="free_steps",
    )(scal, *sums, rotate, courant, mix, edge)


def advance(
    width, here_ref, base, north_ref, north, south_ref, south, cour, adv, xcat, more=None
):
    c_east, c_west = cour
    for o in range(0, width, 128):
        around = north_ref[pl.ds(north + o, 128), :] + south_ref[pl.ds(south + o, 128), :]
        x = (
            (1.0 - 4.0 * diffusion_rate) * here_ref[pl.ds(base + o, 128), :]
            + diffusion_rate * around
            + c_east * here_ref[pl.ds(base + o + 1, 128), :]
            + c_west * here_ref[pl.ds(base + o - 1, 128), :]
        )
        if more is not None:
            moved = pltpu.roll(more[0][pl.ds(o, 128), :], more[1], 1)
            x += jnp.where(lane_iota(x.shape) == 0, moved, 0.0)
        high, low = two_parts(x)
        adv[pl.ds(o, 128), :] = x
        xcat[pl.ds(o, 128), 0:128] = high
        xcat[pl.ds(o, 128), 128:256] = low


def two_at_a_time(first, pairs, load, finish, arrive=None):
    load(first, 0)

    @pl.loop(0, pairs)
    def _(n):
        if arrive is not None:
            arrive(n)
        q = first + 2 * n
        finish(q, 0, lambda: load(q + 1, 1))
        finish(q + 1, 1, lambda: load(q + 2, 0))


def exchange(y, lane, sea, coef):
    back = (128 - lane) % 128
    flux = pltpu.roll(coef, back, 1) * (pltpu.roll(sea, back, 1) - y)
    return jnp.where(lane_iota(y.shape) == 0, flux, 0.0)


def sea_next(width, polar, rows, sea, flux, pad):
    pad[pl.ds(8, width), :] = sea
    east = pad[pl.ds(9, width), :]
    west = pad[pl.ds(7, width), :]
    around = east + west + pltpu.roll(sea, 1, 1) + pltpu.roll(sea, 127, 1)
    new = sea - ocean_gain * flux + ocean_diffusion * (around - 4.0 * sea)
    lane = lane_iota(sea.shape)
    first = jnp.where(polar == 1, ROW0, 0)
    return jnp.where((lane >= first) & (lane < rows + 2 * ROW0), new, 0.0)


def windows_kernel(rows, count, width, blocks, scal, got, own, ring_sea, ring_coef, wide):
    per = rows // blocks
    for j in range(blocks):
        columns = slice(j * width + HALO, j * width + HALO + count)
        for i in range(blocks):
            wide[0, per * i : per * (i + 1), columns] = got[i, per * j : per * (j + 1), :]
        wide[1, :, columns] = got[j, rows:, :]
    rest = width - HALO - count
    for j in range(blocks):
        before = ((j - 1) % blocks) * width + count
        after = ((j + 1) % blocks) * width + HALO
        end = j * width + HALO + count
        wide[:, :, j * width : j * width + HALO] = wide[:, :, before : before + HALO]
        wide[:, :, end : end + rest] = wide[:, :, after : after + rest]
    own[...] = wide[:, :, pl.ds(pl.multiple_of(scal[2] * width, 128), width)]

    @pl.when(scal[1] == 1)
    def _():
        @pl.loop(0, 24)
        def _(q):
            r = jnp.where(scal[0] == 1, rows - 1 - q, q)
            ring_sea[pl.ds(q, 1), :] = wide[0, pl.ds(r, 1), :]

        @pl.loop(0, NPOLE)
        def _(q):
            r = jnp.where(scal[0] == 1, rows - 1 - q, q)
            ring_coef[pl.ds(q, 1), :] = wide[1, pl.ds(r, 1), :]


def windows(rows, count, width, blocks, scal, got):
    vmem = pl.BlockSpec(memory_space=pltpu.VMEM)
    shape = jax.ShapeDtypeStruct
    return pl.pallas_call(
        functools.partial(windows_kernel, rows, count, width, blocks),
        out_shape=[
            shape((2, rows, width), F32),
            shape((24, blocks * width), F32),
            shape((NPOLE, blocks * width), F32),
        ],
        in_specs=[pl.BlockSpec(memory_space=pltpu.SMEM), vmem],
        out_specs=[vmem] * 3,
        scratch_shapes=[pltpu.VMEM((2, rows, blocks * width), F32)],
        compiler_params=pltpu.CompilerParams(vmem_limit_bytes=VMEM_LIMIT // 2),
        name="windows",
    )(scal, got)


def outside_kernel(rows, count, width, fast, steps, scal, *refs):
    first, last = steps[0] == 1, steps[-1] == STEPS
    if first:
        (air, west, east, north, south, own, above, below, courant, mix), refs = refs[:10], refs[10:]
        (state, wedge, side, sea_hist, flux_hist, sea_start, coef, gather_out), refs = (
            refs[:8], refs[8:])
    else:
        (state, sea_hist_in, flux_hist_in, coef, courant, mix), refs = refs[:6], refs[6:]
        (air_out, wedge, side, sea_hist, flux_hist), refs = refs[:5], refs[5:]
    (buf_a, buf_b, adv_a, adv_b, xcat_a, xcat_b, sea, flux, point, more, turn, pad, vcat, sems) = refs
    flip, polar = scal[0], scal[1]
    total = rows + 2 * ROW0
    inner = count + 2 * HALO
    lanes = lane_iota((width, 128))

    def base_of(q):
        return pl.multiple_of(8 + (q + ROW0) * width, 8)

    def q_of(r):
        return jnp.where(flip == 1, rows - 1 - r, r)

    def low_row(step):
        return jnp.where(polar == 1, NPOLE + step - 1, step - STEPS)

    def row_range(body, step, *sizes):
        hi = rows - 1 + STEPS - step
        ref, extent, sem = sizes

        @pl.loop(low_row(step), hi + 1)
        def _(q):
            body(q).start()

        for kind, count_rows in ((1, hi + 1 - NPOLE - step + 1), (0, hi + 1 + STEPS - step)):
            @pl.when(polar == kind)
            def _(count_rows=count_rows):
                whole = ref.at[pl.ds(0, count_rows * extent)]
                pltpu.make_async_copy(whole, whole, sem).wait()

    def begin():
        mixing(mix, vcat)
        beyond = 8 + total * width
        for ref in (buf_a, buf_b):
            ref[0:8, :] = jnp.zeros((8, 128), F32)
            ref[pl.ds(beyond, 3 * width + 8), :] = jnp.zeros((3 * width + 8, 128), F32)
        pad[...] = jnp.zeros_like(pad)

    if first:
        if fast:
            @pl.loop(0, rows)
            def _(r):
                base = base_of(q_of(r))
                for ref, offset, size in (
                    (west, 0, HALO), (air, HALO, count), (east, HALO + count, HALO)
                ):
                    pltpu.make_async_copy(
                        ref.at[r], buf_a.at[pl.ds(base + offset, size)], sems.at[0]
                    ).start()

            @pl.loop(0, ROW0)
            def _(r):
                for ref, at in ((north, r - ROW0), (south, r + rows)):
                    pltpu.make_async_copy(
                        ref.at[r], buf_a.at[pl.ds(base_of(q_of(at)), inner)], sems.at[0]
                    ).start()

            if inner < width:
                @pl.loop(0, total)
                def _(e):
                    buf_a[pl.ds(base_of(e - ROW0) + inner, width - inner), :] = jnp.zeros(
                        (width - inner, 128), F32
                    )

            everything = buf_a.at[pl.ds(0, total * inner)]
        else:
            @pl.loop(0, total)
            def _(e):
                pltpu.make_async_copy(
                    air.at[e], buf_a.at[pl.ds(base_of(q_of(e - ROW0)), width)], sems.at[0]
                ).start()

            everything = buf_a.at[pl.ds(0, total * width)]
        begin()
        for n, ref in ((0, sea), (1, coef)):
            turn[...] = jnp.zeros_like(turn)
            for source, size, at in ((above, ROW0, -ROW0), (own, rows, 0), (below, ROW0, rows)):
                @pl.loop(0, size)
                def _(r, source=source, at=at):
                    turn[pl.ds(q_of(r + at) + ROW0, 1), :] = source[n, pl.ds(r, 1), :]

            ref[...] = jnp.transpose(turn[...])
        sea_start[...] = sea[...]
        pltpu.make_async_copy(everything, everything, sems.at[0]).wait()
    else:
        begin()
        sea[...] = sea_hist_in[steps[0] - 2]
        flux[...] = flux_hist_in[steps[0] - 2]
        row_range(
            lambda q: pltpu.make_async_copy(
                state.at[q + ROW0], buf_a.at[pl.ds(base_of(q), width)], sems.at[0]
            ),
            steps[0] - 1, buf_a, width, sems.at[0],
        )

    def with_flux(y, q):
        gain = air_gain * pltpu.roll(flux[...], 128 - (q + ROW0), 1)
        return y + jnp.where(lanes == 0, gain, 0.0)

    advs, xcats = (adv_a, adv_b), (xcat_a, xcat_b)
    cour = winds(courant)
    src, dst = buf_a, buf_b
    for n, step in enumerate(steps):
        lo = low_row(step)
        hi = rows - 1 + STEPS - step
        pairs = jnp.where(polar == 1, (hi - NPOLE - step + 3) // 2, (hi + 1 + STEPS - step) // 2)
        if step > 1:
            gain = air_gain * flux[...]
            pad[pl.ds(8, width), :] = gain
            more[...] = (
                (1.0 - 4.0 * diffusion_rate) * gain
                + diffusion_rate * (pltpu.roll(gain, 1, 1) + pltpu.roll(gain, 127, 1))
                + cour[2] * pad[pl.ds(9, width), :]
                + cour[3] * pad[pl.ds(7, width), :]
            )
        point[...] = jnp.zeros_like(point)

        def load(q, slot, src=src, step=step):
            base = base_of(q)
            advance(width, src, base, src, base - width, src, base + width, cour[:2],
                    advs[slot], xcats[slot], (more, 128 - (q + ROW0)) if step > 1 else None)

        def finish(q, slot, between, dst=dst):
            mixed = dot(xcats[slot][...], vcat[...])
            between()
            y = advs[slot][...] + mixed[:, :128] + mixed[:, 128:]
            dst[pl.ds(base_of(q), width), :] = y
            point[...] += pltpu.roll(jnp.where(lanes == 0, y, 0.0), q + ROW0, 1)

        two_at_a_time(lo, pairs, load, finish)

        total_flux = jnp.where(lanes >= lo + ROW0, coef[...] * (sea[...] - point[...]), 0.0)
        flux[...] = total_flux
        new_sea = sea_next(width, polar, rows, sea[...], total_flux, pad)
        sea[...] = new_sea
        sea_hist[n] = new_sea
        flux_hist[n] = total_flux
        if step <= WEDGE:
            @pl.when(polar == 1)
            def _(dst=dst, step=step, n=n):
                for ref, q in ((wedge, NPOLE + step - 1), (side, NPOLE + step)):
                    ref[n] = with_flux(dst[pl.ds(base_of(q), width), :], q)
        src, dst = dst, src

    if first:
        state_rows = row_range(
            lambda q: pltpu.make_async_copy(
                src.at[pl.ds(base_of(q), width)], state.at[q + ROW0], sems.at[1]
            ),
            steps[-1], src, width, sems.at[1],
        )
        turned = jnp.transpose(flux_hist[0])[NPOLE + ROW0 : NPOLE + ROW0 + 8]
        for o in range(width // 128):
            gather_out[8 * o : 8 * o + 8, :] = turned[:, 128 * o : 128 * o + 128]
    else:
        start, extent = (HALO, count) if fast else (0, width)
        first_row = jnp.where(polar == 1, NPOLE + WEDGE, 0)

        @pl.loop(first_row, rows)
        def _(q):
            row = pl.ds(base_of(q), width)
            src[row, :] = with_flux(src[row, :], q)
            pltpu.make_async_copy(
                src.at[pl.ds(base_of(q) + start, extent)], air_out.at[q_of(q)], sems.at[1]
            ).start()

        for kind, count_rows in ((1, rows - NPOLE - WEDGE), (0, rows)):
            @pl.when(polar == kind)
            def _(count_rows=count_rows):
                whole = src.at[pl.ds(0, count_rows * extent)]
                pltpu.make_async_copy(whole, whole, sems.at[1]).wait()


def outside_steps(rows, count, width, fast, steps, scal, big, small):
    levels = 128
    any_spec = pl.BlockSpec(memory_space=pl.ANY)
    vmem = pl.BlockSpec(memory_space=pltpu.VMEM)
    total = rows + 2 * ROW0
    shape = jax.ShapeDtypeStruct
    square = shape((width, 128), F32)
    hist = [shape((len(steps), width, 128), F32)] * 4
    if steps[0] == 1:
        out_shape = [shape((total, width, levels), F32)] + hist + [square, square]
        out_shape.append(shape((width // 16, 128), F32))
    else:
        out_shape = [shape((rows, count if fast else width, levels), F32)] + hist
    return pl.pallas_call(
        functools.partial(outside_kernel, rows, count, width, fast, steps),
        out_shape=out_shape,
        in_specs=[pl.BlockSpec(memory_space=pltpu.SMEM)]
        + [any_spec] * len(big)
        + [vmem] * len(small),
        out_specs=[any_spec] + [vmem] * (len(out_shape) - 1),
        scratch_shapes=[
            pltpu.VMEM(((total + 3) * width + 16, levels), F32),
            pltpu.VMEM(((total + 3) * width + 16, levels), F32),
            pltpu.VMEM((width, levels), F32),
            pltpu.VMEM((width, levels), F32),
            pltpu.VMEM((width, 2 * levels), BF16),
            pltpu.VMEM((width, 2 * levels), BF16),
            pltpu.VMEM((width, 128), F32),
            pltpu.VMEM((width, 128), F32),
            pltpu.VMEM((width, 128), F32),
            pltpu.VMEM((width, 128), F32),
            pltpu.VMEM((128, width), F32),
            pltpu.VMEM((width + 16, 128), F32),
            pltpu.VMEM((256, 256), BF16),
            pltpu.SemaphoreType.DMA((2,)),
        ],
        compiler_params=pltpu.CompilerParams(vmem_limit_bytes=VMEM_LIMIT),
        cost_estimate=pl.CostEstimate(
            flops=len(steps) * rows * width * levels * levels * 4,
            bytes_accessed=rows * width * levels * 10,
            transcendentals=0,
        ),
        name="outside_steps",
    )(scal, *big, *small)


def cap_kernel(rows, count, width, blocks, fast, steps, parts, scal, *refs):
    last = steps[-1] == STEPS
    wedge_steps = [step + 1 for step in steps if step < STEPS]
    spec_in, refs = refs[:parts], refs[parts:]
    hists, refs = refs[: 4 * len(cap_hists(steps))], refs[4 * len(cap_hists(steps)) :]
    names = ["free", "t_high", "t_low", "rotate", "coef", "sea", "sea_ring", "coef_ring"]
    if steps[0] > 1:
        names += ["gathered", "flux", "ring_flux", "wedge"]
    if last:
        names += list(range(blocks // 2))
    loads = dict(zip(names, refs[: len(names)]))
    refs = refs[len(names) :]
    weight, courant, mix = refs[:3]
    refs = refs[3:]
    if last:
        refs = refs[1:]
        (air_out, sea_out), refs = refs[:2], refs[2:]
    else:
        (spec_out, wedge_out, sea_out, flux_out, sea_ring_out, ring_out, gather_out), refs = (
            refs[:7], refs[7:])
    (spec_a, spec_b, cur, prev, adv, xcat, kcat_a, kcat_b, kadv_a, kadv_b, point, sea, flux, pad,
     ring, sea_ring, shares, t_high, t_low, stencil, coef, coef_ring, gathered, sea_hist,
     flux_hist, side, turn, free_top, free_row, vcat, load_sems, row_sems) = refs[:32]
    if last:
        back, free_late, sems = refs[32:]
    flip, polar, block = scal[0], scal[1], scal[2]
    lanes = lane_iota((width, 128))
    own = pl.ds(pl.multiple_of(block * width, 128), width)

    def hist(kind, step):
        at = cap_hists(steps).index(0 if step <= 3 else 1)
        return hists[4 * at + kind].at[(step - 1) % 3]

    def own_dot(x):
        return table_dot(t_high[own, :], t_low[own, :], x)

    def wedge_step(step):
        at = wedge_steps.index(step)
        pending = flux_hist[at]
        for j in range(step - 1):
            base = 8 + j * width
            if j == step - 2:
                south_ref, south = side.at[at], 0
            else:
                south_ref, south = cur, base + width
            advance(width, cur, base, prev, 0, south_ref, south, winds(courant)[:2], adv, xcat)
            prev[...] = cur[pl.ds(base, width), :]
            mixed = dot(xcat[...], vcat[...])
            y = adv[...] + mixed[:, :128] + mixed[:, 128:]
            lane = NPOLE + j + ROW0
            out = exchange(y, lane, sea[...], coef[...])
            cur[pl.ds(base, width), :] = y + air_gain * out
            pending += pltpu.roll(out, lane, 1)
        return pending

    def cap_step(step, src, dst, slot):
        count_rows = CAP - step
        if step > 1:
            ready("gathered", "sea_ring", "ring_flux")
        if step > 1:
            for j in range(blocks):
                ring[pl.ds(NPOLE, 8), pl.ds(j * width, width)] = gathered[
                    j, pl.ds(8 * slot, 8), :
                ]
            old, at = sea_ring[...], ring[...]
            place = lax.broadcasted_iota(jnp.int32, old.shape, 0)
            up = jnp.where(place == 0, 0.0, pltpu.roll(old, 1, 0))
            down = pltpu.roll(old, old.shape[0] - 1, 0)
            ring_width = blocks * width
            around = up + down + pltpu.roll(old, 1, 1) + pltpu.roll(old, ring_width - 1, 1)
            sea_ring[...] = old - ocean_gain * at + ocean_diffusion * (around - 4.0 * old)
            spot = lane_iota(at.shape) % width
            at = jnp.where((spot >= HALO) & (spot < HALO + count), at, 0.0)
            high, low = two_parts(at)
            ready("t_high", "t_low", "rotate")
            both = dot(jnp.concatenate([high, low], axis=0), t_high[...])
            sums = both[:24] + both[24:] + dot(high, t_low[...])
            sums = sums * (air_gain * weight[0:1, :])
            sums = jnp.concatenate([sums, jnp.zeros((104, NK), F32)], axis=0)
            moved = jnp.transpose(sums)
            swapped = jnp.concatenate([moved[128:], moved[:128]], axis=0)
            beside = pltpu.roll(moved, 1, 1) + pltpu.roll(moved, 127, 1)
            top = jnp.broadcast_to(courant[0:1, 0:1], (1, 128))
            shares[...] = (
                stencil[0] * moved + diffusion_rate * beside + (stencil[2] * top) * swapped
            )
            stencil[1] = stencil[2] * courant[0:1, :]

        point[...] = jnp.zeros_like(point)
        kcats, kadvs = (kcat_a, kcat_b), (kadv_a, kadv_b)
        first = lane_iota((128, 128)) == 0

        def load(q, slot):
            cut = scal[3 + q]
            for o, other in ((0, 128), (128, 0)):
                more = pltpu.roll(shares[pl.ds(o, 128), :], lax.rem(128 - q, 128), 1)
                x = jnp.where(first, more, 0.0)
                if step > 2:
                    here = src[q + 1, pl.ds(o, 128), :]
                    swapped = src[q + 1, pl.ds(other, 128), :]
                    around = src[q, pl.ds(o, 128), :] + src[q + 2, pl.ds(o, 128), :]
                    x += (
                        stencil[0, pl.ds(o, 128), :] * here
                        + diffusion_rate * around
                        + stencil[1, pl.ds(o, 128), :] * swapped
                    )
                x = jnp.where(lax.broadcasted_iota(jnp.int32, x.shape, 0) <= cut, x, 0.0)
                high, low = two_parts(x)
                kadvs[slot][pl.ds(o, 128), :] = x
                kcats[slot][pl.ds(o, 128), 0:128] = high
                kcats[slot][pl.ds(o, 128), 128:256] = low

        streamed = step == steps[0] and step > 1

        def finish(q, slot, between):
            mixed = dot(kcats[slot][...], vcat[...])
            between()
            y = kadvs[slot][...] + mixed[:, :128] + mixed[:, 128:]
            dst[q + 1] = y
            point[...] += pltpu.roll(jnp.where(lane_iota(y.shape) == 0, y, 0.0), q, 1)

        pairs = (count_rows + 1) // 2
        if streamed:
            spec_row(0).wait()
            spec_row(1).wait()

        def arrive(n):
            spec_row(2 * n + 2).wait()
            spec_row(2 * n + 3).wait()

        if step > 1:
            two_at_a_time(0, pairs, load, finish, arrive if streamed else None)
        if streamed:
            for q in range(2 * pairs + 2, CAP):
                spec_row(q).wait()
        ready("free")
        top = pltpu.roll(free_top[...], (128 - NPOLE * (step - 1)) % 128, 1)
        point[...] += jnp.where(lane_iota((NK, 128)) < NPOLE, top, 0.0)

        ready("t_high", "t_low", "sea_ring", "coef_ring", "coef", "sea", "flux", "hist")
        at_rows = jnp.transpose(point[...])[:NPOLE]
        high, low = two_parts(at_rows)
        both = dot_nt(jnp.concatenate([high, low], axis=0), t_high[...])
        surface = both[:NPOLE] + both[NPOLE:] + dot_nt(high, t_low[...])
        ring[0:NPOLE, :] = coef_ring[...] * (sea_ring[0:NPOLE, :] - surface)

        here = pltpu.roll(own_dot(point[...]), ROW0, 1)
        in_cap = (lanes >= ROW0) & (lanes < ROW0 + NPOLE)
        total = jnp.where(in_cap, coef[...] * (sea[...] - here), flux[...])
        flux[...] = total
        if step < STEPS:
            edge = pltpu.roll(total, 128 - (ROW0 + NPOLE - 1), 1)
            row = free_row[slot] if step == 1 else dst[NPOLE] + free_row[slot]
            prev[...] = own_dot(row) + air_gain * jnp.where(lanes == 0, edge, 0.0)
        new = sea_next(width, polar, rows, sea[...], total, pad)
        sea[...] = jnp.where(lanes >= ROW0 + NPOLE + step - 1, sea_hist[slot], new)

    copies = {}
    order = []

    def fetch(name, source, target):
        copy = pltpu.make_async_copy(source, target, load_sems.at[len(order)])
        order.append(copy)
        copies.setdefault(name, []).append(copy)
        copy.start()

    def ready(*wanted):
        for name in wanted:
            for copy in copies.pop(name, ()):
                copy.wait()

    def spec_row(q):
        return pltpu.make_async_copy(spec_in[0].at[q], spec_a.at[q + 1], row_sems.at[q])

    @pl.when(polar == 1)
    def _():
        if steps[0] > 1:
            fetch("gathered", loads["gathered"], gathered)
            fetch("sea_ring", loads["sea_ring"], sea_ring)
            fetch("ring_flux", loads["ring_flux"], ring.at[pl.ds(0, NPOLE)])
        fetch("t_high", loads["t_high"], t_high)
        fetch("t_low", loads["t_low"], t_low)
        fetch("rotate", loads["rotate"].at[0], stencil.at[0])
        fetch("rotate", loads["rotate"].at[1], stencil.at[2])
        if steps[0] > 1:
            @pl.loop(0, CAP)
            def _(q):
                spec_row(q).start()

        mixing(mix, vcat)
        part = NK // blocks
        some = part // 2
        rows_15 = [step for step in steps if step < STEPS]
        for i in range(blocks):
            owner = (i % 2) * (blocks // 2) + i // 2
            for n in range(2):
                at = pl.ds(KMAX * n + n + some * owner, some)
                take = pl.ds(some * n, some)
                fetch("free", loads["free"].at[i, take], free_top.at[at])
                for slot, step in enumerate(rows_15):
                    take = pl.ds(part * step + some * n, some)
                    fetch("free", loads["free"].at[i, take], free_row.at[slot, at])
        if last:
            side_y, place_z = lax.rem(block, 2), block // 2
            for z in range(blocks // 2):
                for y in range(2):
                    owner = (blocks // 2) * jnp.bitwise_xor(side_y, y) + jnp.bitwise_xor(place_z, z)
                    for n in range(2):
                        at = pl.multiple_of((KMAX + 1) * n + some * owner, some)
                        fetch(
                            "late",
                            loads[z].at[y, :, pl.ds(some * n, some)],
                            free_late.at[:, pl.ds(at, some)],
                        )
        if steps[0] == 1:
            fetch("sea_ring", loads["sea_ring"], sea_ring)
            for i in range(blocks):
                for o in range(width // 128):
                    fetch(
                        "gathered",
                        loads["free"].at[i, pl.ds(STEPS * part + 8 * o, 8)],
                        gathered.at[i, pl.ds(8, 8), pl.ds(128 * o, 128)],
                    )
        fetch("coef_ring", loads["coef_ring"], coef_ring)
        fetch("coef", loads["coef"], coef)
        fetch("sea", loads["sea"], sea)
        fetch("flux", loads["flux"] if steps[0] > 1 else hist(3, 1), flux)
        for n, step in enumerate(steps):
            fetch("hist", hist(2, step), sea_hist.at[n])
        for n, step in enumerate(wedge_steps):
            fetch("hist", hist(3, step), flux_hist.at[n])
            fetch("hist", hist(1, step - 1), side.at[n])
            row = pl.ds(8 + (step - 2) * width, width)
            fetch("hist", hist(0, step - 1), cur.at[row])
        kept = steps[0] - 1
        for j in range(kept):
            fetch("hist", loads["wedge"].at[j], cur.at[pl.ds(8 + j * width, width)])
        for ref in (spec_a, spec_b):
            ref[0] = jnp.zeros((NK, 128), F32)
            for beyond in range(CAP + 1, CAP + 4):
                ref[beyond] = jnp.zeros((NK, 128), F32)
        cur[0:8, :] = jnp.zeros((8, 128), F32)
        pad[...] = jnp.zeros_like(pad)

        src, dst = spec_a, spec_b
        for n, step in enumerate(steps):
            cap_step(step, src, dst, n)
            src, dst = dst, src
            if step < STEPS:
                pending = wedge_step(step + 1)
                flux[...] = pending
                if not last:
                    turned = jnp.transpose(pending)[NPOLE + ROW0 : NPOLE + ROW0 + 8]
                    for to in range(blocks):
                        gather_out[to, pl.ds(8 * n, 8), :] = turned
        ready(*list(copies))
        if last:
            start, extent = (HALO, count) if fast else (0, width)

            def send(ref, offset, q):
                r = jnp.where(flip == 1, rows - 1 - q, q)
                return pltpu.make_async_copy(
                    ref.at[pl.ds(offset + start, extent)], air_out.at[r], sems.at[q]
                )

            for j in range(WEDGE):
                send(cur, 8 + j * width, NPOLE + j).start()

            @pl.loop(0, NPOLE)
            def _(q):
                y = own_dot(src[q + 1] + free_late[q])
                edge = pltpu.roll(flux[...], lax.rem(128 - ROW0 - q, 128), 1)
                back[q] = y + air_gain * jnp.where(lanes == 0, edge, 0.0)
                send(back.at[q], 0, q).start()

            @pl.loop(0, NPOLE)
            def _(q):
                send(back.at[q], 0, q).wait()

            for j in range(WEDGE):
                send(cur, 8 + j * width, NPOLE + j).wait()
        else:
            stores = [pltpu.make_async_copy(src.at[pl.ds(1, CAP)], spec_out, load_sems.at[0])]
            for j in range(len(wedge_steps) + kept):
                stores.append(
                    pltpu.make_async_copy(
                        cur.at[pl.ds(8 + j * width, width)], wedge_out.at[j], load_sems.at[1 + j]
                    )
                )
            for copy in stores:
                copy.start()
            sea_out[...] = sea[...]
            flux_out[...] = flux[...]
            sea_ring_out[...] = sea_ring[...]
            ring_out[...] = ring[0:NPOLE, :]
            for copy in stores:
                copy.wait()

    if last:
        @pl.when(polar == 0)
        def _():
            copy = pltpu.make_async_copy(hist(2, STEPS), sea, load_sems.at[0])
            copy.start()
            copy.wait()

        turn[...] = jnp.transpose(sea[...])

        @pl.loop(0, rows)
        def _(q):
            r = jnp.where(flip == 1, rows - 1 - q, q)
            sea_out[pl.ds(r, 1), :] = turn[pl.ds(q + ROW0, 1), :]


def cap_hists(steps):
    return [0] if steps[-1] < 3 else [0, 1] if steps[0] < 5 else [1]


def cap_steps(rows, count, width, blocks, fast, steps, scal, spec, big, small, air):
    levels = 128
    ring_width = blocks * width
    last = steps[-1] == STEPS
    any_spec = pl.BlockSpec(memory_space=pl.ANY)
    vmem = pl.BlockSpec(memory_space=pltpu.VMEM)
    shape = jax.ShapeDtypeStruct
    square = pltpu.VMEM((width, 128), F32)
    aliases = {}
    extra = []
    if last:
        out_shape = [
            shape((rows, count if fast else width, levels), F32),
            shape((rows, width), F32),
        ]
        out_specs = [any_spec, vmem]
        extra = [
            pltpu.VMEM((NPOLE, width, levels), F32),
            pltpu.VMEM((NPOLE, NK, levels), F32),
            pltpu.SemaphoreType.DMA((NPOLE + WEDGE,)),
        ]
        aliases = {1 + len(spec) + len(big) + len(small): 0}
    else:
        out_shape = [
            shape((CAP, NK, levels), F32),
            shape((steps[-1], width, levels), F32),
            shape((width, 128), F32),
            shape((width, 128), F32),
            shape((24, ring_width), F32),
            shape((NPOLE, ring_width), F32),
            shape((blocks, 16, width), F32),
        ]
        out_specs = [any_spec] * 2 + [vmem] * 5
    return pl.pallas_call(
        functools.partial(cap_kernel, rows, count, width, blocks, fast, steps, len(spec)),
        out_shape=out_shape,
        in_specs=[pl.BlockSpec(memory_space=pltpu.SMEM)]
        + [any_spec] * (len(spec) + len(big))
        + [vmem] * len(small)
        + [any_spec] * len(air),
        out_specs=out_specs,
        scratch_shapes=[
            pltpu.VMEM((CAP + 4, NK, levels), F32),
            pltpu.VMEM((CAP + 4, NK, levels), F32),
            pltpu.VMEM((WEDGE * width + 16, levels), F32),
            square,
            square,
            pltpu.VMEM((width, 2 * levels), BF16),
            pltpu.VMEM((NK, 2 * levels), BF16),
            pltpu.VMEM((NK, 2 * levels), BF16),
            pltpu.VMEM((NK, 128), F32),
            pltpu.VMEM((NK, 128), F32),
            pltpu.VMEM((NK, 128), F32),
            square,
            square,
            pltpu.VMEM((width + 16, 128), F32),
            pltpu.VMEM((24, ring_width), F32),
            pltpu.VMEM((24, ring_width), F32),
            pltpu.VMEM((NK, 128), F32),
            pltpu.VMEM((ring_width, NK), BF16),
            pltpu.VMEM((ring_width, NK), BF16),
            pltpu.VMEM((3, NK, levels), F32),
            square,
            pltpu.VMEM((NPOLE, ring_width), F32),
            pltpu.VMEM((blocks, 16, width), F32),
            pltpu.VMEM((2, width, 128), F32),
            pltpu.VMEM((2, width, 128), F32),
            pltpu.VMEM((2, width, 128), F32),
            pltpu.VMEM((128, width), F32),
            pltpu.VMEM((NK, 128), F32),
            pltpu.VMEM((2, NK, 128), F32),
            pltpu.VMEM((256, 256), BF16),
            pltpu.SemaphoreType.DMA((9 * blocks + 32,)),
            pltpu.SemaphoreType.DMA((CAP,)),
        ]
        + extra,
        input_output_aliases=aliases,
        compiler_params=pltpu.CompilerParams(vmem_limit_bytes=VMEM_LIMIT),
        cost_estimate=pl.CostEstimate(
            flops=len(steps) * CAP * NK * levels * levels * 4,
            bytes_accessed=20_000_000,
            transcendentals=0,
        ),
        name="cap_steps",
    )(scal, *spec, *big, *small, *air)


def shift(x, axis, by, wrap):
    size = lax.axis_size(axis)
    pairs = [(i, (i + by) % size) for i in range(size) if wrap or 0 <= i + by < size]
    return lax.ppermute(x, axis, pairs)


def between_caps(x, by):
    size, bands = lax.axis_size("lon"), lax.axis_size("lat")
    pairs = [(b * size + i, b * size + (i ^ by)) for b in (0, bands - 1) for i in range(size)]
    return lax.ppermute(x, ("lat", "lon"), pairs)


def spread(copies):
    return lax.all_to_all(copies, "lon", split_axis=0, concat_axis=0, tiled=True)


def local(air_temp, sea_temp, land_sea, courant, vertical_mix, cutoffs):
    rows, count, levels = air_temp.shape
    blocks, bands = lax.axis_size("lon"), lax.axis_size("lat")
    nlon = blocks * count
    width = round_up(count + 2 * HALO, 128)
    depth = round_up(count, 128)
    fast = count % 8 == 0
    band, block = lax.axis_index("lat"), lax.axis_index("lon")
    flip = band == bands - 1
    polar = (band == 0) | flip

    cut = jnp.where(flip, cutoffs[::-1][:NPOLE], cutoffs[:NPOLE])
    head = jnp.stack([flip, polar, block]).astype(jnp.int32)
    scal = jnp.concatenate([head, cut, jnp.full((STEPS + 4,), KMAX, jnp.int32)])
    window, forward, weight = tables(blocks, count, width, depth)
    t_high, t_low = (jnp.asarray(part) for part in window)
    rotate = rotations(nlon)
    rotate_owned = jnp.asarray(rotate[:, owner_order(blocks)])
    rotate = jnp.asarray(rotate)
    weights = jnp.asarray(np.tile(weight.astype(np.float32), (8, 1)))
    courant = courant.reshape(1, levels)

    west = shift(air_temp[:, count - HALO :], "lon", 1, True)
    east = shift(air_temp[:, :HALO], "lon", -1, True)
    exchange_coef = jnp.where(land_sea == 1, sea_coef, land_coef).astype(F32)
    sea_blocks = sea_temp.reshape(-1, blocks, count).transpose(1, 0, 2).reshape(rows, count)
    mine = jnp.concatenate([sea_blocks, exchange_coef], 0)
    got = spread(jnp.broadcast_to(mine[None], (blocks,) + mine.shape))
    half = blocks // 2
    keep, send = start_spectra(blocks, scal, air_temp, jnp.asarray(forward))
    send, west, east, got = lax.optimization_barrier((send, west, east, got))

    half_sum = keep + between_caps(send, 1)

    def edge(part):
        return jnp.concatenate([west[part], air_temp[part], east[part]], 1)

    north = shift(edge(slice(rows - ROW0, rows)), "lat", 1, False)
    south = shift(edge(slice(0, ROW0)), "lat", -1, False)
    own_window, sea_ring, coef_ring = windows(rows, count, width, blocks, scal, got)
    above = shift(own_window[:, rows - ROW0 :], "lat", 1, False)
    below = shift(own_window[:, :ROW0], "lat", -1, False)

    if fast:
        air = air_temp
    else:
        middle = jnp.concatenate([west, air_temp, east], 1)
        air = jnp.concatenate([north, middle, south], 0)
        air = jnp.pad(air, ((0, 0), (0, width - count - 2 * HALO), (0, 0)))
    half_sum, own_window = lax.optimization_barrier((half_sum, own_window))
    parts = [between_caps(half_sum[j], 2 * j) for j in range(1, half)]
    outs = outside_steps(
        rows, count, width, fast, (1, 2, 3), scal, (air, west, east, north, south),
        (own_window, above, below, courant, vertical_mix),
    )
    state, early, sea, coef, gathered = outs[0], tuple(outs[1:5]), outs[5], outs[6], outs[7]
    parts, state = lax.optimization_barrier((parts, state))
    gathered, late_free = free_steps(
        blocks, scal, (half_sum[0], *parts), rotate_owned, courant, vertical_mix, gathered
    )
    gathered, state = lax.optimization_barrier((gathered, state))
    late_pair = jnp.stack([late_free, between_caps(late_free, 1)])
    free = spread(gathered)
    outs = outside_steps(
        rows, count, width, fast, (4, 5, 6), scal, (state,),
        (early[2], early[3], coef, courant, vertical_mix),
    )
    air, late = outs[0], tuple(outs[1:5])
    free, air, late = lax.optimization_barrier((free, air, late))

    more, spec = (), ()
    for steps in ((1, 2), (3, 4), (5, 6)):
        hists = sum(((early, late)[h] for h in cap_hists(steps)), ())
        big = hists + (free, t_high, t_low, rotate, coef, sea, sea_ring, coef_ring) + more
        if steps[-1] == STEPS:
            big += tuple(late_free)
        outs = cap_steps(
            rows, count, width, blocks, fast, steps, scal, spec, big,
            (weights, courant, vertical_mix), (air,) if steps[-1] == STEPS else (),
        )
        if steps[-1] < STEPS:
            spec, wedge, sea, flux, sea_ring, ring_flux, mine = outs
            if steps[0] == 1:
                late_pair, mine = lax.optimization_barrier((late_pair, mine))
                late_free = [late_pair] + [
                    between_caps(late_pair, 2 * j) for j in range(1, half)
                ]
            gathered = spread(mine)
            spec, more = (spec,), (gathered, flux, ring_flux, wedge)
    air, sea = outs
    if not fast:
        air = air[:, HALO : HALO + count]
    sea = sea[:, HALO : HALO + count]
    sea = lax.all_to_all(sea, "lon", split_axis=0, concat_axis=1, tiled=True)
    return air, sea


def solution(mesh):
    placed = (P("lat", "lon", None), P(("lat", "lon"), None), P("lat", "lon"), P(), P(), P())
    return jax.shard_map(
        local,
        mesh=mesh,
        in_specs=placed,
        out_specs=(P("lat", "lon", None), P(("lat", "lon"), None)),
        check_vma=False,
    )
```

```python
import functools
import math

import jax
import jax.numpy as jnp
import ml_dtypes
import numpy as np
from jax import lax
from jax.experimental import pallas as pl
from jax.experimental.pallas import tpu as pltpu
from jax.sharding import PartitionSpec as P

NPOLE = 16
KMAX = 127
STEPS = 6
NK = 2 * (KMAX + 1)
CAP = NPOLE + STEPS
HALO = 8
ROW0 = STEPS
WEDGE = STEPS - 1
BEYOND = 5
SPLIT = 2

diffusion_rate = 0.1
air_gain = 0.5
ocean_gain = 0.3
ocean_diffusion = 0.2
sea_coef = 0.5
land_coef = 0.15

F32 = jnp.float32
BF16 = jnp.bfloat16
VMEM_LIMIT = 56 * 1024 * 1024


def round_up(value, unit):
    return -(-value // unit) * unit


def two_parts(x):
    high = x.astype(BF16)
    return high, (x - high.astype(F32)).astype(BF16)


def dot(a, b):
    return jnp.dot(a, b, preferred_element_type=F32)


def dot_nt(a, b):
    return lax.dot_general(a, b, (((1,), (1,)), ((), ())), preferred_element_type=F32)


def table_dot(high, low, x):
    x_high, x_low = two_parts(x)
    both = dot(high, jnp.concatenate([x_high, x_low], axis=1))
    return both[:, :128] + both[:, 128:] + dot(low, x_high)


def numpy_parts(table):
    high = table.astype(ml_dtypes.bfloat16)
    low = (table - high.astype(np.float64)).astype(ml_dtypes.bfloat16)
    return high, low


def owner_order(blocks):
    k = np.arange(KMAX + 1).reshape(blocks, -1)
    return np.concatenate([k, k + KMAX + 1], 1).reshape(-1)


@functools.lru_cache(maxsize=None)
def tables(blocks, count, width, depth):
    nlon = blocks * count
    wavenum = np.arange(KMAX + 1)
    weight = np.where(wavenum == 0, 1.0, 2.0) / nlon

    def table(columns):
        phase = (columns[:, None] * wavenum[None, :]) % nlon * (2.0 * math.pi / nlon)
        return np.concatenate([np.cos(phase), np.sin(phase)], 1)

    window = np.concatenate(
        [table((j * count - HALO + np.arange(width)) % nlon) for j in range(blocks)], 0
    )
    forward = np.zeros((blocks, NK, depth))
    for j in range(blocks):
        own = table(j * count + np.arange(count)) * np.tile(weight, 2)
        forward[j, :, :count] = own.T[owner_order(blocks)]
    high, low = numpy_parts(forward)
    return numpy_parts(window), np.concatenate([high, high, low], 2), np.tile(weight, 2)


@functools.lru_cache(maxsize=None)
def rotations(nlon):
    theta = np.arange(KMAX + 1) * (2.0 * math.pi / nlon)
    stay = 1.0 - 4.0 * diffusion_rate + 2.0 * diffusion_rate * np.tile(np.cos(theta), 2)
    turn = np.concatenate([-np.sin(theta), np.sin(theta)])
    both = np.stack([stay, turn]).astype(np.float32)
    return np.ascontiguousarray(np.broadcast_to(both[:, :, None], (2, NK, 128)))


def mixing(mix, vcat):
    row = lax.broadcasted_iota(jnp.int32, (128, 128), 0)
    high, low = two_parts(jnp.where(row == lane_iota((128, 128)), mix[...] + 1.0, mix[...]))
    vcat[0:128, 0:128] = high
    vcat[128:256, 0:128] = high
    vcat[0:128, 128:256] = low
    vcat[128:256, 128:256] = jnp.zeros_like(low)


def winds(courant):
    c = courant[0:1, :]
    top = jnp.broadcast_to(c[:, 0:1], c.shape)
    return [diffusion_rate + sign * 0.5 * x for x in (c, top) for sign in (-1.0, 1.0)]


def lane_iota(shape):
    return lax.broadcasted_iota(jnp.int32, shape, len(shape) - 1)


def spectra_kernel(
    rows, count, blocks,
    scal, air, table, keep_out, send_out,
    held, own_table, stacked_a, stacked_b, sums, keep, send, sems,
):
    depth = stacked_a.shape[0] // 3
    half, part = blocks // 2, NK // blocks
    flip, block = scal[0], scal[2]
    side, place = lax.rem(block, 2), block // 2
    pairs = CAP // 2

    def row(q):
        r = jnp.where(flip == 1, rows - 1 - q, q)
        return pltpu.make_async_copy(air.at[r], held.at[q], sems.at[q])

    @pl.when(scal[1] == 1)
    def _():
        fetch = pltpu.make_async_copy(table.at[block], own_table, sems.at[CAP])
        row(0).start()
        row(1).start()
        fetch.start()

        @pl.loop(2, CAP)
        def _(q):
            row(q).start()

        for ref in (stacked_a, stacked_b):
            ref[...] = jnp.zeros_like(ref)

        def load(p, slot):
            ref = (stacked_a, stacked_b)[slot]
            for n in range(2):
                high, low = two_parts(held[2 * p + n])
                lanes = slice(128 * n, 128 * n + 128)
                ref[0:count, lanes] = high
                ref[depth : depth + count, lanes] = low
                ref[2 * depth : 2 * depth + count, lanes] = high

        def finish(p, slot, between):
            sums[slot] = dot(own_table[...], (stacked_a, stacked_b)[slot][...])
            between()
            for n in range(2):
                lanes = slice(128 * n, 128 * n + 128)
                for z in range(half):
                    at = jnp.bitwise_xor(place, z)
                    mine = pl.multiple_of((side * half + z) * part, part)
                    other = pl.multiple_of(((1 - side) * half + z) * part, part)
                    keep[at, 2 * p + n] = sums[slot, pl.ds(mine, part), lanes]
                    send[at, 2 * p + n] = sums[slot, pl.ds(other, part), lanes]

        def arrive(n):
            for q in range(2, 6):
                row(4 * n + q).wait()

        row(0).wait()
        row(1).wait()
        fetch.wait()
        two_at_a_time(0, pairs // 2, load, finish, arrive)
        finish(pairs - 1, 0, lambda: None)
        out = [
            pltpu.make_async_copy(send.at[:, pl.ds(0, CAP)], send_out, sems.at[0]),
            pltpu.make_async_copy(keep.at[:, pl.ds(0, CAP)], keep_out, sems.at[1]),
        ]
        for copy in out:
            copy.start()
        for copy in out:
            copy.wait()


def start_spectra(blocks, scal, air_temp, table):
    rows, count, levels = air_temp.shape
    half, part = blocks // 2, NK // blocks
    depth = table.shape[2] // 3
    any_spec = pl.BlockSpec(memory_space=pl.ANY)
    out = jax.ShapeDtypeStruct((half, CAP, part, levels), F32)
    return pl.pallas_call(
        functools.partial(spectra_kernel, rows, count, blocks),
        out_shape=[out, out],
        in_specs=[pl.BlockSpec(memory_space=pltpu.SMEM), any_spec, any_spec],
        out_specs=[any_spec, any_spec],
        scratch_shapes=[
            pltpu.VMEM((CAP, count, levels), F32),
            pltpu.VMEM((NK, 3 * depth), BF16),
            pltpu.VMEM((3 * depth, 2 * levels), BF16),
            pltpu.VMEM((3 * depth, 2 * levels), BF16),
            pltpu.VMEM((2, NK, 2 * levels), F32),
            pltpu.VMEM((half, CAP, part, levels), F32),
            pltpu.VMEM((half, CAP, part, levels), F32),
            pltpu.SemaphoreType.DMA((CAP + 2,)),
        ],
        compiler_params=pltpu.CompilerParams(vmem_limit_bytes=VMEM_LIMIT),
        name="start_spectra",
    )(scal, air_temp, table)


def free_kernel(blocks, parts, scal, *refs):
    sums, refs = refs[:parts], refs[parts:]
    rotate, courant, mix, edge, early, late, state, mask, xcat, vcat = refs
    part = NK // blocks
    some = part // 2
    owner = lax.rem(scal[2], 2) * (blocks // 2) + scal[2] // 2

    @pl.when(scal[1] == 1)
    def _():
        mixing(mix, vcat)
        state[0] = jnp.zeros((part, 128), F32)
        state[1 : CAP + 1] = functools.reduce(jnp.add, [ref[...] for ref in sums])
        at = pl.ds(pl.multiple_of(owner * part, part), part)
        stay, turn = rotate[0, at, :], rotate[1, at, :] * courant[0:1, :]
        wavenum = lax.broadcasted_iota(jnp.int32, (part, 128), 0) % some + owner * some
        for q in range(CAP):
            mask[q] = jnp.where(wavenum <= scal[3 + q], 1.0, 0.0)
        first = lane_iota((part, 128)) == 0
        top = jnp.zeros((part, 128), F32)
        for step in range(1, STEPS + 1):
            size = CAP - step
            here = state[1 : size + 1]
            swapped = jnp.concatenate([here[:, some:], here[:, :some]], axis=1)
            x = stay * here + diffusion_rate * (state[0:size] + state[2 : size + 2])
            x = (x + turn * swapped) * mask[0:size]
            x = x.reshape(size * part, 128)
            high, low = two_parts(x)
            xcat[0 : size * part, 0:128] = high
            xcat[0 : size * part, 128:256] = low
            mixed = dot(xcat[0 : size * part, :], vcat[...])
            y = mixed[:, :128] + mixed[:, 128:]
            state[1 : size + 1] = y.reshape(size, part, 128)
            for q in range(NPOLE):
                lane = NPOLE * (step - 1) + q
                top += pltpu.roll(jnp.where(first, state[q + 1], 0.0), lane, 1)
            if step < STEPS:
                for to in range(blocks):
                    early[to, part * step : part * (step + 1), :] = state[NPOLE]
            else:
                late[...] = state[1 : NPOLE + 1]
        for to in range(blocks):
            early[to, 0:part, :] = top
            early[to, STEPS * part :, :] = edge[...]


def free_steps(blocks, scal, sums, rotate, courant, mix, edge):
    part = NK // blocks
    vmem = pl.BlockSpec(memory_space=pltpu.VMEM)
    shape = jax.ShapeDtypeStruct
    return pl.pallas_call(
        functools.partial(free_kernel, blocks, len(sums)),
        out_shape=[
            shape((blocks, STEPS * part + edge.shape[0], 128), F32),
            shape((NPOLE, part, 128), F32),
        ],
        in_specs=[pl.BlockSpec(memory_space=pltpu.SMEM)] + [vmem] * (len(sums) + 4),
        out_specs=[vmem] * 2,
        scratch_shapes=[
            pltpu.VMEM((CAP + 2, part, 128), F32),
            pltpu.VMEM((CAP, part, 128), F32),
            pltpu.VMEM((CAP * part, 256), BF16),
            pltpu.VMEM((256, 256), BF16),
        ],
        compiler_params=pltpu.CompilerParams(vmem_limit_bytes=VMEM_LIMIT // 4),
        name="free_steps",
    )(scal, *sums, rotate, courant, mix, edge)


def advance(
    width, here_ref, base, north_ref, north, south_ref, south, cour, xcat, more=None, to=0
):
    c_east, c_west = cour
    for o in range(0, width, 128):
        around = north_ref[pl.ds(north + o, 128), :] + south_ref[pl.ds(south + o, 128), :]
        x = (
            (1.0 - 4.0 * diffusion_rate) * here_ref[pl.ds(base + o, 128), :]
            + diffusion_rate * around
            + c_east * here_ref[pl.ds(base + o + 1, 128), :]
            + c_west * here_ref[pl.ds(base + o - 1, 128), :]
        )
        if more is not None:
            moved = pltpu.roll(more[0][pl.ds(o, 128), :], more[1], 1)
            x += jnp.where(lane_iota(x.shape) == 0, moved, 0.0)
        high, low = two_parts(x)
        xcat[pl.ds(to + o, 128), 0:128] = high
        xcat[pl.ds(to + o, 128), 128:256] = low


def two_at_a_time(first, pairs, load, finish, arrive=None, size=1):
    load(first, 0)

    @pl.loop(0, pairs)
    def _(n):
        if arrive is not None:
            arrive(n)
        q = first + 2 * size * n
        finish(q, 0, lambda: load(q + size, 1))
        finish(q + size, 1, lambda: load(q + 2 * size, 0))


def exchange(y, lane, sea, coef):
    back = (128 - lane) % 128
    flux = pltpu.roll(coef, back, 1) * (pltpu.roll(sea, back, 1) - y)
    return jnp.where(lane_iota(y.shape) == 0, flux, 0.0)


def sea_next(width, polar, rows, sea, flux, pad):
    pad[pl.ds(8, width), :] = sea
    east = pad[pl.ds(9, width), :]
    west = pad[pl.ds(7, width), :]
    around = east + west + pltpu.roll(sea, 1, 1) + pltpu.roll(sea, 127, 1)
    new = sea - ocean_gain * flux + ocean_diffusion * (around - 4.0 * sea)
    lane = lane_iota(sea.shape)
    first = jnp.where(polar == 1, ROW0, 0)
    return jnp.where((lane >= first) & (lane < rows + 2 * ROW0), new, 0.0)


def windows_kernel(rows, count, width, blocks, scal, got, air, west, east, *refs):
    own, ring_sea, ring_coef = refs[:3]
    wide, sems = refs[-2:]
    edges = list(zip(refs[3:-2], (rows - ROW0, 0)))
    copies = []
    for n, (ref, first) in enumerate(edges):
        some = pl.ds(first, ROW0)
        for m, (source, offset, size) in enumerate(
            ((west, 0, HALO), (air, HALO, count), (east, HALO + count, HALO))
        ):
            copies.append(
                pltpu.make_async_copy(
                    source.at[some], ref.at[:, pl.ds(offset, size)], sems.at[3 * n + m]
                )
            )
    for copy in copies:
        copy.start()
    per = rows // blocks
    for j in range(blocks):
        columns = slice(j * width + HALO, j * width + HALO + count)
        for i in range(blocks):
            wide[0, per * i : per * (i + 1), columns] = got[i, per * j : per * (j + 1), :]
        wide[1, :, columns] = got[j, rows:, :]
    rest = width - HALO - count
    for j in range(blocks):
        before = ((j - 1) % blocks) * width + count
        after = ((j + 1) % blocks) * width + HALO
        end = j * width + HALO + count
        wide[:, :, j * width : j * width + HALO] = wide[:, :, before : before + HALO]
        wide[:, :, end : end + rest] = wide[:, :, after : after + rest]
    own[...] = wide[:, :, pl.ds(pl.multiple_of(scal[2] * width, 128), width)]
    for ref, first in edges:
        base = count + 2 * HALO
        for n in range(2):
            for r in range(ROW0):
                for o in range(width // 128):
                    at = base + n * (width // 128) + o
                    ref[r, at : at + 1, :] = own[n, first + r : first + r + 1, pl.ds(128 * o, 128)]

    @pl.when(scal[1] == 1)
    def _():
        @pl.loop(0, 24)
        def _(q):
            r = jnp.where(scal[0] == 1, rows - 1 - q, q)
            ring_sea[pl.ds(q, 1), :] = wide[0, pl.ds(r, 1), :]

        @pl.loop(0, NPOLE)
        def _(q):
            r = jnp.where(scal[0] == 1, rows - 1 - q, q)
            ring_coef[pl.ds(q, 1), :] = wide[1, pl.ds(r, 1), :]

    for copy in copies:
        copy.wait()


def edge_extent(count, width):
    inner = count + 2 * HALO
    return round_up(inner, 8), round_up(inner, 8) + 8


def windows(rows, count, width, blocks, fast, scal, got, air, west, east):
    any_spec = pl.BlockSpec(memory_space=pl.ANY)
    edges = [jax.ShapeDtypeStruct((ROW0, edge_extent(count, width)[1], 128), F32)] * 2
    vmem = pl.BlockSpec(memory_space=pltpu.VMEM)
    shape = jax.ShapeDtypeStruct
    return pl.pallas_call(
        functools.partial(windows_kernel, rows, count, width, blocks),
        out_shape=[
            shape((2, rows, width), F32),
            shape((24, blocks * width), F32),
            shape((NPOLE, blocks * width), F32),
        ]
        + (edges if fast else []),
        in_specs=[pl.BlockSpec(memory_space=pltpu.SMEM), vmem] + [any_spec] * 3,
        out_specs=[vmem] * (5 if fast else 3),
        scratch_shapes=[
            pltpu.VMEM((2, rows, blocks * width), F32),
            pltpu.SemaphoreType.DMA((6,)),
        ],
        compiler_params=pltpu.CompilerParams(vmem_limit_bytes=VMEM_LIMIT),
        name="windows",
    )(scal, got, air, west, east)


def outside_kernel(rows, count, width, fast, steps, scal, *refs):
    first, last = steps[0] == 1, steps[-1] == STEPS
    if first:
        (air, west, east, north, south, own, courant, mix), refs = refs[:8], refs[8:]
        (state, *hist_outs, sea_start, coef_out, gather_out), refs = refs[:8], refs[8:]
    else:
        (state, sea_hist_in, flux_hist_in, coef_in, courant, mix), refs = refs[:6], refs[6:]
        (air_out, *hist_outs), refs = refs[:5], refs[5:]
    (buf_a, buf_b, xcat_a, xcat_b, sea, flux, point, more, turn, pad, vcat, edge_seas,
     coef, wedge, side, sea_hist, flux_hist, hist_sems, sems) = refs
    flip, polar = scal[0], scal[1]
    total = rows + 2 * ROW0
    inner = count + 2 * HALO
    lanes = lane_iota((width, 128))
    hist = tuple(zip((wedge, side, sea_hist, flux_hist), hist_outs))

    def hist_copies(n, kinds):
        return [
            pltpu.make_async_copy(hist[k][0].at[n], hist[k][1].at[n], hist_sems.at[4 * n + k])
            for k in kinds
        ]

    def base_of(q):
        return pl.multiple_of(8 + (q + ROW0) * width, 8)

    def q_of(r):
        return jnp.where(flip == 1, rows - 1 - r, r)

    def low_row(step):
        return jnp.where(polar == 1, NPOLE + step - 1, step - STEPS)

    def row_range(body, step, *sizes):
        hi = rows - 1 + STEPS - step
        ref, extent, sem = sizes

        @pl.loop(low_row(step), hi + 1)
        def _(q):
            body(q).start()

        for kind, count_rows in ((1, hi + 1 - NPOLE - step + 1), (0, hi + 1 + STEPS - step)):
            @pl.when(polar == kind)
            def _(count_rows=count_rows):
                whole = ref.at[pl.ds(0, count_rows * extent)]
                pltpu.make_async_copy(whole, whole, sem).wait()

    def begin():
        mixing(mix, vcat)
        beyond = 8 + total * width
        for ref in (buf_a, buf_b):
            ref[0:8, :] = jnp.zeros((8, 128), F32)
            ref[pl.ds(beyond, BEYOND * width + 8), :] = jnp.zeros((BEYOND * width + 8, 128), F32)
        pad[...] = jnp.zeros_like(pad)

    if first:
        needed = jnp.where(polar == 1, NPOLE - 1, -ROW0)
        at, after = edge_extent(count, width)
        for n, ref in enumerate((north, south)):
            pltpu.make_async_copy(
                ref.at[:, pl.ds(at, 8)], edge_seas.at[n], sems.at[2 + n]
            ).start()
        if fast:
            @pl.loop(0, rows)
            def _(r):
                @pl.when(q_of(r) >= needed)
                def _():
                    base = base_of(q_of(r))
                    for ref, offset, size in (
                        (west, 0, HALO), (air, HALO, count), (east, HALO + count, HALO)
                    ):
                        pltpu.make_async_copy(
                            ref.at[r], buf_a.at[pl.ds(base + offset, size)], sems.at[0]
                        ).start()

            @pl.loop(0, ROW0)
            def _(r):
                for ref, place in ((north, r - ROW0), (south, r + rows)):
                    @pl.when(q_of(place) >= needed)
                    def _(ref=ref, place=place):
                        pltpu.make_async_copy(
                            ref.at[r, pl.ds(0, inner)],
                            buf_a.at[pl.ds(base_of(q_of(place)), inner)],
                            sems.at[0],
                        ).start()

            if inner < width:
                @pl.loop(0, total)
                def _(e):
                    buf_a[pl.ds(base_of(e - ROW0) + inner, width - inner), :] = jnp.zeros(
                        (width - inner, 128), F32
                    )

            extents = ((1, (rows + ROW0 - NPOLE + 1) * inner), (0, total * inner))
        else:
            @pl.loop(0, total)
            def _(e):
                pltpu.make_async_copy(
                    air.at[e], buf_a.at[pl.ds(base_of(q_of(e - ROW0)), width)], sems.at[0]
                ).start()

            extents = ((1, total * width), (0, total * width))
        begin()
        for n, ref in enumerate((north, south)):
            pltpu.make_async_copy(
                ref.at[:, pl.ds(at, 8)], edge_seas.at[n], sems.at[2 + n]
            ).wait()
        chunks = width // 128
        for n, ref in ((0, sea), (1, coef)):
            turn[...] = jnp.zeros_like(turn)

            @pl.loop(0, rows)
            def _(r):
                turn[pl.ds(q_of(r) + ROW0, 1), :] = own[n, pl.ds(r, 1), :]

            for m, place in ((0, -ROW0), (1, rows)):
                @pl.loop(0, ROW0)
                def _(r, m=m, place=place):
                    pieces = [
                        edge_seas[m, r, pl.ds(n * chunks + o, 1), :] for o in range(chunks)
                    ]
                    turn[pl.ds(q_of(r + place) + ROW0, 1), :] = jnp.concatenate(pieces, axis=1)

            ref[...] = jnp.transpose(turn[...])
        sea_start[...] = sea[...]
        coef_out[...] = coef[...]
        for kind, extent in extents:
            @pl.when(polar == kind)
            def _(extent=extent):
                whole = buf_a.at[pl.ds(0, extent)]
                pltpu.make_async_copy(whole, whole, sems.at[0]).wait()
    else:
        small = [
            pltpu.make_async_copy(source, target, sems.at[1 + n])
            for n, (source, target) in enumerate(
                ((sea_hist_in.at[SPLIT - 1], sea), (flux_hist_in.at[SPLIT - 1], flux),
                 (coef_in, coef))
            )
        ]
        for copy in small:
            copy.start()
        begin()
        for copy in small:
            copy.wait()
        row_range(
            lambda q: pltpu.make_async_copy(
                state.at[q + ROW0], buf_a.at[pl.ds(base_of(q), width)], sems.at[0]
            ),
            steps[0] - 1, buf_a, width, sems.at[0],
        )

    def with_flux(y, q):
        gain = air_gain * pltpu.roll(flux[...], 128 - (q + ROW0), 1)
        return y + jnp.where(lanes == 0, gain, 0.0)

    xcats = (xcat_a, xcat_b)
    cour = winds(courant)
    src, dst = buf_a, buf_b
    for n, step in enumerate(steps):
        lo = low_row(step)
        hi = rows - 1 + STEPS - step
        pairs = jnp.where(polar == 1, (hi - NPOLE - step + 3) // 2, (hi + 1 + STEPS - step) // 2)
        if step > 1:
            gain = air_gain * flux[...]
            pad[pl.ds(8, width), :] = gain
            more[...] = (
                (1.0 - 4.0 * diffusion_rate) * gain
                + diffusion_rate * (pltpu.roll(gain, 1, 1) + pltpu.roll(gain, 127, 1))
                + cour[2] * pad[pl.ds(9, width), :]
                + cour[3] * pad[pl.ds(7, width), :]
            )
        point[...] = jnp.zeros_like(point)

        def load(q, slot, src=src, step=step):
            for n in range(2):
                base = base_of(q + n)
                shared = (more, lax.rem(128 - (q + n + ROW0), 128)) if step > 1 else None
                advance(width, src, base, src, base - width, src, base + width, cour[:2],
                        xcats[slot], shared, n * width)

        def finish(q, slot, between, dst=dst):
            mixed = dot(xcats[slot][...], vcat[...])
            between()
            tops = []
            for n in range(2):
                row = slice(n * width, (n + 1) * width)
                y = mixed[row, :128] + mixed[row, 128:]
                dst[pl.ds(base_of(q + n), width), :] = y
                tops.append(pltpu.roll(jnp.where(lanes == 0, y, 0.0), q + n + ROW0, 1))
            point[...] += tops[0] + tops[1]

        two_at_a_time(lo, pairs // 2, load, finish, None, 2)

        @pl.when(lax.rem(pairs, 2) == 1)
        def _(finish=finish, lo=lo, pairs=pairs):
            finish(lo + 2 * (pairs - 1), 0, lambda: None)

        total_flux = jnp.where(lanes >= lo + ROW0, coef[...] * (sea[...] - point[...]), 0.0)
        flux[...] = total_flux
        new_sea = sea_next(width, polar, rows, sea[...], total_flux, pad)
        sea[...] = new_sea
        sea_hist[n] = new_sea
        flux_hist[n] = total_flux
        for copy in hist_copies(n, (2, 3)):
            copy.start()
        if step <= WEDGE:
            @pl.when(polar == 1)
            def _(dst=dst, step=step, n=n):
                for ref, q in ((wedge, NPOLE + step - 1), (side, NPOLE + step)):
                    ref[n] = with_flux(dst[pl.ds(base_of(q), width), :], q)
                for copy in hist_copies(n, (0, 1)):
                    copy.start()
        src, dst = dst, src

    if first:
        state_rows = row_range(
            lambda q: pltpu.make_async_copy(
                src.at[pl.ds(base_of(q), width)], state.at[q + ROW0], sems.at[1]
            ),
            steps[-1], src, width, sems.at[1],
        )
        for n in range(len(steps)):
            for copy in hist_copies(n, (2, 3)):
                copy.wait()
        turned = jnp.transpose(flux_hist[0])[NPOLE + ROW0 : NPOLE + ROW0 + 8]
        for o in range(width // 128):
            gather_out[8 * o : 8 * o + 8, :] = turned[:, 128 * o : 128 * o + 128]
    else:
        for n in range(len(steps)):
            for copy in hist_copies(n, (2, 3)):
                copy.wait()
        start, extent = (HALO, count) if fast else (0, width)
        first_row = jnp.where(polar == 1, NPOLE + WEDGE, 0)

        @pl.loop(first_row, rows)
        def _(q):
            row = pl.ds(base_of(q), width)
            src[row, :] = with_flux(src[row, :], q)
            pltpu.make_async_copy(
                src.at[pl.ds(base_of(q) + start, extent)], air_out.at[q_of(q)], sems.at[1]
            ).start()

        for kind, count_rows in ((1, rows - NPOLE - WEDGE), (0, rows)):
            @pl.when(polar == kind)
            def _(count_rows=count_rows):
                whole = src.at[pl.ds(0, count_rows * extent)]
                pltpu.make_async_copy(whole, whole, sems.at[1]).wait()

    @pl.when(polar == 1)
    def _():
        for n, step in enumerate(steps):
            if step <= WEDGE:
                for copy in hist_copies(n, (0, 1)):
                    copy.wait()


def outside_steps(rows, count, width, fast, steps, scal, big, small):
    levels = 128
    any_spec = pl.BlockSpec(memory_space=pl.ANY)
    vmem = pl.BlockSpec(memory_space=pltpu.VMEM)
    total = rows + 2 * ROW0
    shape = jax.ShapeDtypeStruct
    square = shape((width, 128), F32)
    hist = [shape((len(steps), width, 128), F32)] * 4
    if steps[0] == 1:
        out_shape = [shape((total, width, levels), F32)] + hist + [square, square]
        out_shape.append(shape((width // 16, 128), F32))
    else:
        out_shape = [shape((rows, count if fast else width, levels), F32)] + hist
    return pl.pallas_call(
        functools.partial(outside_kernel, rows, count, width, fast, steps),
        out_shape=out_shape,
        in_specs=[pl.BlockSpec(memory_space=pltpu.SMEM)]
        + [any_spec] * len(big)
        + [vmem] * len(small),
        out_specs=[any_spec] * 5 + [vmem] * (len(out_shape) - 5),
        scratch_shapes=[
            pltpu.VMEM(((total + BEYOND) * width + 16, levels), F32),
            pltpu.VMEM(((total + BEYOND) * width + 16, levels), F32),
            pltpu.VMEM((2 * width, 2 * levels), BF16),
            pltpu.VMEM((2 * width, 2 * levels), BF16),
            pltpu.VMEM((width, 128), F32),
            pltpu.VMEM((width, 128), F32),
            pltpu.VMEM((width, 128), F32),
            pltpu.VMEM((width, 128), F32),
            pltpu.VMEM((128, width), F32),
            pltpu.VMEM((width + 16, 128), F32),
            pltpu.VMEM((256, 256), BF16),
            pltpu.VMEM((2, ROW0, 8, 128), F32),
            pltpu.VMEM((width, 128), F32),
        ]
        + [pltpu.VMEM((len(steps), width, 128), F32)] * 4
        + [
            pltpu.SemaphoreType.DMA((4 * len(steps),)),
            pltpu.SemaphoreType.DMA((4,)),
        ],
        compiler_params=pltpu.CompilerParams(vmem_limit_bytes=VMEM_LIMIT),
        cost_estimate=pl.CostEstimate(
            flops=len(steps) * rows * width * levels * levels * 4,
            bytes_accessed=rows * width * levels * 10,
            transcendentals=0,
        ),
        name="outside_steps",
    )(scal, *big, *small)


def cap_kernel(rows, count, width, blocks, fast, steps, parts, scal, *refs):
    last = steps[-1] == STEPS
    wedge_steps = [step + 1 for step in steps if step < STEPS]
    spec_in, refs = refs[:parts], refs[parts:]
    hists, refs = refs[: 4 * len(cap_hists(steps))], refs[4 * len(cap_hists(steps)) :]
    names = ["free", "t_high", "t_low", "rotate", "coef", "sea", "sea_ring", "coef_ring"]
    if steps[0] > 1:
        names += ["gathered", "flux", "ring_flux", "wedge"]
    if last:
        names += list(range(blocks // 2))
    loads = dict(zip(names, refs[: len(names)]))
    refs = refs[len(names) :]
    small_in, refs = refs[:3], refs[3:]
    if last:
        refs = refs[1:]
        (air_out, sea_out), refs = refs[:2], refs[2:]
    else:
        (spec_out, wedge_out, sea_out, flux_out, sea_ring_out, ring_out, gather_to), refs = (
            refs[:7], refs[7:])
    (spec_a, spec_b, cur, prev, xcat, kcat_a, kcat_b, point, sea, flux, pad,
     ring, sea_ring, shares, t_high, t_low, stencil, coef, coef_ring, gathered, sea_hist,
     flux_hist, side, turn, free_top, free_row, vcat, weight, courant, mix, load_sems, row_sems) = refs[:32]
    if last:
        back, free_late, sems = refs[32:]
    else:
        gather_out, store_sems = refs[32:]
    flip, polar, block = scal[0], scal[1], scal[2]
    lanes = lane_iota((width, 128))
    own = pl.ds(pl.multiple_of(block * width, 128), width)

    def hist(kind, step):
        half = 0 if step <= SPLIT else 1
        return hists[4 * cap_hists(steps).index(half) + kind].at[step - 1 - SPLIT * half]

    def own_dot(x):
        return table_dot(t_high[own, :], t_low[own, :], x)

    def wedge_step(step):
        at = wedge_steps.index(step)
        pending = flux_hist[at]
        for j in range(step - 1):
            base = 8 + j * width
            if j == step - 2:
                south_ref, south = side.at[at], 0
            else:
                south_ref, south = cur, base + width
            advance(width, cur, base, prev, 0, south_ref, south, winds(courant)[:2], xcat)
            prev[...] = cur[pl.ds(base, width), :]
            mixed = dot(xcat[...], vcat[...])
            y = mixed[:, :128] + mixed[:, 128:]
            lane = NPOLE + j + ROW0
            out = exchange(y, lane, sea[...], coef[...])
            cur[pl.ds(base, width), :] = y + air_gain * out
            pending += pltpu.roll(out, lane, 1)
        return pending

    def cap_step(step, src, dst, slot):
        count_rows = CAP - step
        if step > 1:
            ready("gathered", "sea_ring", "ring_flux")
        if step > 1:
            for j in range(blocks):
                ring[pl.ds(NPOLE, 8), pl.ds(j * width, width)] = gathered[
                    j, pl.ds(8 * slot, 8), :
                ]
            old, at = sea_ring[...], ring[...]
            place = lax.broadcasted_iota(jnp.int32, old.shape, 0)
            up = jnp.where(place == 0, 0.0, pltpu.roll(old, 1, 0))
            down = pltpu.roll(old, old.shape[0] - 1, 0)
            ring_width = blocks * width
            around = up + down + pltpu.roll(old, 1, 1) + pltpu.roll(old, ring_width - 1, 1)
            sea_ring[...] = old - ocean_gain * at + ocean_diffusion * (around - 4.0 * old)
            spot = lane_iota(at.shape) % width
            at = jnp.where((spot >= HALO) & (spot < HALO + count), at, 0.0)
            high, low = two_parts(at)
            ready("t_high", "t_low", "rotate", "weight")
            both = dot(jnp.concatenate([high, low], axis=0), t_high[...])
            sums = both[:24] + both[24:] + dot(high, t_low[...])
            sums = sums * (air_gain * weight[0:1, :])
            sums = jnp.concatenate([sums, jnp.zeros((104, NK), F32)], axis=0)
            moved = jnp.transpose(sums)
            swapped = jnp.concatenate([moved[128:], moved[:128]], axis=0)
            beside = pltpu.roll(moved, 1, 1) + pltpu.roll(moved, 127, 1)
            top = jnp.broadcast_to(courant[0:1, 0:1], (1, 128))
            shares[...] = (
                stencil[0] * moved + diffusion_rate * beside + (stencil[2] * top) * swapped
            )
            stencil[1] = stencil[2] * courant[0:1, :]

        point[...] = jnp.zeros_like(point)
        kcats = (kcat_a, kcat_b)
        first = lane_iota((128, 128)) == 0

        def load(q, slot):
            cut = scal[3 + q]
            for o, other in ((0, 128), (128, 0)):
                more = pltpu.roll(shares[pl.ds(o, 128), :], lax.rem(128 - q, 128), 1)
                x = jnp.where(first, more, 0.0)
                if step > 2:
                    here = src[q + 1, pl.ds(o, 128), :]
                    swapped = src[q + 1, pl.ds(other, 128), :]
                    around = src[q, pl.ds(o, 128), :] + src[q + 2, pl.ds(o, 128), :]
                    x += (
                        stencil[0, pl.ds(o, 128), :] * here
                        + diffusion_rate * around
                        + stencil[1, pl.ds(o, 128), :] * swapped
                    )
                x = jnp.where(lax.broadcasted_iota(jnp.int32, x.shape, 0) <= cut, x, 0.0)
                high, low = two_parts(x)
                kcats[slot][pl.ds(o, 128), 0:128] = high
                kcats[slot][pl.ds(o, 128), 128:256] = low

        streamed = step == steps[0] and step > 1

        def finish(q, slot, between):
            mixed = dot(kcats[slot][...], vcat[...])
            between()
            y = mixed[:, :128] + mixed[:, 128:]
            dst[q + 1] = y
            point[...] += pltpu.roll(jnp.where(lane_iota(y.shape) == 0, y, 0.0), q, 1)

        pairs = (count_rows + 1) // 2
        if streamed:
            spec_row(0).wait()
            spec_row(1).wait()

        def arrive(n):
            spec_row(2 * n + 2).wait()
            spec_row(2 * n + 3).wait()

        if step > 1:
            two_at_a_time(0, pairs, load, finish, arrive if streamed else None)
        if streamed:
            for q in range(2 * pairs + 2, CAP):
                spec_row(q).wait()
        if step == steps[-1] and not last:
            store(dst.at[pl.ds(1, CAP)], spec_out)
        ready("free")
        top = pltpu.roll(free_top[...], (128 - NPOLE * (step - 1)) % 128, 1)
        point[...] += jnp.where(lane_iota((NK, 128)) < NPOLE, top, 0.0)

        ready("t_high", "t_low", "sea_ring", "coef_ring", "coef", "sea", "flux", "hist")
        at_rows = jnp.transpose(point[...])[:NPOLE]
        high, low = two_parts(at_rows)
        both = dot_nt(jnp.concatenate([high, low], axis=0), t_high[...])
        surface = both[:NPOLE] + both[NPOLE:] + dot_nt(high, t_low[...])
        ring[0:NPOLE, :] = coef_ring[...] * (sea_ring[0:NPOLE, :] - surface)

        here = pltpu.roll(own_dot(point[...]), ROW0, 1)
        in_cap = (lanes >= ROW0) & (lanes < ROW0 + NPOLE)
        total = jnp.where(in_cap, coef[...] * (sea[...] - here), flux[...])
        flux[...] = total
        if step < STEPS:
            edge = pltpu.roll(total, 128 - (ROW0 + NPOLE - 1), 1)
            row = free_row[slot] if step == 1 else dst[NPOLE] + free_row[slot]
            prev[...] = own_dot(row) + air_gain * jnp.where(lanes == 0, edge, 0.0)
        new = sea_next(width, polar, rows, sea[...], total, pad)
        sea[...] = jnp.where(lanes >= ROW0 + NPOLE + step - 1, sea_hist[slot], new)

    copies = {}
    order = []
    stores = []

    def store(source, target):
        copy = pltpu.make_async_copy(source, target, store_sems.at[len(stores)])
        stores.append(copy)
        copy.start()

    def fetch(name, source, target):
        copy = pltpu.make_async_copy(source, target, load_sems.at[len(order)])
        order.append(copy)
        copies.setdefault(name, []).append(copy)
        copy.start()

    def ready(*wanted):
        for name in wanted:
            for copy in copies.pop(name, ()):
                copy.wait()

    def spec_row(q):
        return pltpu.make_async_copy(spec_in[0].at[q], spec_a.at[q + 1], row_sems.at[q])

    @pl.when(polar == 1)
    def _():
        for n, (source, target) in enumerate(zip(small_in, (weight, courant, mix))):
            fetch(("weight", "courant", "mix")[n], source, target)
        if steps[0] > 1:
            fetch("gathered", loads["gathered"], gathered)
            fetch("sea_ring", loads["sea_ring"], sea_ring)
            fetch("ring_flux", loads["ring_flux"], ring.at[pl.ds(0, NPOLE)])
        fetch("t_high", loads["t_high"], t_high)
        fetch("t_low", loads["t_low"], t_low)
        fetch("rotate", loads["rotate"].at[0], stencil.at[0])
        fetch("rotate", loads["rotate"].at[1], stencil.at[2])
        if steps[0] > 1:
            @pl.loop(0, CAP)
            def _(q):
                spec_row(q).start()

        part = NK // blocks
        some = part // 2
        rows_15 = [step for step in steps if step < STEPS]
        for i in range(blocks):
            owner = (i % 2) * (blocks // 2) + i // 2
            for n in range(2):
                at = pl.ds(KMAX * n + n + some * owner, some)
                take = pl.ds(some * n, some)
                fetch("free", loads["free"].at[i, take], free_top.at[at])
                for slot, step in enumerate(rows_15):
                    take = pl.ds(part * step + some * n, some)
                    fetch("free", loads["free"].at[i, take], free_row.at[slot, at])
        if last:
            side_y, place_z = lax.rem(block, 2), block // 2
            for z in range(blocks // 2):
                for y in range(2):
                    owner = (blocks // 2) * jnp.bitwise_xor(side_y, y) + jnp.bitwise_xor(place_z, z)
                    for n in range(2):
                        at = pl.multiple_of((KMAX + 1) * n + some * owner, some)
                        fetch(
                            "late",
                            loads[z].at[y, :, pl.ds(some * n, some)],
                            free_late.at[:, pl.ds(at, some)],
                        )
        if steps[0] == 1:
            fetch("sea_ring", loads["sea_ring"], sea_ring)
            for i in range(blocks):
                for o in range(width // 128):
                    fetch(
                        "gathered",
                        loads["free"].at[i, pl.ds(STEPS * part + 8 * o, 8)],
                        gathered.at[i, pl.ds(8, 8), pl.ds(128 * o, 128)],
                    )
        fetch("coef_ring", loads["coef_ring"], coef_ring)
        fetch("coef", loads["coef"], coef)
        fetch("sea", loads["sea"], sea)
        fetch("flux", loads["flux"] if steps[0] > 1 else hist(3, 1), flux)
        for n, step in enumerate(steps):
            fetch("hist", hist(2, step), sea_hist.at[n])
        for n, step in enumerate(wedge_steps):
            fetch("hist", hist(3, step), flux_hist.at[n])
            fetch("hist", hist(1, step - 1), side.at[n])
            row = pl.ds(8 + (step - 2) * width, width)
            fetch("hist", hist(0, step - 1), cur.at[row])
        kept = steps[0] - 1
        for j in range(kept):
            fetch("hist", loads["wedge"].at[j], cur.at[pl.ds(8 + j * width, width)])
        ready("mix", "courant")
        mixing(mix, vcat)
        for ref in (spec_a, spec_b):
            ref[0] = jnp.zeros((NK, 128), F32)
            for beyond in range(CAP + 1, CAP + 4):
                ref[beyond] = jnp.zeros((NK, 128), F32)
        cur[0:8, :] = jnp.zeros((8, 128), F32)
        pad[...] = jnp.zeros_like(pad)

        src, dst = spec_a, spec_b
        for n, step in enumerate(steps):
            cap_step(step, src, dst, n)
            src, dst = dst, src
            if step < STEPS:
                pending = wedge_step(step + 1)
                flux[...] = pending
                if not last:
                    turned = jnp.transpose(pending)[NPOLE + ROW0 : NPOLE + ROW0 + 8]
                    for to in range(blocks):
                        gather_out[to, pl.ds(8 * n, 8), :] = turned
        ready(*list(copies))
        if last:
            start, extent = (HALO, count) if fast else (0, width)

            def send(ref, offset, q):
                r = jnp.where(flip == 1, rows - 1 - q, q)
                return pltpu.make_async_copy(
                    ref.at[pl.ds(offset + start, extent)], air_out.at[r], sems.at[q]
                )

            for j in range(WEDGE):
                send(cur, 8 + j * width, NPOLE + j).start()

            @pl.loop(0, NPOLE // 2)
            def _(pair):
                parts_of = [two_parts(src[2 * pair + n + 1] + free_late[2 * pair + n])
                            for n in range(2)]
                highs = jnp.concatenate([high for high, _ in parts_of], axis=1)
                crossed = dot(t_low[own, :], highs)
                for n, (high, low) in enumerate(parts_of):
                    q = 2 * pair + n
                    both = dot(t_high[own, :], jnp.concatenate([high, low], axis=1))
                    y = both[:, :128] + both[:, 128:] + crossed[:, 128 * n : 128 * n + 128]
                    edge = pltpu.roll(flux[...], lax.rem(128 - ROW0 - q, 128), 1)
                    back[q] = y + air_gain * jnp.where(lanes == 0, edge, 0.0)
                    send(back.at[q], 0, q).start()

            @pl.loop(0, NPOLE)
            def _(q):
                send(back.at[q], 0, q).wait()

            for j in range(WEDGE):
                send(cur, 8 + j * width, NPOLE + j).wait()
        else:
            for j in range(len(wedge_steps) + kept):
                store(cur.at[pl.ds(8 + j * width, width)], wedge_out.at[j])
            for source, target in (
                (sea, sea_out), (flux, flux_out), (sea_ring, sea_ring_out),
                (ring.at[pl.ds(0, NPOLE)], ring_out), (gather_out, gather_to),
            ):
                store(source, target)
            for copy in stores:
                copy.wait()

    if last:
        @pl.when(polar == 0)
        def _():
            copy = pltpu.make_async_copy(hist(2, STEPS), sea, load_sems.at[0])
            copy.start()
            copy.wait()

        turn[...] = jnp.transpose(pltpu.roll(sea[...], width - HALO, 0))

        @pl.loop(0, rows)
        def _(q):
            r = jnp.where(flip == 1, rows - 1 - q, q)
            sea_out[pl.ds(r, 1), :] = turn[pl.ds(q + ROW0, 1), pl.ds(0, count)]


def cap_hists(steps):
    return ([0] if steps[0] <= SPLIT + 1 else []) + ([1] if steps[-1] + 1 > SPLIT else [])


def cap_steps(rows, count, width, blocks, fast, steps, scal, spec, big, small, air):
    levels = 128
    ring_width = blocks * width
    last = steps[-1] == STEPS
    any_spec = pl.BlockSpec(memory_space=pl.ANY)
    vmem = pl.BlockSpec(memory_space=pltpu.VMEM)
    shape = jax.ShapeDtypeStruct
    square = pltpu.VMEM((width, 128), F32)
    aliases = {}
    extra = []
    if last:
        out_shape = [
            shape((rows, count if fast else width, levels), F32),
            shape((rows, count), F32),
        ]
        out_specs = [any_spec, vmem]
        extra = [
            pltpu.VMEM((NPOLE, width, levels), F32),
            pltpu.VMEM((NPOLE, NK, levels), F32),
            pltpu.SemaphoreType.DMA((NPOLE + WEDGE,)),
        ]
        aliases = {1 + len(spec) + len(big) + len(small): 0}
    else:
        out_shape = [
            shape((CAP, NK, levels), F32),
            shape((steps[-1], width, levels), F32),
            shape((width, 128), F32),
            shape((width, 128), F32),
            shape((24, ring_width), F32),
            shape((NPOLE, ring_width), F32),
            shape((blocks, 16, width), F32),
        ]
        out_specs = [any_spec] * 7
        extra = [pltpu.VMEM((blocks, 16, width), F32), pltpu.SemaphoreType.DMA((16,))]
    return pl.pallas_call(
        functools.partial(cap_kernel, rows, count, width, blocks, fast, steps, len(spec)),
        out_shape=out_shape,
        in_specs=[pl.BlockSpec(memory_space=pltpu.SMEM)]
        + [any_spec] * (len(spec) + len(big))
        + [any_spec] * (len(small) + len(air)),
        out_specs=out_specs,
        scratch_shapes=[
            pltpu.VMEM((CAP + 4, NK, levels), F32),
            pltpu.VMEM((CAP + 4, NK, levels), F32),
            pltpu.VMEM((WEDGE * width + 16, levels), F32),
            square,
            pltpu.VMEM((width, 2 * levels), BF16),
            pltpu.VMEM((NK, 2 * levels), BF16),
            pltpu.VMEM((NK, 2 * levels), BF16),
            pltpu.VMEM((NK, 128), F32),
            square,
            square,
            pltpu.VMEM((width + 16, 128), F32),
            pltpu.VMEM((24, ring_width), F32),
            pltpu.VMEM((24, ring_width), F32),
            pltpu.VMEM((NK, 128), F32),
            pltpu.VMEM((ring_width, NK), BF16),
            pltpu.VMEM((ring_width, NK), BF16),
            pltpu.VMEM((3, NK, levels), F32),
            square,
            pltpu.VMEM((NPOLE, ring_width), F32),
            pltpu.VMEM((blocks, 16, width), F32),
            pltpu.VMEM((2, width, 128), F32),
            pltpu.VMEM((2, width, 128), F32),
            pltpu.VMEM((2, width, 128), F32),
            pltpu.VMEM((128, width), F32),
            pltpu.VMEM((NK, 128), F32),
            pltpu.VMEM((2, NK, 128), F32),
            pltpu.VMEM((256, 256), BF16),
            pltpu.VMEM((8, NK), F32),
            pltpu.VMEM((1, 128), F32),
            pltpu.VMEM((128, 128), F32),
            pltpu.SemaphoreType.DMA((9 * blocks + 32,)),
            pltpu.SemaphoreType.DMA((CAP,)),
        ]
        + extra,
        input_output_aliases=aliases,
        compiler_params=pltpu.CompilerParams(vmem_limit_bytes=VMEM_LIMIT),
        cost_estimate=pl.CostEstimate(
            flops=len(steps) * CAP * NK * levels * levels * 4,
            bytes_accessed=20_000_000,
            transcendentals=0,
        ),
        name="cap_steps",
    )(scal, *spec, *big, *small, *air)


def shift(x, axis, by, wrap):
    size = lax.axis_size(axis)
    pairs = [(i, (i + by) % size) for i in range(size) if wrap or 0 <= i + by < size]
    return lax.ppermute(x, axis, pairs)


def between_caps(x, by):
    size, bands = lax.axis_size("lon"), lax.axis_size("lat")
    pairs = [(b * size + i, b * size + (i ^ by)) for b in (0, bands - 1) for i in range(size)]
    return lax.ppermute(x, ("lat", "lon"), pairs)


def spread(copies):
    return lax.all_to_all(copies, "lon", split_axis=0, concat_axis=0, tiled=True)


def local(air_temp, sea_temp, land_sea, courant, vertical_mix, cutoffs):
    rows, count, levels = air_temp.shape
    blocks, bands = lax.axis_size("lon"), lax.axis_size("lat")
    nlon = blocks * count
    width = round_up(count + 2 * HALO, 128)
    depth = round_up(count, 128)
    fast = count % 8 == 0
    band, block = lax.axis_index("lat"), lax.axis_index("lon")
    flip = band == bands - 1
    polar = (band == 0) | flip

    cut = jnp.where(flip, cutoffs[::-1][:NPOLE], cutoffs[:NPOLE])
    head = jnp.stack([flip, polar, block]).astype(jnp.int32)
    scal = jnp.concatenate([head, cut, jnp.full((STEPS + 4,), KMAX, jnp.int32)])
    window, forward, weight = tables(blocks, count, width, depth)
    t_high, t_low = (jnp.asarray(part) for part in window)
    rotate = rotations(nlon)
    rotate_owned = jnp.asarray(rotate[:, owner_order(blocks)])
    rotate = jnp.asarray(rotate)
    weights = jnp.asarray(np.tile(weight.astype(np.float32), (8, 1)))
    courant = courant.reshape(1, levels)

    west = shift(air_temp[:, count - HALO :], "lon", 1, True)
    east = shift(air_temp[:, :HALO], "lon", -1, True)
    exchange_coef = jnp.where(land_sea == 1, sea_coef, land_coef).astype(F32)
    sea_blocks = sea_temp.reshape(-1, blocks, count).transpose(1, 0, 2).reshape(rows, count)
    mine = jnp.concatenate([sea_blocks, exchange_coef], 0)
    half = blocks // 2
    keep, send = start_spectra(blocks, scal, air_temp, jnp.asarray(forward))
    mine, west, east, send = lax.optimization_barrier((mine, west, east, send))
    got = spread(jnp.broadcast_to(mine[None], (blocks,) + mine.shape))

    half_sum = keep + between_caps(send, 1)

    outs = windows(rows, count, width, blocks, fast, scal, got, air_temp, west, east)
    own_window, sea_ring, coef_ring = outs[:3]
    if fast:
        last_rows, first_rows = outs[3:]
    else:
        def edge(part):
            extra = own_window[:, part].transpose(1, 0, 2).reshape(ROW0, -1, levels)
            at, after = edge_extent(count, width)
            row = jnp.concatenate([west[part], air_temp[part], east[part]], 1)
            row = jnp.pad(row, ((0, 0), (0, at - row.shape[1]), (0, 0)))
            extra = jnp.pad(extra, ((0, 0), (0, after - at - extra.shape[1]), (0, 0)))
            return jnp.concatenate([row, extra], 1)

        last_rows, first_rows = edge(slice(rows - ROW0, rows)), edge(slice(0, ROW0))
    north = shift(last_rows, "lat", 1, False)
    south = shift(first_rows, "lat", -1, False)

    if fast:
        air = air_temp
    else:
        middle = jnp.concatenate([west, air_temp, east], 1)
        inner = count + 2 * HALO
        air = jnp.concatenate([north[:, :inner], middle, south[:, :inner]], 0)
        air = jnp.pad(air, ((0, 0), (0, width - count - 2 * HALO), (0, 0)))
    half_sum, own_window = lax.optimization_barrier((half_sum, own_window))
    parts = [between_caps(half_sum[j], 2 * j) for j in range(1, half)]
    outs = outside_steps(
        rows, count, width, fast, tuple(range(1, SPLIT + 1)), scal, (air, west, east, north, south),
        (own_window, courant, vertical_mix),
    )
    state, early, sea, coef, gathered = outs[0], tuple(outs[1:5]), outs[5], outs[6], outs[7]
    parts, state = lax.optimization_barrier((parts, state))
    gathered, late_free = free_steps(
        blocks, scal, (half_sum[0], *parts), rotate_owned, courant, vertical_mix, gathered
    )
    gathered, state = lax.optimization_barrier((gathered, state))
    late_pair = jnp.stack([late_free, between_caps(late_free, 1)])
    free = spread(gathered)
    outs = outside_steps(
        rows, count, width, fast, tuple(range(SPLIT + 1, STEPS + 1)), scal,
        (state, early[2], early[3], coef), (courant, vertical_mix),
    )
    air, late = outs[0], tuple(outs[1:5])
    free, air, late = lax.optimization_barrier((free, air, late))

    more, spec = (), ()
    for steps in ((1, 2), (3, 4), (5, 6)):
        hists = sum(((early, late)[h] for h in cap_hists(steps)), ())
        big = hists + (free, t_high, t_low, rotate, coef, sea, sea_ring, coef_ring) + more
        if steps[-1] == STEPS:
            big += tuple(late_free)
        outs = cap_steps(
            rows, count, width, blocks, fast, steps, scal, spec, big,
            (weights, courant, vertical_mix), (air,) if steps[-1] == STEPS else (),
        )
        if steps[-1] < STEPS:
            spec, wedge, sea, flux, sea_ring, ring_flux, mine = outs
            if steps[0] == 1:
                late_pair, mine = lax.optimization_barrier((late_pair, mine))
                late_free = [late_pair] + [
                    between_caps(late_pair, 2 * j) for j in range(1, half)
                ]
            gathered = spread(mine)
            spec, more = (spec,), (gathered, flux, ring_flux, wedge)
    air, sea = outs
    if not fast:
        air = air[:, HALO : HALO + count]
    sea = lax.all_to_all(sea, "lon", split_axis=0, concat_axis=1, tiled=True)
    return air, sea


def solution(mesh):
    placed = (P("lat", "lon", None), P(("lat", "lon"), None), P("lat", "lon"), P(), P(), P())
    return jax.shard_map(
        local,
        mesh=mesh,
        in_specs=placed,
        out_specs=(P("lat", "lon", None), P(("lat", "lon"), None)),
        check_vma=False,
    )
```

```python
import functools
import math

import jax
import jax.numpy as jnp
import ml_dtypes
import numpy as np
from jax import lax
from jax.experimental import pallas as pl
from jax.experimental.pallas import tpu as pltpu
from jax.sharding import PartitionSpec as P

NPOLE = 16
KMAX = 127
STEPS = 6
NK = 2 * (KMAX + 1)
CAP = NPOLE + STEPS
HALO = 8
ROW0 = STEPS
WEDGE = STEPS - 1
BEYOND = 5
SPLIT = 2

diffusion_rate = 0.1
air_gain = 0.5
ocean_gain = 0.3
ocean_diffusion = 0.2
sea_coef = 0.5
land_coef = 0.15

F32 = jnp.float32
BF16 = jnp.bfloat16
VMEM_LIMIT = 56 * 1024 * 1024


def round_up(value, unit):
    return -(-value // unit) * unit


def two_parts(x):
    high = x.astype(BF16)
    return high, (x - high.astype(F32)).astype(BF16)


def dot(a, b):
    return jnp.dot(a, b, preferred_element_type=F32)


def dot_nt(a, b):
    return lax.dot_general(a, b, (((1,), (1,)), ((), ())), preferred_element_type=F32)


def table_dot(high, low, x):
    x_high, x_low = two_parts(x)
    both = dot(high, jnp.concatenate([x_high, x_low], axis=1))
    return both[:, :128] + both[:, 128:] + dot(low, x_high)


def numpy_parts(table):
    high = table.astype(ml_dtypes.bfloat16)
    low = (table - high.astype(np.float64)).astype(ml_dtypes.bfloat16)
    return high, low


def owner_order(blocks):
    k = np.arange(KMAX + 1).reshape(blocks, -1)
    return np.concatenate([k, k + KMAX + 1], 1).reshape(-1)


@functools.lru_cache(maxsize=None)
def tables(blocks, count, width, depth):
    nlon = blocks * count
    wavenum = np.arange(KMAX + 1)
    weight = np.where(wavenum == 0, 1.0, 2.0) / nlon

    def table(columns):
        phase = (columns[:, None] * wavenum[None, :]) % nlon * (2.0 * math.pi / nlon)
        return np.concatenate([np.cos(phase), np.sin(phase)], 1)

    window = np.concatenate(
        [table((j * count - HALO + np.arange(width)) % nlon) for j in range(blocks)], 0
    )
    forward = np.zeros((blocks, NK, depth))
    for j in range(blocks):
        own = table(j * count + np.arange(count)) * np.tile(weight, 2)
        forward[j, :, :count] = own.T[owner_order(blocks)]
    high, low = numpy_parts(forward)
    return numpy_parts(window), np.concatenate([high, high, low], 2), np.tile(weight, 2)


@functools.lru_cache(maxsize=None)
def rotations(nlon):
    theta = np.arange(KMAX + 1) * (2.0 * math.pi / nlon)
    stay = 1.0 - 4.0 * diffusion_rate + 2.0 * diffusion_rate * np.tile(np.cos(theta), 2)
    turn = np.concatenate([-np.sin(theta), np.sin(theta)])
    both = np.stack([stay, turn]).astype(np.float32)
    return np.ascontiguousarray(np.broadcast_to(both[:, :, None], (2, NK, 128)))


def mixing(mix, vcat):
    row = lax.broadcasted_iota(jnp.int32, (128, 128), 0)
    high, low = two_parts(jnp.where(row == lane_iota((128, 128)), mix[...] + 1.0, mix[...]))
    vcat[0:128, 0:128] = high
    vcat[128:256, 0:128] = high
    vcat[0:128, 128:256] = low
    vcat[128:256, 128:256] = jnp.zeros_like(low)


def winds(courant):
    c = courant[0:1, :]
    top = jnp.broadcast_to(c[:, 0:1], c.shape)
    return [diffusion_rate + sign * 0.5 * x for x in (c, top) for sign in (-1.0, 1.0)]


class Place:
    def __init__(self, cutoffs):
        band, bands = lax.axis_index("lat"), lax.axis_size("lat")
        flip = (band == bands - 1).astype(jnp.int32)
        polar = jnp.maximum(flip, (band == 0).astype(jnp.int32))
        self.cutoffs = cutoffs
        self.head = (flip, polar, lax.axis_index("lon"))

    def __getitem__(self, at):
        if isinstance(at, int) and at < 3:
            return self.head[at]
        q = at - 3
        inside = jnp.minimum(q, NPOLE - 1)
        r = jnp.where(self.head[0] == 1, 2 * NPOLE - 1 - inside, inside)
        return jnp.where(q < NPOLE, self.cutoffs[r], KMAX)


def lane_iota(shape):
    return lax.broadcasted_iota(jnp.int32, shape, len(shape) - 1)


def spectra_kernel(
    rows, count, blocks,
    scal, air, table, keep_out, send_out,
    held, own_table, stacked_a, stacked_b, sums, keep, send, sems,
):
    scal = Place(scal)
    depth = stacked_a.shape[0] // 3
    half, part = blocks // 2, NK // blocks
    flip, block = scal[0], scal[2]
    side, place = lax.rem(block, 2), block // 2
    pairs = CAP // 2

    def row(q):
        r = jnp.where(flip == 1, rows - 1 - q, q)
        return pltpu.make_async_copy(air.at[r], held.at[q], sems.at[q])

    @pl.when(scal[1] == 1)
    def _():
        fetch = pltpu.make_async_copy(table.at[block], own_table, sems.at[CAP])
        row(0).start()
        row(1).start()
        fetch.start()

        @pl.loop(2, CAP)
        def _(q):
            row(q).start()

        for ref in (stacked_a, stacked_b):
            ref[...] = jnp.zeros_like(ref)

        def load(p, slot):
            ref = (stacked_a, stacked_b)[slot]
            for n in range(2):
                high, low = two_parts(held[2 * p + n])
                lanes = slice(128 * n, 128 * n + 128)
                ref[0:count, lanes] = high
                ref[depth : depth + count, lanes] = low
                ref[2 * depth : 2 * depth + count, lanes] = high

        def finish(p, slot, between):
            sums[slot] = dot(own_table[...], (stacked_a, stacked_b)[slot][...])
            between()
            for n in range(2):
                lanes = slice(128 * n, 128 * n + 128)
                for z in range(half):
                    at = jnp.bitwise_xor(place, z)
                    mine = pl.multiple_of((side * half + z) * part, part)
                    other = pl.multiple_of(((1 - side) * half + z) * part, part)
                    keep[at, 2 * p + n] = sums[slot, pl.ds(mine, part), lanes]
                    send[at, 2 * p + n] = sums[slot, pl.ds(other, part), lanes]

        def arrive(n):
            for q in range(2, 6):
                row(4 * n + q).wait()

        row(0).wait()
        row(1).wait()
        fetch.wait()
        two_at_a_time(0, pairs // 2, load, finish, arrive)
        finish(pairs - 1, 0, lambda: None)
        out = [
            pltpu.make_async_copy(send.at[:, pl.ds(0, CAP)], send_out, sems.at[0]),
            pltpu.make_async_copy(keep.at[:, pl.ds(0, CAP)], keep_out, sems.at[1]),
        ]
        for copy in out:
            copy.start()
        for copy in out:
            copy.wait()


def start_spectra(blocks, scal, air_temp, table):
    rows, count, levels = air_temp.shape
    half, part = blocks // 2, NK // blocks
    depth = table.shape[2] // 3
    any_spec = pl.BlockSpec(memory_space=pl.ANY)
    out = jax.ShapeDtypeStruct((half, CAP, part, levels), F32)
    return pl.pallas_call(
        functools.partial(spectra_kernel, rows, count, blocks),
        out_shape=[out, out],
        in_specs=[pl.BlockSpec(memory_space=pltpu.SMEM), any_spec, any_spec],
        out_specs=[any_spec, any_spec],
        scratch_shapes=[
            pltpu.VMEM((CAP, count, levels), F32),
            pltpu.VMEM((NK, 3 * depth), BF16),
            pltpu.VMEM((3 * depth, 2 * levels), BF16),
            pltpu.VMEM((3 * depth, 2 * levels), BF16),
            pltpu.VMEM((2, NK, 2 * levels), F32),
            pltpu.VMEM((half, CAP, part, levels), F32),
            pltpu.VMEM((half, CAP, part, levels), F32),
            pltpu.SemaphoreType.DMA((CAP + 2,)),
        ],
        compiler_params=pltpu.CompilerParams(vmem_limit_bytes=VMEM_LIMIT),
        name="start_spectra",
    )(scal, air_temp, table)


def free_kernel(blocks, parts, scal, *refs):
    scal = Place(scal)
    sums, refs = refs[:parts], refs[parts:]
    rotate, courant, mix, edge, early, late, state, mask, xcat, vcat = refs
    part = NK // blocks
    some = part // 2
    owner = lax.rem(scal[2], 2) * (blocks // 2) + scal[2] // 2

    @pl.when(scal[1] == 1)
    def _():
        mixing(mix, vcat)
        state[0] = jnp.zeros((part, 128), F32)
        state[1 : CAP + 1] = functools.reduce(jnp.add, [ref[...] for ref in sums])
        at = pl.ds(pl.multiple_of(owner * part, part), part)
        stay, turn = rotate[0, at, :], rotate[1, at, :] * courant[0:1, :]
        wavenum = lax.broadcasted_iota(jnp.int32, (part, 128), 0) % some + owner * some
        for q in range(CAP):
            mask[q] = jnp.where(wavenum <= scal[3 + q], 1.0, 0.0)
        first = lane_iota((part, 128)) == 0
        top = jnp.zeros((part, 128), F32)
        for step in range(1, STEPS + 1):
            size = CAP - step
            here = state[1 : size + 1]
            swapped = jnp.concatenate([here[:, some:], here[:, :some]], axis=1)
            x = stay * here + diffusion_rate * (state[0:size] + state[2 : size + 2])
            x = (x + turn * swapped) * mask[0:size]
            x = x.reshape(size * part, 128)
            high, low = two_parts(x)
            xcat[0 : size * part, 0:128] = high
            xcat[0 : size * part, 128:256] = low
            mixed = dot(xcat[0 : size * part, :], vcat[...])
            y = mixed[:, :128] + mixed[:, 128:]
            state[1 : size + 1] = y.reshape(size, part, 128)
            for q in range(NPOLE):
                lane = NPOLE * (step - 1) + q
                top += pltpu.roll(jnp.where(first, state[q + 1], 0.0), lane, 1)
            if step < STEPS:
                for to in range(blocks):
                    early[to, part * step : part * (step + 1), :] = state[NPOLE]
            else:
                late[...] = state[1 : NPOLE + 1]
        for to in range(blocks):
            early[to, 0:part, :] = top
            early[to, STEPS * part :, :] = edge[...]


def free_steps(blocks, scal, sums, rotate, courant, mix, edge):
    part = NK // blocks
    vmem = pl.BlockSpec(memory_space=pltpu.VMEM)
    shape = jax.ShapeDtypeStruct
    return pl.pallas_call(
        functools.partial(free_kernel, blocks, len(sums)),
        out_shape=[
            shape((blocks, STEPS * part + edge.shape[0], 128), F32),
            shape((NPOLE, part, 128), F32),
        ],
        in_specs=[pl.BlockSpec(memory_space=pltpu.SMEM)] + [vmem] * (len(sums) + 4),
        out_specs=[vmem] * 2,
        scratch_shapes=[
            pltpu.VMEM((CAP + 2, part, 128), F32),
            pltpu.VMEM((CAP, part, 128), F32),
            pltpu.VMEM((CAP * part, 256), BF16),
            pltpu.VMEM((256, 256), BF16),
        ],
        compiler_params=pltpu.CompilerParams(vmem_limit_bytes=VMEM_LIMIT // 4),
        name="free_steps",
    )(scal, *sums, rotate, courant, mix, edge)


def advance(
    width, here_ref, base, north_ref, north, south_ref, south, cour, xcat, more=None, to=0
):
    c_east, c_west = cour
    for o in range(0, width, 128):
        around = north_ref[pl.ds(north + o, 128), :] + south_ref[pl.ds(south + o, 128), :]
        x = (
            (1.0 - 4.0 * diffusion_rate) * here_ref[pl.ds(base + o, 128), :]
            + diffusion_rate * around
            + c_east * here_ref[pl.ds(base + o + 1, 128), :]
            + c_west * here_ref[pl.ds(base + o - 1, 128), :]
        )
        if more is not None:
            moved = pltpu.roll(more[0][pl.ds(o, 128), :], more[1], 1)
            x += jnp.where(lane_iota(x.shape) == 0, moved, 0.0)
        high, low = two_parts(x)
        xcat[pl.ds(to + o, 128), 0:128] = high
        xcat[pl.ds(to + o, 128), 128:256] = low


def two_at_a_time(first, pairs, load, finish, arrive=None, size=1):
    load(first, 0)

    @pl.loop(0, pairs)
    def _(n):
        if arrive is not None:
            arrive(n)
        q = first + 2 * size * n
        finish(q, 0, lambda: load(q + size, 1))
        finish(q + size, 1, lambda: load(q + 2 * size, 0))


def exchange(y, lane, sea, coef):
    back = (128 - lane) % 128
    flux = pltpu.roll(coef, back, 1) * (pltpu.roll(sea, back, 1) - y)
    return jnp.where(lane_iota(y.shape) == 0, flux, 0.0)


def sea_next(width, polar, rows, sea, flux, pad):
    pad[pl.ds(8, width), :] = sea
    east = pad[pl.ds(9, width), :]
    west = pad[pl.ds(7, width), :]
    around = east + west + pltpu.roll(sea, 1, 1) + pltpu.roll(sea, 127, 1)
    new = sea - ocean_gain * flux + ocean_diffusion * (around - 4.0 * sea)
    lane = lane_iota(sea.shape)
    first = jnp.where(polar == 1, ROW0, 0)
    return jnp.where((lane >= first) & (lane < rows + 2 * ROW0), new, 0.0)


def share_kernel(rows, count, blocks, sea, land, out):
    per = rows // blocks
    for i in range(blocks):
        piece = sea[:, i * count : (i + 1) * count]
        for to in range(blocks):
            out[to, i * per : (i + 1) * per, :] = piece
    coef = jnp.where(land[...] == 1, sea_coef, land_coef).astype(F32)
    for to in range(blocks):
        out[to, rows:, :] = coef


def shares_of_sea(rows, count, blocks, sea, land):
    vmem = pl.BlockSpec(memory_space=pltpu.VMEM)
    return pl.pallas_call(
        functools.partial(share_kernel, rows, count, blocks),
        out_shape=jax.ShapeDtypeStruct((blocks, 2 * rows, count), F32),
        in_specs=[vmem, vmem],
        out_specs=vmem,
        compiler_params=pltpu.CompilerParams(vmem_limit_bytes=VMEM_LIMIT // 4),
        name="shares_of_sea",
    )(sea, land)


def windows_kernel(rows, count, width, blocks, scal, got, air, west, east, *refs):
    scal = Place(scal)
    own, ring_sea, ring_coef = refs[:3]
    wide, sems = refs[-2:]
    edges = list(zip(refs[3:-2], (rows - ROW0, 0)))
    copies = []
    for n, (ref, first) in enumerate(edges):
        some = pl.ds(first, ROW0)
        for m, (source, offset, size) in enumerate(
            ((west, 0, HALO), (air, HALO, count), (east, HALO + count, HALO))
        ):
            copies.append(
                pltpu.make_async_copy(
                    source.at[some], ref.at[:, pl.ds(offset, size)], sems.at[3 * n + m]
                )
            )
    for copy in copies:
        copy.start()
    per = rows // blocks
    for j in range(blocks):
        columns = slice(j * width + HALO, j * width + HALO + count)
        for i in range(blocks):
            wide[0, per * i : per * (i + 1), columns] = got[i, per * j : per * (j + 1), :]
        wide[1, :, columns] = got[j, rows:, :]
    rest = width - HALO - count
    for j in range(blocks):
        before = ((j - 1) % blocks) * width + count
        after = ((j + 1) % blocks) * width + HALO
        end = j * width + HALO + count
        wide[:, :, j * width : j * width + HALO] = wide[:, :, before : before + HALO]
        wide[:, :, end : end + rest] = wide[:, :, after : after + rest]
    own[...] = wide[:, :, pl.ds(pl.multiple_of(scal[2] * width, 128), width)]
    for ref, first in edges:
        base = count + 2 * HALO
        for n in range(2):
            for r in range(ROW0):
                for o in range(width // 128):
                    at = base + n * (width // 128) + o
                    ref[r, at : at + 1, :] = own[n, first + r : first + r + 1, pl.ds(128 * o, 128)]

    @pl.when(scal[1] == 1)
    def _():
        @pl.loop(0, 24)
        def _(q):
            r = jnp.where(scal[0] == 1, rows - 1 - q, q)
            ring_sea[pl.ds(q, 1), :] = wide[0, pl.ds(r, 1), :]

        @pl.loop(0, NPOLE)
        def _(q):
            r = jnp.where(scal[0] == 1, rows - 1 - q, q)
            ring_coef[pl.ds(q, 1), :] = wide[1, pl.ds(r, 1), :]

    for copy in copies:
        copy.wait()


def edge_extent(count, width):
    inner = count + 2 * HALO
    return round_up(inner, 8), round_up(inner, 8) + 8


def windows(rows, count, width, blocks, fast, scal, got, air, west, east):
    any_spec = pl.BlockSpec(memory_space=pl.ANY)
    edges = [jax.ShapeDtypeStruct((ROW0, edge_extent(count, width)[1], 128), F32)] * 2
    vmem = pl.BlockSpec(memory_space=pltpu.VMEM)
    shape = jax.ShapeDtypeStruct
    return pl.pallas_call(
        functools.partial(windows_kernel, rows, count, width, blocks),
        out_shape=[
            shape((2, rows, width), F32),
            shape((24, blocks * width), F32),
            shape((NPOLE, blocks * width), F32),
        ]
        + (edges if fast else []),
        in_specs=[pl.BlockSpec(memory_space=pltpu.SMEM), vmem] + [any_spec] * 3,
        out_specs=[vmem] * (5 if fast else 3),
        scratch_shapes=[
            pltpu.VMEM((2, rows, blocks * width), F32),
            pltpu.SemaphoreType.DMA((6,)),
        ],
        compiler_params=pltpu.CompilerParams(vmem_limit_bytes=VMEM_LIMIT),
        name="windows",
    )(scal, got, air, west, east)


def outside_kernel(rows, count, width, fast, steps, scal, *refs):
    scal = Place(scal)
    first, last = steps[0] == 1, steps[-1] == STEPS
    if first:
        (air, west, east, north, south, own, courant, mix), refs = refs[:8], refs[8:]
        (state, *hist_outs, sea_start, coef_out, gather_out), refs = refs[:8], refs[8:]
    else:
        (state, sea_hist_in, flux_hist_in, coef_in, courant, mix), refs = refs[:6], refs[6:]
        (air_out, *hist_outs), refs = refs[:5], refs[5:]
    (buf_a, buf_b, xcat_a, xcat_b, sea, flux, point, more, turn, pad, vcat, edge_seas,
     coef, wedge, side, sea_hist, flux_hist, hist_sems, sems) = refs
    flip, polar = scal[0], scal[1]
    total = rows + 2 * ROW0
    inner = count + 2 * HALO
    lanes = lane_iota((width, 128))
    hist = tuple(zip((wedge, side, sea_hist, flux_hist), hist_outs))

    def hist_copies(n, kinds):
        return [
            pltpu.make_async_copy(hist[k][0].at[n], hist[k][1].at[n], hist_sems.at[4 * n + k])
            for k in kinds
        ]

    def base_of(q):
        return pl.multiple_of(8 + (q + ROW0) * width, 8)

    def q_of(r):
        return jnp.where(flip == 1, rows - 1 - r, r)

    def low_row(step):
        return jnp.where(polar == 1, NPOLE + step - 1, step - STEPS)

    def row_range(body, step, *sizes):
        hi = rows - 1 + STEPS - step
        ref, extent, sem = sizes

        @pl.loop(low_row(step), hi + 1)
        def _(q):
            body(q).start()

        for kind, count_rows in ((1, hi + 1 - NPOLE - step + 1), (0, hi + 1 + STEPS - step)):
            @pl.when(polar == kind)
            def _(count_rows=count_rows):
                whole = ref.at[pl.ds(0, count_rows * extent)]
                pltpu.make_async_copy(whole, whole, sem).wait()

    def begin():
        mixing(mix, vcat)
        beyond = 8 + total * width
        for ref in (buf_a, buf_b):
            ref[0:8, :] = jnp.zeros((8, 128), F32)
            ref[pl.ds(beyond, BEYOND * width + 8), :] = jnp.zeros((BEYOND * width + 8, 128), F32)
        pad[...] = jnp.zeros_like(pad)

    if first:
        needed = jnp.where(polar == 1, NPOLE - 1, -ROW0)
        at, after = edge_extent(count, width)
        for n, ref in enumerate((north, south)):
            pltpu.make_async_copy(
                ref.at[:, pl.ds(at, 8)], edge_seas.at[n], sems.at[2 + n]
            ).start()
        if fast:
            @pl.loop(0, rows)
            def _(r):
                @pl.when(q_of(r) >= needed)
                def _():
                    base = base_of(q_of(r))
                    for ref, offset, size in (
                        (west, 0, HALO), (air, HALO, count), (east, HALO + count, HALO)
                    ):
                        pltpu.make_async_copy(
                            ref.at[r], buf_a.at[pl.ds(base + offset, size)], sems.at[0]
                        ).start()

            @pl.loop(0, ROW0)
            def _(r):
                for ref, place in ((north, r - ROW0), (south, r + rows)):
                    @pl.when(q_of(place) >= needed)
                    def _(ref=ref, place=place):
                        pltpu.make_async_copy(
                            ref.at[r, pl.ds(0, inner)],
                            buf_a.at[pl.ds(base_of(q_of(place)), inner)],
                            sems.at[0],
                        ).start()

            if inner < width:
                @pl.loop(0, total)
                def _(e):
                    buf_a[pl.ds(base_of(e - ROW0) + inner, width - inner), :] = jnp.zeros(
                        (width - inner, 128), F32
                    )

            extents = ((1, (rows + ROW0 - NPOLE + 1) * inner), (0, total * inner))
        else:
            @pl.loop(0, total)
            def _(e):
                pltpu.make_async_copy(
                    air.at[e], buf_a.at[pl.ds(base_of(q_of(e - ROW0)), width)], sems.at[0]
                ).start()

            extents = ((1, total * width), (0, total * width))
        begin()
        for n, ref in enumerate((north, south)):
            pltpu.make_async_copy(
                ref.at[:, pl.ds(at, 8)], edge_seas.at[n], sems.at[2 + n]
            ).wait()
        chunks = width // 128
        for n, ref in ((0, sea), (1, coef)):
            turn[...] = jnp.zeros_like(turn)

            @pl.loop(0, rows)
            def _(r):
                turn[pl.ds(q_of(r) + ROW0, 1), :] = own[n, pl.ds(r, 1), :]

            for m, place in ((0, -ROW0), (1, rows)):
                @pl.loop(0, ROW0)
                def _(r, m=m, place=place):
                    pieces = [
                        edge_seas[m, r, pl.ds(n * chunks + o, 1), :] for o in range(chunks)
                    ]
                    turn[pl.ds(q_of(r + place) + ROW0, 1), :] = jnp.concatenate(pieces, axis=1)

            ref[...] = jnp.transpose(turn[...])
        sea_start[...] = sea[...]
        coef_out[...] = coef[...]
        for kind, extent in extents:
            @pl.when(polar == kind)
            def _(extent=extent):
                whole = buf_a.at[pl.ds(0, extent)]
                pltpu.make_async_copy(whole, whole, sems.at[0]).wait()
    else:
        small = [
            pltpu.make_async_copy(source, target, sems.at[1 + n])
            for n, (source, target) in enumerate(
                ((sea_hist_in.at[SPLIT - 1], sea), (flux_hist_in.at[SPLIT - 1], flux),
                 (coef_in, coef))
            )
        ]
        for copy in small:
            copy.start()
        begin()
        for copy in small:
            copy.wait()
        row_range(
            lambda q: pltpu.make_async_copy(
                state.at[q + ROW0], buf_a.at[pl.ds(base_of(q), width)], sems.at[0]
            ),
            steps[0] - 1, buf_a, width, sems.at[0],
        )

    def with_flux(y, q):
        gain = air_gain * pltpu.roll(flux[...], 128 - (q + ROW0), 1)
        return y + jnp.where(lanes == 0, gain, 0.0)

    xcats = (xcat_a, xcat_b)
    cour = winds(courant)
    src, dst = buf_a, buf_b
    for n, step in enumerate(steps):
        lo = low_row(step)
        hi = rows - 1 + STEPS - step
        pairs = jnp.where(polar == 1, (hi - NPOLE - step + 3) // 2, (hi + 1 + STEPS - step) // 2)
        if step > 1:
            gain = air_gain * flux[...]
            pad[pl.ds(8, width), :] = gain
            more[...] = (
                (1.0 - 4.0 * diffusion_rate) * gain
                + diffusion_rate * (pltpu.roll(gain, 1, 1) + pltpu.roll(gain, 127, 1))
                + cour[2] * pad[pl.ds(9, width), :]
                + cour[3] * pad[pl.ds(7, width), :]
            )
        point[...] = jnp.zeros_like(point)

        def load(q, slot, src=src, step=step):
            for n in range(2):
                base = base_of(q + n)
                shared = (more, lax.rem(128 - (q + n + ROW0), 128)) if step > 1 else None
                advance(width, src, base, src, base - width, src, base + width, cour[:2],
                        xcats[slot], shared, n * width)

        def finish(q, slot, between, dst=dst):
            mixed = dot(xcats[slot][...], vcat[...])
            between()
            tops = []
            for n in range(2):
                row = slice(n * width, (n + 1) * width)
                y = mixed[row, :128] + mixed[row, 128:]
                dst[pl.ds(base_of(q + n), width), :] = y
                tops.append(pltpu.roll(jnp.where(lanes == 0, y, 0.0), q + n + ROW0, 1))
            point[...] += tops[0] + tops[1]

        two_at_a_time(lo, pairs // 2, load, finish, None, 2)

        @pl.when(lax.rem(pairs, 2) == 1)
        def _(finish=finish, lo=lo, pairs=pairs):
            finish(lo + 2 * (pairs - 1), 0, lambda: None)

        total_flux = jnp.where(lanes >= lo + ROW0, coef[...] * (sea[...] - point[...]), 0.0)
        flux[...] = total_flux
        new_sea = sea_next(width, polar, rows, sea[...], total_flux, pad)
        sea[...] = new_sea
        sea_hist[n] = new_sea
        flux_hist[n] = total_flux
        for copy in hist_copies(n, (2, 3)):
            copy.start()
        if step <= WEDGE:
            @pl.when(polar == 1)
            def _(dst=dst, step=step, n=n):
                for ref, q in ((wedge, NPOLE + step - 1), (side, NPOLE + step)):
                    ref[n] = with_flux(dst[pl.ds(base_of(q), width), :], q)
                for copy in hist_copies(n, (0, 1)):
                    copy.start()
        src, dst = dst, src

    if first:
        state_rows = row_range(
            lambda q: pltpu.make_async_copy(
                src.at[pl.ds(base_of(q), width)], state.at[q + ROW0], sems.at[1]
            ),
            steps[-1], src, width, sems.at[1],
        )
        for n in range(len(steps)):
            for copy in hist_copies(n, (2, 3)):
                copy.wait()
        turned = jnp.transpose(flux_hist[0])[NPOLE + ROW0 : NPOLE + ROW0 + 8]
        for o in range(width // 128):
            gather_out[8 * o : 8 * o + 8, :] = turned[:, 128 * o : 128 * o + 128]
    else:
        for n in range(len(steps)):
            for copy in hist_copies(n, (2, 3)):
                copy.wait()
        start, extent = (HALO, count) if fast else (0, width)
        first_row = jnp.where(polar == 1, NPOLE + WEDGE, 0)

        @pl.loop(first_row, rows)
        def _(q):
            row = pl.ds(base_of(q), width)
            src[row, :] = with_flux(src[row, :], q)
            pltpu.make_async_copy(
                src.at[pl.ds(base_of(q) + start, extent)], air_out.at[q_of(q)], sems.at[1]
            ).start()

        for kind, count_rows in ((1, rows - NPOLE - WEDGE), (0, rows)):
            @pl.when(polar == kind)
            def _(count_rows=count_rows):
                whole = src.at[pl.ds(0, count_rows * extent)]
                pltpu.make_async_copy(whole, whole, sems.at[1]).wait()

    @pl.when(polar == 1)
    def _():
        for n, step in enumerate(steps):
            if step <= WEDGE:
                for copy in hist_copies(n, (0, 1)):
                    copy.wait()


def outside_steps(rows, count, width, fast, steps, scal, big, small):
    levels = 128
    any_spec = pl.BlockSpec(memory_space=pl.ANY)
    vmem = pl.BlockSpec(memory_space=pltpu.VMEM)
    total = rows + 2 * ROW0
    shape = jax.ShapeDtypeStruct
    square = shape((width, 128), F32)
    hist = [shape((len(steps), width, 128), F32)] * 4
    if steps[0] == 1:
        out_shape = [shape((total, width, levels), F32)] + hist + [square, square]
        out_shape.append(shape((width // 16, 128), F32))
    else:
        out_shape = [shape((rows, count if fast else width, levels), F32)] + hist
    return pl.pallas_call(
        functools.partial(outside_kernel, rows, count, width, fast, steps),
        out_shape=out_shape,
        in_specs=[pl.BlockSpec(memory_space=pltpu.SMEM)]
        + [any_spec] * len(big)
        + [vmem] * len(small),
        out_specs=[any_spec] * 5 + [vmem] * (len(out_shape) - 5),
        scratch_shapes=[
            pltpu.VMEM(((total + BEYOND) * width + 16, levels), F32),
            pltpu.VMEM(((total + BEYOND) * width + 16, levels), F32),
            pltpu.VMEM((2 * width, 2 * levels), BF16),
            pltpu.VMEM((2 * width, 2 * levels), BF16),
            pltpu.VMEM((width, 128), F32),
            pltpu.VMEM((width, 128), F32),
            pltpu.VMEM((width, 128), F32),
            pltpu.VMEM((width, 128), F32),
            pltpu.VMEM((128, width), F32),
            pltpu.VMEM((width + 16, 128), F32),
            pltpu.VMEM((256, 256), BF16),
            pltpu.VMEM((2, ROW0, 8, 128), F32),
            pltpu.VMEM((width, 128), F32),
        ]
        + [pltpu.VMEM((len(steps), width, 128), F32)] * 4
        + [
            pltpu.SemaphoreType.DMA((4 * len(steps),)),
            pltpu.SemaphoreType.DMA((4,)),
        ],
        compiler_params=pltpu.CompilerParams(vmem_limit_bytes=VMEM_LIMIT),
        cost_estimate=pl.CostEstimate(
            flops=len(steps) * rows * width * levels * levels * 4,
            bytes_accessed=rows * width * levels * 10,
            transcendentals=0,
        ),
        name="outside_steps",
    )(scal, *big, *small)


def cap_kernel(rows, count, width, blocks, fast, steps, parts, scal, *refs):
    scal = Place(scal)
    last = steps[-1] == STEPS
    wedge_steps = [step + 1 for step in steps if step < STEPS]
    spec_in, refs = refs[:parts], refs[parts:]
    hists, refs = refs[: 4 * len(cap_hists(steps))], refs[4 * len(cap_hists(steps)) :]
    names = ["free", "t_high", "t_low", "rotate", "coef", "sea", "sea_ring", "coef_ring"]
    if steps[0] > 1:
        names += ["gathered", "flux", "ring_flux", "wedge"]
    if last:
        names += list(range(blocks // 2))
    loads = dict(zip(names, refs[: len(names)]))
    refs = refs[len(names) :]
    small_in, refs = refs[:3], refs[3:]
    if last:
        refs = refs[1:]
        (air_out, sea_out), refs = refs[:2], refs[2:]
    else:
        (spec_out, wedge_out, sea_out, flux_out, sea_ring_out, ring_out, gather_to), refs = (
            refs[:7], refs[7:])
    (spec_a, spec_b, cur, prev, xcat, kcat_a, kcat_b, point, sea, flux, pad,
     ring, sea_ring, shares, t_high, t_low, stencil, coef, coef_ring, gathered, sea_hist,
     flux_hist, side, turn, free_top, free_row, vcat, weight, courant, mix, load_sems, row_sems) = refs[:32]
    if last:
        back, free_late, sems = refs[32:]
    else:
        gather_out, store_sems = refs[32:]
    flip, polar, block = scal[0], scal[1], scal[2]
    lanes = lane_iota((width, 128))
    own = pl.ds(pl.multiple_of(block * width, 128), width)

    def hist(kind, step):
        half = 0 if step <= SPLIT else 1
        return hists[4 * cap_hists(steps).index(half) + kind].at[step - 1 - SPLIT * half]

    def own_dot(x):
        return table_dot(t_high[own, :], t_low[own, :], x)

    def wedge_step(step):
        at = wedge_steps.index(step)
        pending = flux_hist[at]
        for j in range(step - 1):
            base = 8 + j * width
            if j == step - 2:
                south_ref, south = side.at[at], 0
            else:
                south_ref, south = cur, base + width
            advance(width, cur, base, prev, 0, south_ref, south, winds(courant)[:2], xcat)
            prev[...] = cur[pl.ds(base, width), :]
            mixed = dot(xcat[...], vcat[...])
            y = mixed[:, :128] + mixed[:, 128:]
            lane = NPOLE + j + ROW0
            out = exchange(y, lane, sea[...], coef[...])
            cur[pl.ds(base, width), :] = y + air_gain * out
            pending += pltpu.roll(out, lane, 1)
        return pending

    def cap_step(step, src, dst, slot):
        count_rows = CAP - step
        if step > 1:
            ready("gathered", "sea_ring", "ring_flux")
        if step > 1:
            for j in range(blocks):
                ring[pl.ds(NPOLE, 8), pl.ds(j * width, width)] = gathered[
                    j, pl.ds(8 * slot, 8), :
                ]
            old, at = sea_ring[...], ring[...]
            place = lax.broadcasted_iota(jnp.int32, old.shape, 0)
            up = jnp.where(place == 0, 0.0, pltpu.roll(old, 1, 0))
            down = pltpu.roll(old, old.shape[0] - 1, 0)
            ring_width = blocks * width
            around = up + down + pltpu.roll(old, 1, 1) + pltpu.roll(old, ring_width - 1, 1)
            sea_ring[...] = old - ocean_gain * at + ocean_diffusion * (around - 4.0 * old)
            spot = lane_iota(at.shape) % width
            at = jnp.where((spot >= HALO) & (spot < HALO + count), at, 0.0)
            high, low = two_parts(at)
            ready("t_high", "t_low", "rotate", "weight")
            both = dot(jnp.concatenate([high, low], axis=0), t_high[...])
            sums = both[:24] + both[24:] + dot(high, t_low[...])
            sums = sums * (air_gain * weight[0:1, :])
            sums = jnp.concatenate([sums, jnp.zeros((104, NK), F32)], axis=0)
            moved = jnp.transpose(sums)
            swapped = jnp.concatenate([moved[128:], moved[:128]], axis=0)
            beside = pltpu.roll(moved, 1, 1) + pltpu.roll(moved, 127, 1)
            top = jnp.broadcast_to(courant[0:1, 0:1], (1, 128))
            shares[...] = (
                stencil[0] * moved + diffusion_rate * beside + (stencil[2] * top) * swapped
            )
            stencil[1] = stencil[2] * courant[0:1, :]

        point[...] = jnp.zeros_like(point)
        kcats = (kcat_a, kcat_b)
        first = lane_iota((128, 128)) == 0

        def load(q, slot):
            cut = scal[3 + q]
            for o, other in ((0, 128), (128, 0)):
                more = pltpu.roll(shares[pl.ds(o, 128), :], lax.rem(128 - q, 128), 1)
                x = jnp.where(first, more, 0.0)
                if step > 2:
                    here = src[q + 1, pl.ds(o, 128), :]
                    swapped = src[q + 1, pl.ds(other, 128), :]
                    around = src[q, pl.ds(o, 128), :] + src[q + 2, pl.ds(o, 128), :]
                    x += (
                        stencil[0, pl.ds(o, 128), :] * here
                        + diffusion_rate * around
                        + stencil[1, pl.ds(o, 128), :] * swapped
                    )
                x = jnp.where(lax.broadcasted_iota(jnp.int32, x.shape, 0) <= cut, x, 0.0)
                high, low = two_parts(x)
                kcats[slot][pl.ds(o, 128), 0:128] = high
                kcats[slot][pl.ds(o, 128), 128:256] = low

        streamed = step == steps[0] and step > 1

        def finish(q, slot, between):
            mixed = dot(kcats[slot][...], vcat[...])
            between()
            y = mixed[:, :128] + mixed[:, 128:]
            dst[q + 1] = y
            point[...] += pltpu.roll(jnp.where(lane_iota(y.shape) == 0, y, 0.0), q, 1)

        pairs = (count_rows + 1) // 2
        if streamed:
            spec_row(0).wait()
            spec_row(1).wait()

        def arrive(n):
            spec_row(2 * n + 2).wait()
            spec_row(2 * n + 3).wait()

        if step > 1:
            two_at_a_time(0, pairs, load, finish, arrive if streamed else None)
        if streamed:
            for q in range(2 * pairs + 2, CAP):
                spec_row(q).wait()
        if step == steps[-1] and not last:
            store(dst.at[pl.ds(1, CAP)], spec_out)
        ready("free")
        top = pltpu.roll(free_top[...], (128 - NPOLE * (step - 1)) % 128, 1)
        point[...] += jnp.where(lane_iota((NK, 128)) < NPOLE, top, 0.0)

        ready("t_high", "t_low", "sea_ring", "coef_ring", "coef", "sea", "flux", "hist")
        at_rows = jnp.transpose(point[...])[:NPOLE]
        high, low = two_parts(at_rows)
        both = dot_nt(jnp.concatenate([high, low], axis=0), t_high[...])
        surface = both[:NPOLE] + both[NPOLE:] + dot_nt(high, t_low[...])
        ring[0:NPOLE, :] = coef_ring[...] * (sea_ring[0:NPOLE, :] - surface)

        here = pltpu.roll(own_dot(point[...]), ROW0, 1)
        in_cap = (lanes >= ROW0) & (lanes < ROW0 + NPOLE)
        total = jnp.where(in_cap, coef[...] * (sea[...] - here), flux[...])
        flux[...] = total
        if step < STEPS:
            edge = pltpu.roll(total, 128 - (ROW0 + NPOLE - 1), 1)
            row = free_row[slot] if step == 1 else dst[NPOLE] + free_row[slot]
            prev[...] = own_dot(row) + air_gain * jnp.where(lanes == 0, edge, 0.0)
        new = sea_next(width, polar, rows, sea[...], total, pad)
        sea[...] = jnp.where(lanes >= ROW0 + NPOLE + step - 1, sea_hist[slot], new)

    copies = {}
    order = []
    stores = []

    def store(source, target):
        copy = pltpu.make_async_copy(source, target, store_sems.at[len(stores)])
        stores.append(copy)
        copy.start()

    def fetch(name, source, target):
        copy = pltpu.make_async_copy(source, target, load_sems.at[len(order)])
        order.append(copy)
        copies.setdefault(name, []).append(copy)
        copy.start()

    def ready(*wanted):
        for name in wanted:
            for copy in copies.pop(name, ()):
                copy.wait()

    def spec_row(q):
        return pltpu.make_async_copy(spec_in[0].at[q], spec_a.at[q + 1], row_sems.at[q])

    @pl.when(polar == 1)
    def _():
        for n, (source, target) in enumerate(zip(small_in, (weight, courant, mix))):
            fetch(("weight", "courant", "mix")[n], source, target)
        if steps[0] > 1:
            fetch("gathered", loads["gathered"], gathered)
            fetch("sea_ring", loads["sea_ring"], sea_ring)
            fetch("ring_flux", loads["ring_flux"], ring.at[pl.ds(0, NPOLE)])
        fetch("t_high", loads["t_high"], t_high)
        fetch("t_low", loads["t_low"], t_low)
        fetch("rotate", loads["rotate"].at[0], stencil.at[0])
        fetch("rotate", loads["rotate"].at[1], stencil.at[2])
        if steps[0] > 1:
            @pl.loop(0, CAP)
            def _(q):
                spec_row(q).start()

        part = NK // blocks
        some = part // 2
        rows_15 = [step for step in steps if step < STEPS]
        for i in range(blocks):
            owner = (i % 2) * (blocks // 2) + i // 2
            for n in range(2):
                at = pl.ds(KMAX * n + n + some * owner, some)
                take = pl.ds(some * n, some)
                fetch("free", loads["free"].at[i, take], free_top.at[at])
                for slot, step in enumerate(rows_15):
                    take = pl.ds(part * step + some * n, some)
                    fetch("free", loads["free"].at[i, take], free_row.at[slot, at])
        if last:
            side_y, place_z = lax.rem(block, 2), block // 2
            for z in range(blocks // 2):
                for y in range(2):
                    owner = (blocks // 2) * jnp.bitwise_xor(side_y, y) + jnp.bitwise_xor(place_z, z)
                    for n in range(2):
                        at = pl.multiple_of((KMAX + 1) * n + some * owner, some)
                        fetch(
                            "late",
                            loads[z].at[y, :, pl.ds(some * n, some)],
                            free_late.at[:, pl.ds(at, some)],
                        )
        if steps[0] == 1:
            fetch("sea_ring", loads["sea_ring"], sea_ring)
            for i in range(blocks):
                for o in range(width // 128):
                    fetch(
                        "gathered",
                        loads["free"].at[i, pl.ds(STEPS * part + 8 * o, 8)],
                        gathered.at[i, pl.ds(8, 8), pl.ds(128 * o, 128)],
                    )
        fetch("coef_ring", loads["coef_ring"], coef_ring)
        fetch("coef", loads["coef"], coef)
        fetch("sea", loads["sea"], sea)
        fetch("flux", loads["flux"] if steps[0] > 1 else hist(3, 1), flux)
        for n, step in enumerate(steps):
            fetch("hist", hist(2, step), sea_hist.at[n])
        for n, step in enumerate(wedge_steps):
            fetch("hist", hist(3, step), flux_hist.at[n])
            fetch("hist", hist(1, step - 1), side.at[n])
            row = pl.ds(8 + (step - 2) * width, width)
            fetch("hist", hist(0, step - 1), cur.at[row])
        kept = steps[0] - 1
        for j in range(kept):
            fetch("hist", loads["wedge"].at[j], cur.at[pl.ds(8 + j * width, width)])
        ready("mix", "courant")
        mixing(mix, vcat)
        for ref in (spec_a, spec_b):
            ref[0] = jnp.zeros((NK, 128), F32)
            for beyond in range(CAP + 1, CAP + 4):
                ref[beyond] = jnp.zeros((NK, 128), F32)
        cur[0:8, :] = jnp.zeros((8, 128), F32)
        pad[...] = jnp.zeros_like(pad)

        src, dst = spec_a, spec_b
        for n, step in enumerate(steps):
            cap_step(step, src, dst, n)
            src, dst = dst, src
            if step < STEPS:
                pending = wedge_step(step + 1)
                flux[...] = pending
                if not last:
                    turned = jnp.transpose(pending)[NPOLE + ROW0 : NPOLE + ROW0 + 8]
                    for to in range(blocks):
                        gather_out[to, pl.ds(8 * n, 8), :] = turned
        ready(*list(copies))
        if last:
            start, extent = (HALO, count) if fast else (0, width)

            def send(ref, offset, q):
                r = jnp.where(flip == 1, rows - 1 - q, q)
                return pltpu.make_async_copy(
                    ref.at[pl.ds(offset + start, extent)], air_out.at[r], sems.at[q]
                )

            for j in range(WEDGE):
                send(cur, 8 + j * width, NPOLE + j).start()

            @pl.loop(0, NPOLE // 2)
            def _(pair):
                parts_of = [two_parts(src[2 * pair + n + 1] + free_late[2 * pair + n])
                            for n in range(2)]
                highs = jnp.concatenate([high for high, _ in parts_of], axis=1)
                crossed = dot(t_low[own, :], highs)
                for n, (high, low) in enumerate(parts_of):
                    q = 2 * pair + n
                    both = dot(t_high[own, :], jnp.concatenate([high, low], axis=1))
                    y = both[:, :128] + both[:, 128:] + crossed[:, 128 * n : 128 * n + 128]
                    edge = pltpu.roll(flux[...], lax.rem(128 - ROW0 - q, 128), 1)
                    back[q] = y + air_gain * jnp.where(lanes == 0, edge, 0.0)
                    send(back.at[q], 0, q).start()

            @pl.loop(0, NPOLE)
            def _(q):
                send(back.at[q], 0, q).wait()

            for j in range(WEDGE):
                send(cur, 8 + j * width, NPOLE + j).wait()
        else:
            for j in range(len(wedge_steps) + kept):
                store(cur.at[pl.ds(8 + j * width, width)], wedge_out.at[j])
            for source, target in (
                (sea, sea_out), (flux, flux_out), (sea_ring, sea_ring_out),
                (ring.at[pl.ds(0, NPOLE)], ring_out), (gather_out, gather_to),
            ):
                store(source, target)
            for copy in stores:
                copy.wait()

    if last:
        @pl.when(polar == 0)
        def _():
            copy = pltpu.make_async_copy(hist(2, STEPS), sea, load_sems.at[0])
            copy.start()
            copy.wait()

        turn[...] = jnp.transpose(pltpu.roll(sea[...], width - HALO, 0))

        @pl.loop(0, rows)
        def _(q):
            r = jnp.where(flip == 1, rows - 1 - q, q)
            sea_out[pl.ds(r, 1), :] = turn[pl.ds(q + ROW0, 1), pl.ds(0, count)]


def cap_hists(steps):
    return ([0] if steps[0] <= SPLIT + 1 else []) + ([1] if steps[-1] + 1 > SPLIT else [])


def cap_steps(rows, count, width, blocks, fast, steps, scal, spec, big, small, air):
    levels = 128
    ring_width = blocks * width
    last = steps[-1] == STEPS
    any_spec = pl.BlockSpec(memory_space=pl.ANY)
    vmem = pl.BlockSpec(memory_space=pltpu.VMEM)
    shape = jax.ShapeDtypeStruct
    square = pltpu.VMEM((width, 128), F32)
    aliases = {}
    extra = []
    if last:
        out_shape = [
            shape((rows, count if fast else width, levels), F32),
            shape((rows, count), F32),
        ]
        out_specs = [any_spec, vmem]
        extra = [
            pltpu.VMEM((NPOLE, width, levels), F32),
            pltpu.VMEM((NPOLE, NK, levels), F32),
            pltpu.SemaphoreType.DMA((NPOLE + WEDGE,)),
        ]
        aliases = {1 + len(spec) + len(big) + len(small): 0}
    else:
        out_shape = [
            shape((CAP, NK, levels), F32),
            shape((steps[-1], width, levels), F32),
            shape((width, 128), F32),
            shape((width, 128), F32),
            shape((24, ring_width), F32),
            shape((NPOLE, ring_width), F32),
            shape((blocks, 16, width), F32),
        ]
        out_specs = [any_spec] * 7
        extra = [pltpu.VMEM((blocks, 16, width), F32), pltpu.SemaphoreType.DMA((16,))]
    return pl.pallas_call(
        functools.partial(cap_kernel, rows, count, width, blocks, fast, steps, len(spec)),
        out_shape=out_shape,
        in_specs=[pl.BlockSpec(memory_space=pltpu.SMEM)]
        + [any_spec] * (len(spec) + len(big))
        + [any_spec] * (len(small) + len(air)),
        out_specs=out_specs,
        scratch_shapes=[
            pltpu.VMEM((CAP + 4, NK, levels), F32),
            pltpu.VMEM((CAP + 4, NK, levels), F32),
            pltpu.VMEM((WEDGE * width + 16, levels), F32),
            square,
            pltpu.VMEM((width, 2 * levels), BF16),
            pltpu.VMEM((NK, 2 * levels), BF16),
            pltpu.VMEM((NK, 2 * levels), BF16),
            pltpu.VMEM((NK, 128), F32),
            square,
            square,
            pltpu.VMEM((width + 16, 128), F32),
            pltpu.VMEM((24, ring_width), F32),
            pltpu.VMEM((24, ring_width), F32),
            pltpu.VMEM((NK, 128), F32),
            pltpu.VMEM((ring_width, NK), BF16),
            pltpu.VMEM((ring_width, NK), BF16),
            pltpu.VMEM((3, NK, levels), F32),
            square,
            pltpu.VMEM((NPOLE, ring_width), F32),
            pltpu.VMEM((blocks, 16, width), F32),
            pltpu.VMEM((2, width, 128), F32),
            pltpu.VMEM((2, width, 128), F32),
            pltpu.VMEM((2, width, 128), F32),
            pltpu.VMEM((128, width), F32),
            pltpu.VMEM((NK, 128), F32),
            pltpu.VMEM((2, NK, 128), F32),
            pltpu.VMEM((256, 256), BF16),
            pltpu.VMEM((8, NK), F32),
            pltpu.VMEM((1, 128), F32),
            pltpu.VMEM((128, 128), F32),
            pltpu.SemaphoreType.DMA((9 * blocks + 32,)),
            pltpu.SemaphoreType.DMA((CAP,)),
        ]
        + extra,
        input_output_aliases=aliases,
        compiler_params=pltpu.CompilerParams(vmem_limit_bytes=VMEM_LIMIT),
        cost_estimate=pl.CostEstimate(
            flops=len(steps) * CAP * NK * levels * levels * 4,
            bytes_accessed=20_000_000,
            transcendentals=0,
        ),
        name="cap_steps",
    )(scal, *spec, *big, *small, *air)


def shift(x, axis, by, wrap):
    size = lax.axis_size(axis)
    pairs = [(i, (i + by) % size) for i in range(size) if wrap or 0 <= i + by < size]
    return lax.ppermute(x, axis, pairs)


def between_caps(x, by):
    size, bands = lax.axis_size("lon"), lax.axis_size("lat")
    pairs = [(b * size + i, b * size + (i ^ by)) for b in (0, bands - 1) for i in range(size)]
    return lax.ppermute(x, ("lat", "lon"), pairs)


def spread(copies):
    return lax.all_to_all(copies, "lon", split_axis=0, concat_axis=0, tiled=True)


def local(air_temp, sea_temp, land_sea, courant, vertical_mix, cutoffs):
    rows, count, levels = air_temp.shape
    blocks = lax.axis_size("lon")
    nlon = blocks * count
    width = round_up(count + 2 * HALO, 128)
    depth = round_up(count, 128)
    fast = count % 8 == 0
    scal = cutoffs

    window, forward, weight = tables(blocks, count, width, depth)
    t_high, t_low = (jnp.asarray(part) for part in window)
    rotate = rotations(nlon)
    rotate_owned = jnp.asarray(rotate[:, owner_order(blocks)])
    rotate = jnp.asarray(rotate)
    weights = jnp.asarray(np.tile(weight.astype(np.float32), (8, 1)))
    courant = courant.reshape(1, levels)

    west = shift(air_temp[:, count - HALO :], "lon", 1, True)
    east = shift(air_temp[:, :HALO], "lon", -1, True)
    mine = shares_of_sea(rows, count, blocks, sea_temp, land_sea)
    half = blocks // 2
    keep, send = start_spectra(blocks, scal, air_temp, jnp.asarray(forward))
    mine, west, east, send = lax.optimization_barrier((mine, west, east, send))
    got = spread(mine)

    taken = between_caps(send, 1)
    half_sum = [keep[j] + taken[j] for j in range(half)]

    outs = windows(rows, count, width, blocks, fast, scal, got, air_temp, west, east)
    own_window, sea_ring, coef_ring = outs[:3]
    if fast:
        last_rows, first_rows = outs[3:]
    else:
        def edge(part):
            extra = own_window[:, part].transpose(1, 0, 2).reshape(ROW0, -1, levels)
            at, after = edge_extent(count, width)
            row = jnp.concatenate([west[part], air_temp[part], east[part]], 1)
            row = jnp.pad(row, ((0, 0), (0, at - row.shape[1]), (0, 0)))
            extra = jnp.pad(extra, ((0, 0), (0, after - at - extra.shape[1]), (0, 0)))
            return jnp.concatenate([row, extra], 1)

        last_rows, first_rows = edge(slice(rows - ROW0, rows)), edge(slice(0, ROW0))
    north = shift(last_rows, "lat", 1, False)
    south = shift(first_rows, "lat", -1, False)

    if fast:
        air = air_temp
    else:
        middle = jnp.concatenate([west, air_temp, east], 1)
        inner = count + 2 * HALO
        air = jnp.concatenate([north[:, :inner], middle, south[:, :inner]], 0)
        air = jnp.pad(air, ((0, 0), (0, width - count - 2 * HALO), (0, 0)))
    half_sum, own_window = lax.optimization_barrier((half_sum, own_window))
    parts = [between_caps(half_sum[j], 2 * j) for j in range(1, half)]
    outs = outside_steps(
        rows, count, width, fast, tuple(range(1, SPLIT + 1)), scal, (air, west, east, north, south),
        (own_window, courant, vertical_mix),
    )
    state, early, sea, coef, gathered = outs[0], tuple(outs[1:5]), outs[5], outs[6], outs[7]
    parts, state = lax.optimization_barrier((parts, state))
    gathered, late_free = free_steps(
        blocks, scal, (half_sum[0], *parts), rotate_owned, courant, vertical_mix, gathered
    )
    gathered, state = lax.optimization_barrier((gathered, state))
    late_pair = jnp.stack([late_free, between_caps(late_free, 1)])
    free = spread(gathered)
    outs = outside_steps(
        rows, count, width, fast, tuple(range(SPLIT + 1, STEPS + 1)), scal,
        (state, early[2], early[3], coef), (courant, vertical_mix),
    )
    air, late = outs[0], tuple(outs[1:5])
    free, air, late = lax.optimization_barrier((free, air, late))

    more, spec = (), ()
    for steps in ((1, 2), (3, 4), (5, 6)):
        hists = sum(((early, late)[h] for h in cap_hists(steps)), ())
        big = hists + (free, t_high, t_low, rotate, coef, sea, sea_ring, coef_ring) + more
        if steps[-1] == STEPS:
            big += tuple(late_free)
        outs = cap_steps(
            rows, count, width, blocks, fast, steps, scal, spec, big,
            (weights, courant, vertical_mix), (air,) if steps[-1] == STEPS else (),
        )
        if steps[-1] < STEPS:
            spec, wedge, sea, flux, sea_ring, ring_flux, mine = outs
            if steps[0] == 1:
                late_pair, mine = lax.optimization_barrier((late_pair, mine))
                late_free = [late_pair] + [
                    between_caps(late_pair, 2 * j) for j in range(1, half)
                ]
            gathered = spread(mine)
            spec, more = (spec,), (gathered, flux, ring_flux, wedge)
    air, sea = outs
    if not fast:
        air = air[:, HALO : HALO + count]
    sea = lax.all_to_all(sea, "lon", split_axis=0, concat_axis=1, tiled=True)
    return air, sea


def solution(mesh):
    placed = (P("lat", "lon", None), P(("lat", "lon"), None), P("lat", "lon"), P(), P(), P())
    return jax.shard_map(
        local,
        mesh=mesh,
        in_specs=placed,
        out_specs=(P("lat", "lon", None), P(("lat", "lon"), None)),
        check_vma=False,
    )
```

```python
import functools
import math

import jax
import jax.numpy as jnp
import ml_dtypes
import numpy as np
from jax import lax
from jax.experimental import pallas as pl
from jax.experimental.pallas import tpu as pltpu
from jax.sharding import PartitionSpec as P

NPOLE = 16
KMAX = 127
STEPS = 6
NK = 2 * (KMAX + 1)
CAP = NPOLE + STEPS
HALO = 8
ROW0 = STEPS
WEDGE = STEPS - 1
BEYOND = 5
SPLIT = 2

diffusion_rate = 0.1
air_gain = 0.5
ocean_gain = 0.3
ocean_diffusion = 0.2
sea_coef = 0.5
land_coef = 0.15

F32 = jnp.float32
BF16 = jnp.bfloat16
VMEM_LIMIT = 56 * 1024 * 1024


def round_up(value, unit):
    return -(-value // unit) * unit


def two_parts(x):
    high = x.astype(BF16)
    return high, (x - high.astype(F32)).astype(BF16)


def dot(a, b):
    return jnp.dot(a, b, preferred_element_type=F32)


def dot_nt(a, b):
    return lax.dot_general(a, b, (((1,), (1,)), ((), ())), preferred_element_type=F32)


def table_dot(high, low, x):
    x_high, x_low = two_parts(x)
    both = dot(high, jnp.concatenate([x_high, x_low], axis=1))
    return both[:, :128] + both[:, 128:] + dot(low, x_high)


def numpy_parts(table):
    high = table.astype(ml_dtypes.bfloat16)
    low = (table - high.astype(np.float64)).astype(ml_dtypes.bfloat16)
    return high, low


def owner_order(blocks):
    k = np.arange(KMAX + 1).reshape(blocks, -1)
    return np.concatenate([k, k + KMAX + 1], 1).reshape(-1)


@functools.lru_cache(maxsize=None)
def tables(blocks, count, width, depth):
    nlon = blocks * count
    wavenum = np.arange(KMAX + 1)
    weight = np.where(wavenum == 0, 1.0, 2.0) / nlon

    def table(columns):
        phase = (columns[:, None] * wavenum[None, :]) % nlon * (2.0 * math.pi / nlon)
        return np.concatenate([np.cos(phase), np.sin(phase)], 1)

    window = np.concatenate(
        [table((j * count - HALO + np.arange(width)) % nlon) for j in range(blocks)], 0
    )
    forward = np.zeros((blocks, NK, depth))
    for j in range(blocks):
        own = table(j * count + np.arange(count)) * np.tile(weight, 2)
        forward[j, :, :count] = own.T[owner_order(blocks)]
    high, low = numpy_parts(forward)
    return numpy_parts(window), np.concatenate([high, high, low], 2), np.tile(weight, 2)


@functools.lru_cache(maxsize=None)
def rotations(nlon):
    theta = np.arange(KMAX + 1) * (2.0 * math.pi / nlon)
    stay = 1.0 - 4.0 * diffusion_rate + 2.0 * diffusion_rate * np.tile(np.cos(theta), 2)
    turn = np.concatenate([-np.sin(theta), np.sin(theta)])
    both = np.stack([stay, turn]).astype(np.float32)
    return np.ascontiguousarray(np.broadcast_to(both[:, :, None], (2, NK, 128)))


def mixing(mix, vcat):
    row = lax.broadcasted_iota(jnp.int32, (128, 128), 0)
    high, low = two_parts(jnp.where(row == lane_iota((128, 128)), mix[...] + 1.0, mix[...]))
    vcat[0:128, 0:128] = high
    vcat[128:256, 0:128] = high
    vcat[0:128, 128:256] = low
    vcat[128:256, 128:256] = jnp.zeros_like(low)


def winds(courant):
    c = courant[0:1, :]
    top = jnp.broadcast_to(c[:, 0:1], c.shape)
    return [diffusion_rate + sign * 0.5 * x for x in (c, top) for sign in (-1.0, 1.0)]


class Place:
    def __init__(self, cutoffs):
        band, bands = lax.axis_index("lat"), lax.axis_size("lat")
        flip = (band == bands - 1).astype(jnp.int32)
        polar = jnp.maximum(flip, (band == 0).astype(jnp.int32))
        self.cutoffs = cutoffs
        self.head = (flip, polar, lax.axis_index("lon"))

    def __getitem__(self, at):
        if isinstance(at, int) and at < 3:
            return self.head[at]
        q = at - 3
        inside = jnp.minimum(q, NPOLE - 1)
        r = jnp.where(self.head[0] == 1, 2 * NPOLE - 1 - inside, inside)
        return jnp.where(q < NPOLE, self.cutoffs[r], KMAX)


def lane_iota(shape):
    return lax.broadcasted_iota(jnp.int32, shape, len(shape) - 1)


def spectra_kernel(
    rows, count, blocks,
    scal, air, table, keep_out, send_out,
    held, own_table, stacked_a, stacked_b, sums, keep, send, sems,
):
    scal = Place(scal)
    depth = stacked_a.shape[0] // 3
    half, part = blocks // 2, NK // blocks
    flip, block = scal[0], scal[2]
    side, place = lax.rem(block, 2), block // 2
    pairs = CAP // 2

    def row(q):
        r = jnp.where(flip == 1, rows - 1 - q, q)
        return pltpu.make_async_copy(air.at[r], held.at[q], sems.at[q])

    @pl.when(scal[1] == 1)
    def _():
        fetch = pltpu.make_async_copy(table.at[block], own_table, sems.at[CAP])
        row(0).start()
        row(1).start()
        fetch.start()

        @pl.loop(2, CAP)
        def _(q):
            row(q).start()

        for ref in (stacked_a, stacked_b):
            ref[...] = jnp.zeros_like(ref)

        def load(p, slot):
            ref = (stacked_a, stacked_b)[slot]
            for n in range(2):
                high, low = two_parts(held[2 * p + n])
                lanes = slice(128 * n, 128 * n + 128)
                ref[0:count, lanes] = high
                ref[depth : depth + count, lanes] = low
                ref[2 * depth : 2 * depth + count, lanes] = high

        def finish(p, slot, between):
            sums[slot] = dot(own_table[...], (stacked_a, stacked_b)[slot][...])
            between()
            for n in range(2):
                lanes = slice(128 * n, 128 * n + 128)
                for z in range(half):
                    at = jnp.bitwise_xor(place, z)
                    mine = pl.multiple_of((side * half + z) * part, part)
                    other = pl.multiple_of(((1 - side) * half + z) * part, part)
                    keep[at, 2 * p + n] = sums[slot, pl.ds(mine, part), lanes]
                    send[at, 2 * p + n] = sums[slot, pl.ds(other, part), lanes]

        def arrive(n):
            for q in range(2, 6):
                row(4 * n + q).wait()

        row(0).wait()
        row(1).wait()
        fetch.wait()
        two_at_a_time(0, pairs // 2, load, finish, arrive)
        finish(pairs - 1, 0, lambda: None)
        out = [
            pltpu.make_async_copy(send.at[:, pl.ds(0, CAP)], send_out, sems.at[0]),
            pltpu.make_async_copy(keep.at[:, pl.ds(0, CAP)], keep_out, sems.at[1]),
        ]
        for copy in out:
            copy.start()
        for copy in out:
            copy.wait()


def start_spectra(blocks, scal, air_temp, table):
    rows, count, levels = air_temp.shape
    half, part = blocks // 2, NK // blocks
    depth = table.shape[2] // 3
    any_spec = pl.BlockSpec(memory_space=pl.ANY)
    out = jax.ShapeDtypeStruct((half, CAP, part, levels), F32)
    return pl.pallas_call(
        functools.partial(spectra_kernel, rows, count, blocks),
        out_shape=[out, out],
        in_specs=[pl.BlockSpec(memory_space=pltpu.SMEM), any_spec, any_spec],
        out_specs=[any_spec, any_spec],
        scratch_shapes=[
            pltpu.VMEM((CAP, count, levels), F32),
            pltpu.VMEM((NK, 3 * depth), BF16),
            pltpu.VMEM((3 * depth, 2 * levels), BF16),
            pltpu.VMEM((3 * depth, 2 * levels), BF16),
            pltpu.VMEM((2, NK, 2 * levels), F32),
            pltpu.VMEM((half, CAP, part, levels), F32),
            pltpu.VMEM((half, CAP, part, levels), F32),
            pltpu.SemaphoreType.DMA((CAP + 2,)),
        ],
        compiler_params=pltpu.CompilerParams(vmem_limit_bytes=VMEM_LIMIT),
        name="start_spectra",
    )(scal, air_temp, table)


def free_kernel(blocks, parts, scal, *refs):
    scal = Place(scal)
    sums, refs = refs[:parts], refs[parts:]
    rotate, courant, mix, edge, cap_coef, early, late, state, mask, xcat, vcat = refs
    part = NK // blocks
    some = part // 2
    owner = lax.rem(scal[2], 2) * (blocks // 2) + scal[2] // 2

    @pl.when(scal[1] == 1)
    def _():
        mixing(mix, vcat)
        state[0] = jnp.zeros((part, 128), F32)
        state[1 : CAP + 1] = functools.reduce(jnp.add, [ref[...] for ref in sums])
        at = pl.ds(pl.multiple_of(owner * part, part), part)
        stay, turn = rotate[0, at, :], rotate[1, at, :] * courant[0:1, :]
        wavenum = lax.broadcasted_iota(jnp.int32, (part, 128), 0) % some + owner * some
        for q in range(CAP):
            mask[q] = jnp.where(wavenum <= scal[3 + q], 1.0, 0.0)
        first = lane_iota((part, 128)) == 0
        top = jnp.zeros((part, 128), F32)
        for step in range(1, STEPS + 1):
            size = CAP - step
            here = state[1 : size + 1]
            swapped = jnp.concatenate([here[:, some:], here[:, :some]], axis=1)
            x = stay * here + diffusion_rate * (state[0:size] + state[2 : size + 2])
            x = (x + turn * swapped) * mask[0:size]
            x = x.reshape(size * part, 128)
            high, low = two_parts(x)
            xcat[0 : size * part, 0:128] = high
            xcat[0 : size * part, 128:256] = low
            mixed = dot(xcat[0 : size * part, :], vcat[...])
            y = mixed[:, :128] + mixed[:, 128:]
            state[1 : size + 1] = y.reshape(size, part, 128)
            for q in range(NPOLE):
                lane = NPOLE * (step - 1) + q
                top += pltpu.roll(jnp.where(first, state[q + 1], 0.0), lane, 1)
            if step < STEPS:
                for to in range(blocks):
                    early[to, part * step : part * (step + 1), :] = state[NPOLE]
            else:
                late[...] = state[1 : NPOLE + 1]
        for to in range(blocks):
            early[to, 0:part, :] = top
            early[to, STEPS * part : STEPS * part + edge.shape[0], :] = edge[...]
            early[to, STEPS * part + edge.shape[0] :, :] = cap_coef[...]


def free_steps(blocks, scal, sums, rotate, courant, mix, edge, cap_coef):
    part = NK // blocks
    vmem = pl.BlockSpec(memory_space=pltpu.VMEM)
    shape = jax.ShapeDtypeStruct
    return pl.pallas_call(
        functools.partial(free_kernel, blocks, len(sums)),
        out_shape=[
            shape((blocks, STEPS * part + edge.shape[0] + cap_coef.shape[0], 128), F32),
            shape((NPOLE, part, 128), F32),
        ],
        in_specs=[pl.BlockSpec(memory_space=pltpu.SMEM)] + [vmem] * (len(sums) + 5),
        out_specs=[vmem] * 2,
        scratch_shapes=[
            pltpu.VMEM((CAP + 2, part, 128), F32),
            pltpu.VMEM((CAP, part, 128), F32),
            pltpu.VMEM((CAP * part, 256), BF16),
            pltpu.VMEM((256, 256), BF16),
        ],
        compiler_params=pltpu.CompilerParams(vmem_limit_bytes=VMEM_LIMIT // 4),
        name="free_steps",
    )(scal, *sums, rotate, courant, mix, edge, cap_coef)


def advance(
    width, here_ref, base, north_ref, north, south_ref, south, cour, xcat, more=None, to=0
):
    c_east, c_west = cour
    for o in range(0, width, 128):
        around = north_ref[pl.ds(north + o, 128), :] + south_ref[pl.ds(south + o, 128), :]
        x = (
            (1.0 - 4.0 * diffusion_rate) * here_ref[pl.ds(base + o, 128), :]
            + diffusion_rate * around
            + c_east * here_ref[pl.ds(base + o + 1, 128), :]
            + c_west * here_ref[pl.ds(base + o - 1, 128), :]
        )
        if more is not None:
            moved = pltpu.roll(more[0][pl.ds(o, 128), :], more[1], 1)
            x += jnp.where(lane_iota(x.shape) == 0, moved, 0.0)
        high, low = two_parts(x)
        xcat[pl.ds(to + o, 128), 0:128] = high
        xcat[pl.ds(to + o, 128), 128:256] = low


def two_at_a_time(first, pairs, load, finish, arrive=None, size=1):
    load(first, 0)

    @pl.loop(0, pairs)
    def _(n):
        if arrive is not None:
            arrive(n)
        q = first + 2 * size * n
        finish(q, 0, lambda: load(q + size, 1))
        finish(q + size, 1, lambda: load(q + 2 * size, 0))


def exchange(y, lane, sea, coef):
    back = (128 - lane) % 128
    flux = pltpu.roll(coef, back, 1) * (pltpu.roll(sea, back, 1) - y)
    return jnp.where(lane_iota(y.shape) == 0, flux, 0.0)


def sea_next(width, polar, rows, sea, flux, pad):
    pad[pl.ds(8, width), :] = sea
    east = pad[pl.ds(9, width), :]
    west = pad[pl.ds(7, width), :]
    around = east + west + pltpu.roll(sea, 1, 1) + pltpu.roll(sea, 127, 1)
    new = sea - ocean_gain * flux + ocean_diffusion * (around - 4.0 * sea)
    lane = lane_iota(sea.shape)
    first = jnp.where(polar == 1, ROW0, 0)
    return jnp.where((lane >= first) & (lane < rows + 2 * ROW0), new, 0.0)


def share_kernel(rows, count, blocks, sea, land, out):
    per = rows // blocks
    coef = coefficients(land)
    ends = (coef[:, 0:HALO], coef[:, count - HALO : count])
    for to in range(blocks):
        for i in range(blocks):
            out[to, i * per : (i + 1) * per, 0:count] = sea[:, i * count : (i + 1) * count]
        for n, end in enumerate(ends):
            out[to, :, count + HALO * n : count + HALO * (n + 1)] = end


def coefficients(land):
    return jnp.where(land[...] == 1, sea_coef, land_coef).astype(F32)


def shares_of_sea(rows, count, blocks, sea, land):
    vmem = pl.BlockSpec(memory_space=pltpu.VMEM)
    return pl.pallas_call(
        functools.partial(share_kernel, rows, count, blocks),
        out_shape=jax.ShapeDtypeStruct((blocks, rows, count + 2 * HALO), F32),
        in_specs=[vmem, vmem],
        out_specs=vmem,
        compiler_params=pltpu.CompilerParams(vmem_limit_bytes=VMEM_LIMIT // 4),
        name="shares_of_sea",
    )(sea, land)


def windows_kernel(rows, count, width, blocks, scal, got, land, air, west, east, *refs):
    scal = Place(scal)
    own, ring_sea, cap_coef = refs[:3]
    wide, held, sems = refs[-3:]
    edges = list(zip(refs[3:-3], (rows - ROW0, 0)))
    copies = []
    for n, (ref, first) in enumerate(edges):
        some = pl.ds(first, ROW0)
        for m, (source, offset, size) in enumerate(
            ((west, 0, HALO), (air, HALO, count), (east, HALO + count, HALO))
        ):
            copies.append(
                pltpu.make_async_copy(
                    source.at[some], ref.at[:, pl.ds(offset, size)], sems.at[3 * n + m]
                )
            )
    for copy in copies:
        copy.start()
    per = rows // blocks
    for j in range(blocks):
        columns = slice(j * width + HALO, j * width + HALO + count)
        for i in range(blocks):
            wide[per * i : per * (i + 1), columns] = got[i, per * j : per * (j + 1), 0:count]
    rest = width - HALO - count
    for j in range(blocks):
        before = ((j - 1) % blocks) * width + count
        after = ((j + 1) % blocks) * width + HALO
        end = j * width + HALO + count
        wide[:, j * width : j * width + HALO] = wide[:, before : before + HALO]
        wide[:, end : end + rest] = wide[:, after : after + rest]
    block = scal[2]
    own[0] = wide[:, pl.ds(pl.multiple_of(block * width, 128), width)]
    before, after = lax.rem(block + blocks - 1, blocks), lax.rem(block + 1, blocks)
    own[1, :, 0:HALO] = got[before, :, count + HALO : count + 2 * HALO]
    own[1, :, HALO : HALO + count] = coefficients(land)
    own[1, :, HALO + count : 2 * HALO + count] = got[after, :, count : count + HALO]
    if rest > HALO:
        own[1, :, 2 * HALO + count :] = jnp.zeros((rows, rest - HALO), F32)
    for ref, first in edges:
        base = count + 2 * HALO
        for n in range(2):
            for r in range(ROW0):
                for o in range(width // 128):
                    at = base + n * (width // 128) + o
                    ref[r, at : at + 1, :] = own[n, first + r : first + r + 1, pl.ds(128 * o, 128)]

    @pl.when(scal[1] == 1)
    def _():
        @pl.loop(0, 24)
        def _(q):
            r = jnp.where(scal[0] == 1, rows - 1 - q, q)
            ring_sea[pl.ds(q, 1), :] = wide[pl.ds(r, 1), :]

        @pl.loop(0, NPOLE)
        def _(q):
            r = jnp.where(scal[0] == 1, rows - 1 - q, q)
            held[pl.ds(q, 1), :] = own[1, pl.ds(r, 1), :]

        for o in range(width // 128):
            cap_coef[NPOLE * o : NPOLE * (o + 1), :] = held[:, 128 * o : 128 * (o + 1)]

    for copy in copies:
        copy.wait()


def edge_extent(count, width):
    inner = count + 2 * HALO
    return round_up(inner, 8), round_up(inner, 8) + 8


def windows(rows, count, width, blocks, fast, scal, got, land, air, west, east):
    any_spec = pl.BlockSpec(memory_space=pl.ANY)
    edges = [jax.ShapeDtypeStruct((ROW0, edge_extent(count, width)[1], 128), F32)] * 2
    vmem = pl.BlockSpec(memory_space=pltpu.VMEM)
    shape = jax.ShapeDtypeStruct
    return pl.pallas_call(
        functools.partial(windows_kernel, rows, count, width, blocks),
        out_shape=[
            shape((2, rows, width), F32),
            shape((24, blocks * width), F32),
            shape((NPOLE * (width // 128), 128), F32),
        ]
        + (edges if fast else []),
        in_specs=[pl.BlockSpec(memory_space=pltpu.SMEM), vmem, vmem] + [any_spec] * 3,
        out_specs=[vmem] * (5 if fast else 3),
        scratch_shapes=[
            pltpu.VMEM((rows, blocks * width), F32),
            pltpu.VMEM((NPOLE, width), F32),
            pltpu.SemaphoreType.DMA((6,)),
        ],
        compiler_params=pltpu.CompilerParams(vmem_limit_bytes=VMEM_LIMIT),
        name="windows",
    )(scal, got, land, air, west, east)


def outside_kernel(rows, count, width, fast, steps, scal, *refs):
    scal = Place(scal)
    first, last = steps[0] == 1, steps[-1] == STEPS
    if first:
        (air, west, east, north, south, own, courant, mix), refs = refs[:8], refs[8:]
        (state, *hist_outs, sea_start, coef_out, gather_out), refs = refs[:8], refs[8:]
    else:
        (state, sea_hist_in, flux_hist_in, coef_in, courant, mix), refs = refs[:6], refs[6:]
        (air_out, *hist_outs), refs = refs[:5], refs[5:]
    (buf_a, buf_b, xcat_a, xcat_b, sea, flux, point, more, turn, pad, vcat, edge_seas,
     coef, wedge, side, sea_hist, flux_hist, hist_sems, sems) = refs
    flip, polar = scal[0], scal[1]
    total = rows + 2 * ROW0
    inner = count + 2 * HALO
    lanes = lane_iota((width, 128))
    hist = tuple(zip((wedge, side, sea_hist, flux_hist), hist_outs))

    def hist_copies(n, kinds):
        return [
            pltpu.make_async_copy(hist[k][0].at[n], hist[k][1].at[n], hist_sems.at[4 * n + k])
            for k in kinds
        ]

    def base_of(q):
        return pl.multiple_of(8 + (q + ROW0) * width, 8)

    def q_of(r):
        return jnp.where(flip == 1, rows - 1 - r, r)

    def low_row(step):
        return jnp.where(polar == 1, NPOLE + step - 1, step - STEPS)

    def row_range(body, step, *sizes, meanwhile=lambda: None):
        hi = rows - 1 + STEPS - step
        ref, extent, sem = sizes

        @pl.loop(low_row(step), hi + 1)
        def _(q):
            body(q).start()

        meanwhile()
        for kind, count_rows in ((1, hi + 1 - NPOLE - step + 1), (0, hi + 1 + STEPS - step)):
            @pl.when(polar == kind)
            def _(count_rows=count_rows):
                whole = ref.at[pl.ds(0, count_rows * extent)]
                pltpu.make_async_copy(whole, whole, sem).wait()

    def begin():
        mixing(mix, vcat)
        beyond = 8 + total * width
        for ref in (buf_a, buf_b):
            ref[0:8, :] = jnp.zeros((8, 128), F32)
            ref[pl.ds(beyond, BEYOND * width + 8), :] = jnp.zeros((BEYOND * width + 8, 128), F32)
        pad[...] = jnp.zeros_like(pad)

    if first:
        needed = jnp.where(polar == 1, NPOLE - 1, -ROW0)
        at, after = edge_extent(count, width)
        for n, ref in enumerate((north, south)):
            pltpu.make_async_copy(
                ref.at[:, pl.ds(at, 8)], edge_seas.at[n], sems.at[2 + n]
            ).start()
        if fast:
            @pl.loop(0, rows)
            def _(r):
                @pl.when(q_of(r) >= needed)
                def _():
                    base = base_of(q_of(r))
                    for ref, offset, size in (
                        (west, 0, HALO), (air, HALO, count), (east, HALO + count, HALO)
                    ):
                        pltpu.make_async_copy(
                            ref.at[r], buf_a.at[pl.ds(base + offset, size)], sems.at[0]
                        ).start()

            @pl.loop(0, ROW0)
            def _(r):
                for ref, place in ((north, r - ROW0), (south, r + rows)):
                    @pl.when(q_of(place) >= needed)
                    def _(ref=ref, place=place):
                        pltpu.make_async_copy(
                            ref.at[r, pl.ds(0, inner)],
                            buf_a.at[pl.ds(base_of(q_of(place)), inner)],
                            sems.at[0],
                        ).start()

            if inner < width:
                @pl.loop(0, total)
                def _(e):
                    buf_a[pl.ds(base_of(e - ROW0) + inner, width - inner), :] = jnp.zeros(
                        (width - inner, 128), F32
                    )

            extents = ((1, (rows + ROW0 - NPOLE + 1) * inner), (0, total * inner))
        else:
            @pl.loop(0, total)
            def _(e):
                pltpu.make_async_copy(
                    air.at[e], buf_a.at[pl.ds(base_of(q_of(e - ROW0)), width)], sems.at[0]
                ).start()

            extents = ((1, total * width), (0, total * width))
        begin()
        for n, ref in enumerate((north, south)):
            pltpu.make_async_copy(
                ref.at[:, pl.ds(at, 8)], edge_seas.at[n], sems.at[2 + n]
            ).wait()
        chunks = width // 128
        for n, ref in ((0, sea), (1, coef)):
            turn[...] = jnp.zeros_like(turn)

            @pl.loop(0, rows)
            def _(r):
                turn[pl.ds(q_of(r) + ROW0, 1), :] = own[n, pl.ds(r, 1), :]

            for m, place in ((0, -ROW0), (1, rows)):
                @pl.loop(0, ROW0)
                def _(r, m=m, place=place):
                    pieces = [
                        edge_seas[m, r, pl.ds(n * chunks + o, 1), :] for o in range(chunks)
                    ]
                    turn[pl.ds(q_of(r + place) + ROW0, 1), :] = jnp.concatenate(pieces, axis=1)

            ref[...] = jnp.transpose(turn[...])
        sea_start[...] = sea[...]
        coef_out[...] = coef[...]
        for kind, extent in extents:
            @pl.when(polar == kind)
            def _(extent=extent):
                whole = buf_a.at[pl.ds(0, extent)]
                pltpu.make_async_copy(whole, whole, sems.at[0]).wait()
    else:
        small = [
            pltpu.make_async_copy(source, target, sems.at[1 + n])
            for n, (source, target) in enumerate(
                ((sea_hist_in.at[SPLIT - 1], sea), (flux_hist_in.at[SPLIT - 1], flux),
                 (coef_in, coef))
            )
        ]
        for copy in small:
            copy.start()
        row_range(
            lambda q: pltpu.make_async_copy(
                state.at[q + ROW0], buf_a.at[pl.ds(base_of(q), width)], sems.at[0]
            ),
            steps[0] - 1, buf_a, width, sems.at[0], meanwhile=begin,
        )
        for copy in small:
            copy.wait()

    def with_flux(y, q):
        gain = air_gain * pltpu.roll(flux[...], 128 - (q + ROW0), 1)
        return y + jnp.where(lanes == 0, gain, 0.0)

    xcats = (xcat_a, xcat_b)
    cour = winds(courant)
    src, dst = buf_a, buf_b
    for n, step in enumerate(steps):
        lo = low_row(step)
        hi = rows - 1 + STEPS - step
        pairs = jnp.where(polar == 1, (hi - NPOLE - step + 3) // 2, (hi + 1 + STEPS - step) // 2)
        if step > 1:
            gain = air_gain * flux[...]
            pad[pl.ds(8, width), :] = gain
            more[...] = (
                (1.0 - 4.0 * diffusion_rate) * gain
                + diffusion_rate * (pltpu.roll(gain, 1, 1) + pltpu.roll(gain, 127, 1))
                + cour[2] * pad[pl.ds(9, width), :]
                + cour[3] * pad[pl.ds(7, width), :]
            )
        point[...] = jnp.zeros_like(point)

        def load(q, slot, src=src, step=step):
            for n in range(2):
                base = base_of(q + n)
                shared = (more, lax.rem(128 - (q + n + ROW0), 128)) if step > 1 else None
                advance(width, src, base, src, base - width, src, base + width, cour[:2],
                        xcats[slot], shared, n * width)

        def finish(q, slot, between, dst=dst):
            mixed = dot(xcats[slot][...], vcat[...])
            between()
            tops = []
            for n in range(2):
                row = slice(n * width, (n + 1) * width)
                y = mixed[row, :128] + mixed[row, 128:]
                dst[pl.ds(base_of(q + n), width), :] = y
                tops.append(pltpu.roll(jnp.where(lanes == 0, y, 0.0), q + n + ROW0, 1))
            point[...] += tops[0] + tops[1]

        two_at_a_time(lo, pairs // 2, load, finish, None, 2)

        @pl.when(lax.rem(pairs, 2) == 1)
        def _(finish=finish, lo=lo, pairs=pairs):
            finish(lo + 2 * (pairs - 1), 0, lambda: None)

        total_flux = jnp.where(lanes >= lo + ROW0, coef[...] * (sea[...] - point[...]), 0.0)
        flux[...] = total_flux
        new_sea = sea_next(width, polar, rows, sea[...], total_flux, pad)
        sea[...] = new_sea
        sea_hist[n] = new_sea
        flux_hist[n] = total_flux
        for copy in hist_copies(n, (2, 3)):
            copy.start()
        if step <= WEDGE:
            @pl.when(polar == 1)
            def _(dst=dst, step=step, n=n):
                for ref, q in ((wedge, NPOLE + step - 1), (side, NPOLE + step)):
                    ref[n] = with_flux(dst[pl.ds(base_of(q), width), :], q)
                for copy in hist_copies(n, (0, 1)):
                    copy.start()
        src, dst = dst, src

    if first:
        state_rows = row_range(
            lambda q: pltpu.make_async_copy(
                src.at[pl.ds(base_of(q), width)], state.at[q + ROW0], sems.at[1]
            ),
            steps[-1], src, width, sems.at[1],
        )
        for n in range(len(steps)):
            for copy in hist_copies(n, (2, 3)):
                copy.wait()
        turned = jnp.transpose(flux_hist[0])[NPOLE + ROW0 : NPOLE + ROW0 + 8]
        for o in range(width // 128):
            gather_out[8 * o : 8 * o + 8, :] = turned[:, 128 * o : 128 * o + 128]
    else:
        for n in range(len(steps)):
            for copy in hist_copies(n, (2, 3)):
                copy.wait()
        start, extent = (HALO, count) if fast else (0, width)
        first_row = jnp.where(polar == 1, NPOLE + WEDGE, 0)

        @pl.loop(first_row, rows)
        def _(q):
            row = pl.ds(base_of(q), width)
            src[row, :] = with_flux(src[row, :], q)
            pltpu.make_async_copy(
                src.at[pl.ds(base_of(q) + start, extent)], air_out.at[q_of(q)], sems.at[1]
            ).start()

        for kind, count_rows in ((1, rows - NPOLE - WEDGE), (0, rows)):
            @pl.when(polar == kind)
            def _(count_rows=count_rows):
                whole = src.at[pl.ds(0, count_rows * extent)]
                pltpu.make_async_copy(whole, whole, sems.at[1]).wait()

    @pl.when(polar == 1)
    def _():
        for n, step in enumerate(steps):
            if step <= WEDGE:
                for copy in hist_copies(n, (0, 1)):
                    copy.wait()


def outside_steps(rows, count, width, fast, steps, scal, big, small):
    levels = 128
    any_spec = pl.BlockSpec(memory_space=pl.ANY)
    vmem = pl.BlockSpec(memory_space=pltpu.VMEM)
    total = rows + 2 * ROW0
    shape = jax.ShapeDtypeStruct
    square = shape((width, 128), F32)
    hist = [shape((len(steps), width, 128), F32)] * 4
    if steps[0] == 1:
        out_shape = [shape((total, width, levels), F32)] + hist + [square, square]
        out_shape.append(shape((width // 16, 128), F32))
    else:
        out_shape = [shape((rows, count if fast else width, levels), F32)] + hist
    return pl.pallas_call(
        functools.partial(outside_kernel, rows, count, width, fast, steps),
        out_shape=out_shape,
        in_specs=[pl.BlockSpec(memory_space=pltpu.SMEM)]
        + [any_spec] * len(big)
        + [vmem] * len(small),
        out_specs=[any_spec] * 5 + [vmem] * (len(out_shape) - 5),
        scratch_shapes=[
            pltpu.VMEM(((total + BEYOND) * width + 16, levels), F32),
            pltpu.VMEM(((total + BEYOND) * width + 16, levels), F32),
            pltpu.VMEM((2 * width, 2 * levels), BF16),
            pltpu.VMEM((2 * width, 2 * levels), BF16),
            pltpu.VMEM((width, 128), F32),
            pltpu.VMEM((width, 128), F32),
            pltpu.VMEM((width, 128), F32),
            pltpu.VMEM((width, 128), F32),
            pltpu.VMEM((128, width), F32),
            pltpu.VMEM((width + 16, 128), F32),
            pltpu.VMEM((256, 256), BF16),
            pltpu.VMEM((2, ROW0, 8, 128), F32),
            pltpu.VMEM((width, 128), F32),
        ]
        + [pltpu.VMEM((len(steps), width, 128), F32)] * 4
        + [
            pltpu.SemaphoreType.DMA((4 * len(steps),)),
            pltpu.SemaphoreType.DMA((4,)),
        ],
        compiler_params=pltpu.CompilerParams(vmem_limit_bytes=VMEM_LIMIT),
        cost_estimate=pl.CostEstimate(
            flops=len(steps) * rows * width * levels * levels * 4,
            bytes_accessed=rows * width * levels * 10,
            transcendentals=0,
        ),
        name="outside_steps",
    )(scal, *big, *small)


def cap_kernel(rows, count, width, blocks, fast, steps, parts, scal, *refs):
    scal = Place(scal)
    last = steps[-1] == STEPS
    wedge_steps = [step + 1 for step in steps if step < STEPS]
    spec_in, refs = refs[:parts], refs[parts:]
    hists, refs = refs[: 4 * len(cap_hists(steps))], refs[4 * len(cap_hists(steps)) :]
    names = ["free", "t_high", "t_low", "rotate", "coef", "sea", "sea_ring"]
    if steps[0] > 1:
        names += ["gathered", "flux", "ring_flux", "wedge"]
    if last:
        names += list(range(blocks // 2))
    loads = dict(zip(names, refs[: len(names)]))
    refs = refs[len(names) :]
    small_in, refs = refs[:3], refs[3:]
    if last:
        refs = refs[1:]
        (air_out, sea_out), refs = refs[:2], refs[2:]
    else:
        (spec_out, wedge_out, sea_out, flux_out, sea_ring_out, ring_out, gather_to), refs = (
            refs[:7], refs[7:])
    (spec_a, spec_b, cur, prev, xcat, kcat_a, kcat_b, point, sea, flux, pad,
     ring, sea_ring, shares, t_high, t_low, stencil, coef, coef_ring, gathered, sea_hist,
     flux_hist, side, turn, free_top, free_row, vcat, weight, courant, mix, load_sems, row_sems) = refs[:32]
    if last:
        back, free_late, sems = refs[32:]
    else:
        gather_out, store_sems = refs[32:]
    flip, polar, block = scal[0], scal[1], scal[2]
    lanes = lane_iota((width, 128))
    own = pl.ds(pl.multiple_of(block * width, 128), width)

    def hist(kind, step):
        half = 0 if step <= SPLIT else 1
        return hists[4 * cap_hists(steps).index(half) + kind].at[step - 1 - SPLIT * half]

    def own_dot(x):
        return table_dot(t_high[own, :], t_low[own, :], x)

    def wedge_step(step):
        at = wedge_steps.index(step)
        pending = flux_hist[at]
        for j in range(step - 1):
            base = 8 + j * width
            if j == step - 2:
                south_ref, south = side.at[at], 0
            else:
                south_ref, south = cur, base + width
            advance(width, cur, base, prev, 0, south_ref, south, winds(courant)[:2], xcat)
            prev[...] = cur[pl.ds(base, width), :]
            mixed = dot(xcat[...], vcat[...])
            y = mixed[:, :128] + mixed[:, 128:]
            lane = NPOLE + j + ROW0
            out = exchange(y, lane, sea[...], coef[...])
            cur[pl.ds(base, width), :] = y + air_gain * out
            pending += pltpu.roll(out, lane, 1)
        return pending

    def cap_step(step, src, dst, slot):
        count_rows = CAP - step
        if step > 1:
            ready("gathered", "sea_ring", "ring_flux")
        if step > 1:
            for j in range(blocks):
                ring[pl.ds(NPOLE, 8), pl.ds(j * width, width)] = gathered[
                    j, pl.ds(8 * slot, 8), :
                ]
            old, at = sea_ring[...], ring[...]
            place = lax.broadcasted_iota(jnp.int32, old.shape, 0)
            up = jnp.where(place == 0, 0.0, pltpu.roll(old, 1, 0))
            down = pltpu.roll(old, old.shape[0] - 1, 0)
            ring_width = blocks * width
            around = up + down + pltpu.roll(old, 1, 1) + pltpu.roll(old, ring_width - 1, 1)
            sea_ring[...] = old - ocean_gain * at + ocean_diffusion * (around - 4.0 * old)
            spot = lane_iota(at.shape) % width
            at = jnp.where((spot >= HALO) & (spot < HALO + count), at, 0.0)
            high, low = two_parts(at)
            ready("t_high", "t_low", "rotate", "weight")
            both = dot(jnp.concatenate([high, low], axis=0), t_high[...])
            sums = both[:24] + both[24:] + dot(high, t_low[...])
            sums = sums * (air_gain * weight[0:1, :])
            sums = jnp.concatenate([sums, jnp.zeros((104, NK), F32)], axis=0)
            moved = jnp.transpose(sums)
            swapped = jnp.concatenate([moved[128:], moved[:128]], axis=0)
            beside = pltpu.roll(moved, 1, 1) + pltpu.roll(moved, 127, 1)
            top = jnp.broadcast_to(courant[0:1, 0:1], (1, 128))
            shares[...] = (
                stencil[0] * moved + diffusion_rate * beside + (stencil[2] * top) * swapped
            )
            stencil[1] = stencil[2] * courant[0:1, :]

        point[...] = jnp.zeros_like(point)
        kcats = (kcat_a, kcat_b)
        first = lane_iota((128, 128)) == 0

        def load(q, slot):
            cut = scal[3 + q]
            for o, other in ((0, 128), (128, 0)):
                more = pltpu.roll(shares[pl.ds(o, 128), :], lax.rem(128 - q, 128), 1)
                x = jnp.where(first, more, 0.0)
                if step > 2:
                    here = src[q + 1, pl.ds(o, 128), :]
                    swapped = src[q + 1, pl.ds(other, 128), :]
                    around = src[q, pl.ds(o, 128), :] + src[q + 2, pl.ds(o, 128), :]
                    x += (
                        stencil[0, pl.ds(o, 128), :] * here
                        + diffusion_rate * around
                        + stencil[1, pl.ds(o, 128), :] * swapped
                    )
                x = jnp.where(lax.broadcasted_iota(jnp.int32, x.shape, 0) <= cut, x, 0.0)
                high, low = two_parts(x)
                kcats[slot][pl.ds(o, 128), 0:128] = high
                kcats[slot][pl.ds(o, 128), 128:256] = low

        streamed = step == steps[0] and step > 1

        def finish(q, slot, between):
            mixed = dot(kcats[slot][...], vcat[...])
            between()
            y = mixed[:, :128] + mixed[:, 128:]
            dst[q + 1] = y
            point[...] += pltpu.roll(jnp.where(lane_iota(y.shape) == 0, y, 0.0), q, 1)

        pairs = (count_rows + 1) // 2
        if streamed:
            spec_row(0).wait()
            spec_row(1).wait()

        def arrive(n):
            spec_row(2 * n + 2).wait()
            spec_row(2 * n + 3).wait()

        if step > 1:
            two_at_a_time(0, pairs, load, finish, arrive if streamed else None)
        if streamed:
            for q in range(2 * pairs + 2, CAP):
                spec_row(q).wait()
        if step == steps[-1] and not last:
            store(dst.at[pl.ds(1, CAP)], spec_out)
        ready("free")
        top = pltpu.roll(free_top[...], (128 - NPOLE * (step - 1)) % 128, 1)
        point[...] += jnp.where(lane_iota((NK, 128)) < NPOLE, top, 0.0)

        ready("t_high", "t_low", "sea_ring", "coef_ring", "coef", "sea", "flux", "hist")
        at_rows = jnp.transpose(point[...])[:NPOLE]
        high, low = two_parts(at_rows)
        both = dot_nt(jnp.concatenate([high, low], axis=0), t_high[...])
        surface = both[:NPOLE] + both[NPOLE:] + dot_nt(high, t_low[...])
        ring[0:NPOLE, :] = coef_ring[...] * (sea_ring[0:NPOLE, :] - surface)

        here = pltpu.roll(own_dot(point[...]), ROW0, 1)
        in_cap = (lanes >= ROW0) & (lanes < ROW0 + NPOLE)
        total = jnp.where(in_cap, coef[...] * (sea[...] - here), flux[...])
        flux[...] = total
        if step < STEPS:
            edge = pltpu.roll(total, 128 - (ROW0 + NPOLE - 1), 1)
            row = free_row[slot] if step == 1 else dst[NPOLE] + free_row[slot]
            prev[...] = own_dot(row) + air_gain * jnp.where(lanes == 0, edge, 0.0)
        new = sea_next(width, polar, rows, sea[...], total, pad)
        sea[...] = jnp.where(lanes >= ROW0 + NPOLE + step - 1, sea_hist[slot], new)

    copies = {}
    order = []
    stores = []

    def store(source, target):
        copy = pltpu.make_async_copy(source, target, store_sems.at[len(stores)])
        stores.append(copy)
        copy.start()

    def fetch(name, source, target):
        copy = pltpu.make_async_copy(source, target, load_sems.at[len(order)])
        order.append(copy)
        copies.setdefault(name, []).append(copy)
        copy.start()

    def ready(*wanted):
        for name in wanted:
            for copy in copies.pop(name, ()):
                copy.wait()

    def spec_row(q):
        return pltpu.make_async_copy(spec_in[0].at[q], spec_a.at[q + 1], row_sems.at[q])

    @pl.when(polar == 1)
    def _():
        for n, (source, target) in enumerate(zip(small_in, (weight, courant, mix))):
            fetch(("weight", "courant", "mix")[n], source, target)
        if steps[0] > 1:
            fetch("gathered", loads["gathered"], gathered)
            fetch("sea_ring", loads["sea_ring"], sea_ring)
            fetch("ring_flux", loads["ring_flux"], ring.at[pl.ds(0, NPOLE)])
        fetch("t_high", loads["t_high"], t_high)
        fetch("t_low", loads["t_low"], t_low)
        fetch("rotate", loads["rotate"].at[0], stencil.at[0])
        fetch("rotate", loads["rotate"].at[1], stencil.at[2])
        if steps[0] > 1:
            @pl.loop(0, CAP)
            def _(q):
                spec_row(q).start()

        part = NK // blocks
        some = part // 2
        rows_15 = [step for step in steps if step < STEPS]
        for i in range(blocks):
            owner = (i % 2) * (blocks // 2) + i // 2
            for n in range(2):
                at = pl.ds(KMAX * n + n + some * owner, some)
                take = pl.ds(some * n, some)
                fetch("free", loads["free"].at[i, take], free_top.at[at])
                for slot, step in enumerate(rows_15):
                    take = pl.ds(part * step + some * n, some)
                    fetch("free", loads["free"].at[i, take], free_row.at[slot, at])
        if last:
            side_y, place_z = lax.rem(block, 2), block // 2
            for z in range(blocks // 2):
                for y in range(2):
                    owner = (blocks // 2) * jnp.bitwise_xor(side_y, y) + jnp.bitwise_xor(place_z, z)
                    for n in range(2):
                        at = pl.multiple_of((KMAX + 1) * n + some * owner, some)
                        fetch(
                            "late",
                            loads[z].at[y, :, pl.ds(some * n, some)],
                            free_late.at[:, pl.ds(at, some)],
                        )
        if steps[0] == 1:
            fetch("sea_ring", loads["sea_ring"], sea_ring)
            for i in range(blocks):
                for o in range(width // 128):
                    fetch(
                        "gathered",
                        loads["free"].at[i, pl.ds(STEPS * part + 8 * o, 8)],
                        gathered.at[i, pl.ds(8, 8), pl.ds(128 * o, 128)],
                    )
        for i in range(blocks):
            for o in range(width // 128):
                at = STEPS * (NK // blocks) + width // 16 + NPOLE * o
                fetch(
                    "coef_ring",
                    loads["free"].at[i, pl.ds(at, NPOLE)],
                    coef_ring.at[:, pl.ds(i * width + 128 * o, 128)],
                )
        fetch("coef", loads["coef"], coef)
        fetch("sea", loads["sea"], sea)
        fetch("flux", loads["flux"] if steps[0] > 1 else hist(3, 1), flux)
        for n, step in enumerate(steps):
            fetch("hist", hist(2, step), sea_hist.at[n])
        for n, step in enumerate(wedge_steps):
            fetch("hist", hist(3, step), flux_hist.at[n])
            fetch("hist", hist(1, step - 1), side.at[n])
            row = pl.ds(8 + (step - 2) * width, width)
            fetch("hist", hist(0, step - 1), cur.at[row])
        kept = steps[0] - 1
        for j in range(kept):
            fetch("hist", loads["wedge"].at[j], cur.at[pl.ds(8 + j * width, width)])
        ready("mix", "courant")
        mixing(mix, vcat)
        for ref in (spec_a, spec_b):
            ref[0] = jnp.zeros((NK, 128), F32)
            for beyond in range(CAP + 1, CAP + 4):
                ref[beyond] = jnp.zeros((NK, 128), F32)
        cur[0:8, :] = jnp.zeros((8, 128), F32)
        pad[...] = jnp.zeros_like(pad)

        src, dst = spec_a, spec_b
        for n, step in enumerate(steps):
            cap_step(step, src, dst, n)
            src, dst = dst, src
            if step < STEPS:
                pending = wedge_step(step + 1)
                flux[...] = pending
                if not last:
                    turned = jnp.transpose(pending)[NPOLE + ROW0 : NPOLE + ROW0 + 8]
                    for to in range(blocks):
                        gather_out[to, pl.ds(8 * n, 8), :] = turned
        ready(*list(copies))
        if last:
            start, extent = (HALO, count) if fast else (0, width)

            def send(ref, offset, q):
                r = jnp.where(flip == 1, rows - 1 - q, q)
                return pltpu.make_async_copy(
                    ref.at[pl.ds(offset + start, extent)], air_out.at[r], sems.at[q]
                )

            for j in range(WEDGE):
                send(cur, 8 + j * width, NPOLE + j).start()

            @pl.loop(0, NPOLE // 2)
            def _(pair):
                parts_of = [two_parts(src[2 * pair + n + 1] + free_late[2 * pair + n])
                            for n in range(2)]
                highs = jnp.concatenate([high for high, _ in parts_of], axis=1)
                crossed = dot(t_low[own, :], highs)
                for n, (high, low) in enumerate(parts_of):
                    q = 2 * pair + n
                    both = dot(t_high[own, :], jnp.concatenate([high, low], axis=1))
                    y = both[:, :128] + both[:, 128:] + crossed[:, 128 * n : 128 * n + 128]
                    edge = pltpu.roll(flux[...], lax.rem(128 - ROW0 - q, 128), 1)
                    back[q] = y + air_gain * jnp.where(lanes == 0, edge, 0.0)
                    send(back.at[q], 0, q).start()

            @pl.loop(0, NPOLE)
            def _(q):
                send(back.at[q], 0, q).wait()

            for j in range(WEDGE):
                send(cur, 8 + j * width, NPOLE + j).wait()
        else:
            for j in range(len(wedge_steps) + kept):
                store(cur.at[pl.ds(8 + j * width, width)], wedge_out.at[j])
            for source, target in (
                (sea, sea_out), (flux, flux_out), (sea_ring, sea_ring_out),
                (ring.at[pl.ds(0, NPOLE)], ring_out), (gather_out, gather_to),
            ):
                store(source, target)
            for copy in stores:
                copy.wait()

    if last:
        @pl.when(polar == 0)
        def _():
            copy = pltpu.make_async_copy(hist(2, STEPS), sea, load_sems.at[0])
            copy.start()
            copy.wait()

        turn[...] = jnp.transpose(pltpu.roll(sea[...], width - HALO, 0))

        @pl.loop(0, rows)
        def _(q):
            r = jnp.where(flip == 1, rows - 1 - q, q)
            sea_out[pl.ds(r, 1), :] = turn[pl.ds(q + ROW0, 1), pl.ds(0, count)]


def cap_hists(steps):
    return ([0] if steps[0] <= SPLIT + 1 else []) + ([1] if steps[-1] + 1 > SPLIT else [])


def cap_steps(rows, count, width, blocks, fast, steps, scal, spec, big, small, air):
    levels = 128
    ring_width = blocks * width
    last = steps[-1] == STEPS
    any_spec = pl.BlockSpec(memory_space=pl.ANY)
    vmem = pl.BlockSpec(memory_space=pltpu.VMEM)
    shape = jax.ShapeDtypeStruct
    square = pltpu.VMEM((width, 128), F32)
    aliases = {}
    extra = []
    if last:
        out_shape = [
            shape((rows, count if fast else width, levels), F32),
            shape((rows, count), F32),
        ]
        out_specs = [any_spec, vmem]
        extra = [
            pltpu.VMEM((NPOLE, width, levels), F32),
            pltpu.VMEM((NPOLE, NK, levels), F32),
            pltpu.SemaphoreType.DMA((NPOLE + WEDGE,)),
        ]
        aliases = {1 + len(spec) + len(big) + len(small): 0}
    else:
        out_shape = [
            shape((CAP, NK, levels), F32),
            shape((steps[-1], width, levels), F32),
            shape((width, 128), F32),
            shape((width, 128), F32),
            shape((24, ring_width), F32),
            shape((NPOLE, ring_width), F32),
            shape((blocks, 16, width), F32),
        ]
        out_specs = [any_spec] * 7
        extra = [pltpu.VMEM((blocks, 16, width), F32), pltpu.SemaphoreType.DMA((16,))]
    return pl.pallas_call(
        functools.partial(cap_kernel, rows, count, width, blocks, fast, steps, len(spec)),
        out_shape=out_shape,
        in_specs=[pl.BlockSpec(memory_space=pltpu.SMEM)]
        + [any_spec] * (len(spec) + len(big))
        + [any_spec] * (len(small) + len(air)),
        out_specs=out_specs,
        scratch_shapes=[
            pltpu.VMEM((CAP + 4, NK, levels), F32),
            pltpu.VMEM((CAP + 4, NK, levels), F32),
            pltpu.VMEM((WEDGE * width + 16, levels), F32),
            square,
            pltpu.VMEM((width, 2 * levels), BF16),
            pltpu.VMEM((NK, 2 * levels), BF16),
            pltpu.VMEM((NK, 2 * levels), BF16),
            pltpu.VMEM((NK, 128), F32),
            square,
            square,
            pltpu.VMEM((width + 16, 128), F32),
            pltpu.VMEM((24, ring_width), F32),
            pltpu.VMEM((24, ring_width), F32),
            pltpu.VMEM((NK, 128), F32),
            pltpu.VMEM((ring_width, NK), BF16),
            pltpu.VMEM((ring_width, NK), BF16),
            pltpu.VMEM((3, NK, levels), F32),
            square,
            pltpu.VMEM((NPOLE, ring_width), F32),
            pltpu.VMEM((blocks, 16, width), F32),
            pltpu.VMEM((2, width, 128), F32),
            pltpu.VMEM((2, width, 128), F32),
            pltpu.VMEM((2, width, 128), F32),
            pltpu.VMEM((128, width), F32),
            pltpu.VMEM((NK, 128), F32),
            pltpu.VMEM((2, NK, 128), F32),
            pltpu.VMEM((256, 256), BF16),
            pltpu.VMEM((8, NK), F32),
            pltpu.VMEM((1, 128), F32),
            pltpu.VMEM((128, 128), F32),
            pltpu.SemaphoreType.DMA((13 * blocks + 32,)),
            pltpu.SemaphoreType.DMA((CAP,)),
        ]
        + extra,
        input_output_aliases=aliases,
        compiler_params=pltpu.CompilerParams(vmem_limit_bytes=VMEM_LIMIT),
        cost_estimate=pl.CostEstimate(
            flops=len(steps) * CAP * NK * levels * levels * 4,
            bytes_accessed=20_000_000,
            transcendentals=0,
        ),
        name="cap_steps",
    )(scal, *spec, *big, *small, *air)


def shift(x, axis, by, wrap):
    size = lax.axis_size(axis)
    pairs = [(i, (i + by) % size) for i in range(size) if wrap or 0 <= i + by < size]
    return lax.ppermute(x, axis, pairs)


def between_caps(x, by):
    size, bands = lax.axis_size("lon"), lax.axis_size("lat")
    pairs = [(b * size + i, b * size + (i ^ by)) for b in (0, bands - 1) for i in range(size)]
    return lax.ppermute(x, ("lat", "lon"), pairs)


def spread(copies):
    return lax.all_to_all(copies, "lon", split_axis=0, concat_axis=0, tiled=True)


def local(air_temp, sea_temp, land_sea, courant, vertical_mix, cutoffs):
    rows, count, levels = air_temp.shape
    blocks = lax.axis_size("lon")
    nlon = blocks * count
    width = round_up(count + 2 * HALO, 128)
    depth = round_up(count, 128)
    fast = count % 8 == 0
    scal = cutoffs

    window, forward, weight = tables(blocks, count, width, depth)
    t_high, t_low = (jnp.asarray(part) for part in window)
    rotate = rotations(nlon)
    rotate_owned = jnp.asarray(rotate[:, owner_order(blocks)])
    rotate = jnp.asarray(rotate)
    weights = jnp.asarray(np.tile(weight.astype(np.float32), (8, 1)))
    courant = courant.reshape(1, levels)

    west = shift(air_temp[:, count - HALO :], "lon", 1, True)
    east = shift(air_temp[:, :HALO], "lon", -1, True)
    mine = shares_of_sea(rows, count, blocks, sea_temp, land_sea)
    half = blocks // 2
    keep, send = start_spectra(blocks, scal, air_temp, jnp.asarray(forward))
    mine, west, east = lax.optimization_barrier((mine, west, east))
    got = spread(mine)

    taken = between_caps(send, 1)
    half_sum = [keep[j] + taken[j] for j in range(half)]

    outs = windows(
        rows, count, width, blocks, fast, scal, got, land_sea, air_temp, west, east
    )
    own_window, sea_ring, cap_coef = outs[:3]
    if fast:
        last_rows, first_rows = outs[3:]
    else:
        def edge(part):
            extra = own_window[:, part].transpose(1, 0, 2).reshape(ROW0, -1, levels)
            at, after = edge_extent(count, width)
            row = jnp.concatenate([west[part], air_temp[part], east[part]], 1)
            row = jnp.pad(row, ((0, 0), (0, at - row.shape[1]), (0, 0)))
            extra = jnp.pad(extra, ((0, 0), (0, after - at - extra.shape[1]), (0, 0)))
            return jnp.concatenate([row, extra], 1)

        last_rows, first_rows = edge(slice(rows - ROW0, rows)), edge(slice(0, ROW0))
    north = shift(last_rows, "lat", 1, False)
    south = shift(first_rows, "lat", -1, False)

    if fast:
        air = air_temp
    else:
        middle = jnp.concatenate([west, air_temp, east], 1)
        inner = count + 2 * HALO
        air = jnp.concatenate([north[:, :inner], middle, south[:, :inner]], 0)
        air = jnp.pad(air, ((0, 0), (0, width - count - 2 * HALO), (0, 0)))
    half_sum, own_window = lax.optimization_barrier((half_sum, own_window))
    parts = [between_caps(half_sum[j], 2 * j) for j in range(1, half)]
    outs = outside_steps(
        rows, count, width, fast, tuple(range(1, SPLIT + 1)), scal, (air, west, east, north, south),
        (own_window, courant, vertical_mix),
    )
    state, early, sea, coef, gathered = outs[0], tuple(outs[1:5]), outs[5], outs[6], outs[7]
    parts, state = lax.optimization_barrier((parts, state))
    gathered, late_free = free_steps(
        blocks, scal, (half_sum[0], *parts), rotate_owned, courant, vertical_mix, gathered,
        cap_coef,
    )
    gathered, state = lax.optimization_barrier((gathered, state))
    late_pair = jnp.stack([late_free, between_caps(late_free, 1)])
    free = spread(gathered)
    outs = outside_steps(
        rows, count, width, fast, tuple(range(SPLIT + 1, STEPS + 1)), scal,
        (state, early[2], early[3], coef), (courant, vertical_mix),
    )
    air, late = outs[0], tuple(outs[1:5])
    free, air, late = lax.optimization_barrier((free, air, late))

    more, spec = (), ()
    for steps in ((1, 2), (3, 4), (5, 6)):
        hists = sum(((early, late)[h] for h in cap_hists(steps)), ())
        big = hists + (free, t_high, t_low, rotate, coef, sea, sea_ring) + more
        if steps[-1] == STEPS:
            big += tuple(late_free)
        outs = cap_steps(
            rows, count, width, blocks, fast, steps, scal, spec, big,
            (weights, courant, vertical_mix), (air,) if steps[-1] == STEPS else (),
        )
        if steps[-1] < STEPS:
            spec, wedge, sea, flux, sea_ring, ring_flux, mine = outs
            if steps[0] == 1:
                late_pair, mine = lax.optimization_barrier((late_pair, mine))
                late_free = [late_pair] + [
                    between_caps(late_pair, 2 * j) for j in range(1, half)
                ]
            gathered = spread(mine)
            spec, more = (spec,), (gathered, flux, ring_flux, wedge)
    air, sea = outs
    if not fast:
        air = air[:, HALO : HALO + count]
    sea = lax.all_to_all(sea, "lon", split_axis=0, concat_axis=1, tiled=True)
    return air, sea


def solution(mesh):
    placed = (P("lat", "lon", None), P(("lat", "lon"), None), P("lat", "lon"), P(), P(), P())
    return jax.shard_map(
        local,
        mesh=mesh,
        in_specs=placed,
        out_specs=(P("lat", "lon", None), P(("lat", "lon"), None)),
        check_vma=False,
    )
```

```python
import functools
import math

import jax
import jax.numpy as jnp
import ml_dtypes
import numpy as np
from jax import lax
from jax.experimental import pallas as pl
from jax.experimental.pallas import tpu as pltpu
from jax.sharding import PartitionSpec as P

NPOLE = 16
KMAX = 127
STEPS = 6
NK = 2 * (KMAX + 1)
CAP = NPOLE + STEPS
HALO = 8
ROW0 = STEPS
WEDGE = STEPS - 1
BEYOND = 5
SPLIT = 3

diffusion_rate = 0.1
air_gain = 0.5
ocean_gain = 0.3
ocean_diffusion = 0.2
sea_coef = 0.5
land_coef = 0.15

F32 = jnp.float32
BF16 = jnp.bfloat16
VMEM_LIMIT = 56 * 1024 * 1024


def round_up(value, unit):
    return -(-value // unit) * unit


def two_parts(x):
    high = x.astype(BF16)
    return high, (x - high.astype(F32)).astype(BF16)


def dot(a, b):
    return jnp.dot(a, b, preferred_element_type=F32)


def dot_nt(a, b):
    return lax.dot_general(a, b, (((1,), (1,)), ((), ())), preferred_element_type=F32)


def table_dot(high, low, x):
    x_high, x_low = two_parts(x)
    both = dot(high, jnp.concatenate([x_high, x_low], axis=1))
    return both[:, :128] + both[:, 128:] + dot(low, x_high)


def numpy_parts(table):
    high = table.astype(ml_dtypes.bfloat16)
    low = (table - high.astype(np.float64)).astype(ml_dtypes.bfloat16)
    return high, low


def owner_order(blocks):
    k = np.arange(KMAX + 1).reshape(blocks, -1)
    return np.concatenate([k, k + KMAX + 1], 1).reshape(-1)


@functools.lru_cache(maxsize=None)
def tables(blocks, count, width, depth):
    nlon = blocks * count
    wavenum = np.arange(KMAX + 1)
    weight = np.where(wavenum == 0, 1.0, 2.0) / nlon

    def table(columns):
        phase = (columns[:, None] * wavenum[None, :]) % nlon * (2.0 * math.pi / nlon)
        return np.concatenate([np.cos(phase), np.sin(phase)], 1)

    window = np.concatenate(
        [table((j * count - HALO + np.arange(width)) % nlon) for j in range(blocks)], 0
    )
    forward = np.zeros((blocks, NK, depth))
    for j in range(blocks):
        own = table(j * count + np.arange(count)) * np.tile(weight, 2)
        forward[j, :, :count] = own.T[owner_order(blocks)]
    high, low = numpy_parts(forward)
    return numpy_parts(window), np.concatenate([high, high, low], 2), np.tile(weight, 2)


@functools.lru_cache(maxsize=None)
def rotations(nlon):
    theta = np.arange(KMAX + 1) * (2.0 * math.pi / nlon)
    stay = 1.0 - 4.0 * diffusion_rate + 2.0 * diffusion_rate * np.tile(np.cos(theta), 2)
    turn = np.concatenate([-np.sin(theta), np.sin(theta)])
    both = np.stack([stay, turn]).astype(np.float32)
    return np.ascontiguousarray(np.broadcast_to(both[:, :, None], (2, NK, 128)))


def mixing(mix, vcat):
    row = lax.broadcasted_iota(jnp.int32, (128, 128), 0)
    high, low = two_parts(jnp.where(row == lane_iota((128, 128)), mix[...] + 1.0, mix[...]))
    vcat[0:128, 0:128] = high
    vcat[128:256, 0:128] = high
    vcat[0:128, 128:256] = low
    vcat[128:256, 128:256] = jnp.zeros_like(low)


def winds(courant):
    c = courant[0:1, :]
    top = jnp.broadcast_to(c[:, 0:1], c.shape)
    return [diffusion_rate + sign * 0.5 * x for x in (c, top) for sign in (-1.0, 1.0)]


class Place:
    def __init__(self, cutoffs):
        band, bands = lax.axis_index("lat"), lax.axis_size("lat")
        flip = (band == bands - 1).astype(jnp.int32)
        polar = jnp.maximum(flip, (band == 0).astype(jnp.int32))
        self.cutoffs = cutoffs
        self.head = (flip, polar, lax.axis_index("lon"))

    def __getitem__(self, at):
        if isinstance(at, int) and at < 3:
            return self.head[at]
        q = at - 3
        inside = jnp.minimum(q, NPOLE - 1)
        r = jnp.where(self.head[0] == 1, 2 * NPOLE - 1 - inside, inside)
        return jnp.where(q < NPOLE, self.cutoffs[r], KMAX)


def lane_iota(shape):
    return lax.broadcasted_iota(jnp.int32, shape, len(shape) - 1)


def spectra_kernel(
    rows, count, blocks,
    scal, air, table, keep_out, send_out,
    held, own_table, stacked_a, stacked_b, sums, keep, send, sems,
):
    scal = Place(scal)
    depth = stacked_a.shape[0] // 3
    half, part = blocks // 2, NK // blocks
    flip, block = scal[0], scal[2]
    side, place = lax.rem(block, 2), block // 2
    pairs = CAP // 2

    def row(q):
        r = jnp.where(flip == 1, rows - 1 - q, q)
        return pltpu.make_async_copy(air.at[r], held.at[q], sems.at[q])

    @pl.when(scal[1] == 1)
    def _():
        fetch = pltpu.make_async_copy(table.at[block], own_table, sems.at[CAP])
        row(0).start()
        row(1).start()
        fetch.start()

        @pl.loop(2, CAP)
        def _(q):
            row(q).start()

        for ref in (stacked_a, stacked_b):
            ref[...] = jnp.zeros_like(ref)

        def load(p, slot):
            ref = (stacked_a, stacked_b)[slot]
            for n in range(2):
                high, low = two_parts(held[2 * p + n])
                lanes = slice(128 * n, 128 * n + 128)
                ref[0:count, lanes] = high
                ref[depth : depth + count, lanes] = low
                ref[2 * depth : 2 * depth + count, lanes] = high

        def finish(p, slot, between):
            sums[slot] = dot(own_table[...], (stacked_a, stacked_b)[slot][...])
            between()
            for n in range(2):
                lanes = slice(128 * n, 128 * n + 128)
                for z in range(half):
                    at = jnp.bitwise_xor(place, z)
                    mine = pl.multiple_of((side * half + z) * part, part)
                    other = pl.multiple_of(((1 - side) * half + z) * part, part)
                    keep[at, 2 * p + n] = sums[slot, pl.ds(mine, part), lanes]
                    send[at, 2 * p + n] = sums[slot, pl.ds(other, part), lanes]

        def arrive(n):
            for q in range(2, 6):
                row(4 * n + q).wait()

        row(0).wait()
        row(1).wait()
        fetch.wait()
        two_at_a_time(0, pairs // 2, load, finish, arrive)
        finish(pairs - 1, 0, lambda: None)
        out = [
            pltpu.make_async_copy(send.at[:, pl.ds(0, CAP)], send_out, sems.at[0]),
            pltpu.make_async_copy(keep.at[:, pl.ds(0, CAP)], keep_out, sems.at[1]),
        ]
        for copy in out:
            copy.start()
        for copy in out:
            copy.wait()


def start_spectra(blocks, scal, air_temp, table):
    rows, count, levels = air_temp.shape
    half, part = blocks // 2, NK // blocks
    depth = table.shape[2] // 3
    any_spec = pl.BlockSpec(memory_space=pl.ANY)
    out = jax.ShapeDtypeStruct((half, CAP, part, levels), F32)
    return pl.pallas_call(
        functools.partial(spectra_kernel, rows, count, blocks),
        out_shape=[out, out],
        in_specs=[pl.BlockSpec(memory_space=pltpu.SMEM), any_spec, any_spec],
        out_specs=[any_spec, any_spec],
        scratch_shapes=[
            pltpu.VMEM((CAP, count, levels), F32),
            pltpu.VMEM((NK, 3 * depth), BF16),
            pltpu.VMEM((3 * depth, 2 * levels), BF16),
            pltpu.VMEM((3 * depth, 2 * levels), BF16),
            pltpu.VMEM((2, NK, 2 * levels), F32),
            pltpu.VMEM((half, CAP, part, levels), F32),
            pltpu.VMEM((half, CAP, part, levels), F32),
            pltpu.SemaphoreType.DMA((CAP + 2,)),
        ],
        compiler_params=pltpu.CompilerParams(vmem_limit_bytes=VMEM_LIMIT),
        name="start_spectra",
    )(scal, air_temp, table)


def free_kernel(blocks, parts, scal, *refs):
    scal = Place(scal)
    sums, refs = refs[:parts], refs[parts:]
    rotate, courant, mix, edge, cap_coef, early, late, state, mask, xcat, vcat = refs
    part = NK // blocks
    some = part // 2
    owner = lax.rem(scal[2], 2) * (blocks // 2) + scal[2] // 2

    @pl.when(scal[1] == 1)
    def _():
        mixing(mix, vcat)
        state[0] = jnp.zeros((part, 128), F32)
        state[1 : CAP + 1] = functools.reduce(jnp.add, [ref[...] for ref in sums])
        at = pl.ds(pl.multiple_of(owner * part, part), part)
        stay, turn = rotate[0, at, :], rotate[1, at, :] * courant[0:1, :]
        wavenum = lax.broadcasted_iota(jnp.int32, (part, 128), 0) % some + owner * some
        for q in range(CAP):
            mask[q] = jnp.where(wavenum <= scal[3 + q], 1.0, 0.0)
        first = lane_iota((part, 128)) == 0
        top = jnp.zeros((part, 128), F32)
        for step in range(1, STEPS + 1):
            size = CAP - step
            here = state[1 : size + 1]
            swapped = jnp.concatenate([here[:, some:], here[:, :some]], axis=1)
            x = stay * here + diffusion_rate * (state[0:size] + state[2 : size + 2])
            x = (x + turn * swapped) * mask[0:size]
            x = x.reshape(size * part, 128)
            high, low = two_parts(x)
            xcat[0 : size * part, 0:128] = high
            xcat[0 : size * part, 128:256] = low
            mixed = dot(xcat[0 : size * part, :], vcat[...])
            y = mixed[:, :128] + mixed[:, 128:]
            state[1 : size + 1] = y.reshape(size, part, 128)
            for q in range(NPOLE):
                lane = NPOLE * (step - 1) + q
                top += pltpu.roll(jnp.where(first, state[q + 1], 0.0), lane, 1)
            if step < STEPS:
                for to in range(blocks):
                    early[to, part * step : part * (step + 1), :] = state[NPOLE]
            else:
                late[...] = state[1 : NPOLE + 1]
        for to in range(blocks):
            early[to, 0:part, :] = top
            early[to, STEPS * part : STEPS * part + edge.shape[0], :] = edge[...]
            early[to, STEPS * part + edge.shape[0] :, :] = cap_coef[...]


def free_steps(blocks, scal, sums, rotate, courant, mix, edge, cap_coef):
    part = NK // blocks
    vmem = pl.BlockSpec(memory_space=pltpu.VMEM)
    shape = jax.ShapeDtypeStruct
    return pl.pallas_call(
        functools.partial(free_kernel, blocks, len(sums)),
        out_shape=[
            shape((blocks, STEPS * part + edge.shape[0] + cap_coef.shape[0], 128), F32),
            shape((NPOLE, part, 128), F32),
        ],
        in_specs=[pl.BlockSpec(memory_space=pltpu.SMEM)] + [vmem] * (len(sums) + 5),
        out_specs=[vmem] * 2,
        scratch_shapes=[
            pltpu.VMEM((CAP + 2, part, 128), F32),
            pltpu.VMEM((CAP, part, 128), F32),
            pltpu.VMEM((CAP * part, 256), BF16),
            pltpu.VMEM((256, 256), BF16),
        ],
        compiler_params=pltpu.CompilerParams(vmem_limit_bytes=VMEM_LIMIT // 4),
        name="free_steps",
    )(scal, *sums, rotate, courant, mix, edge, cap_coef)


def advance(
    width, here_ref, base, north_ref, north, south_ref, south, cour, xcat, more=None, to=0
):
    c_east, c_west = cour
    for o in range(0, width, 128):
        around = north_ref[pl.ds(north + o, 128), :] + south_ref[pl.ds(south + o, 128), :]
        x = (
            (1.0 - 4.0 * diffusion_rate) * here_ref[pl.ds(base + o, 128), :]
            + diffusion_rate * around
            + c_east * here_ref[pl.ds(base + o + 1, 128), :]
            + c_west * here_ref[pl.ds(base + o - 1, 128), :]
        )
        if more is not None:
            moved = pltpu.roll(more[0][pl.ds(o, 128), :], more[1], 1)
            x += jnp.where(lane_iota(x.shape) == 0, moved, 0.0)
        high, low = two_parts(x)
        xcat[pl.ds(to + o, 128), 0:128] = high
        xcat[pl.ds(to + o, 128), 128:256] = low


def two_at_a_time(first, pairs, load, finish, arrive=None, size=1):
    load(first, 0)

    @pl.loop(0, pairs)
    def _(n):
        if arrive is not None:
            arrive(n)
        q = first + 2 * size * n
        finish(q, 0, lambda: load(q + size, 1))
        finish(q + size, 1, lambda: load(q + 2 * size, 0))


def exchange(y, lane, sea, coef):
    back = (128 - lane) % 128
    flux = pltpu.roll(coef, back, 1) * (pltpu.roll(sea, back, 1) - y)
    return jnp.where(lane_iota(y.shape) == 0, flux, 0.0)


def sea_next(width, polar, rows, sea, flux, pad):
    pad[pl.ds(8, width), :] = sea
    east = pad[pl.ds(9, width), :]
    west = pad[pl.ds(7, width), :]
    around = east + west + pltpu.roll(sea, 1, 1) + pltpu.roll(sea, 127, 1)
    new = sea - ocean_gain * flux + ocean_diffusion * (around - 4.0 * sea)
    lane = lane_iota(sea.shape)
    first = jnp.where(polar == 1, ROW0, 0)
    return jnp.where((lane >= first) & (lane < rows + 2 * ROW0), new, 0.0)


def share_kernel(rows, count, blocks, sea, land, out):
    per = rows // blocks
    coef = coefficients(land)
    ends = (coef[:, 0:HALO], coef[:, count - HALO : count])
    for to in range(blocks):
        for i in range(blocks):
            out[to, i * per : (i + 1) * per, 0:count] = sea[:, i * count : (i + 1) * count]
        for n, end in enumerate(ends):
            out[to, :, count + HALO * n : count + HALO * (n + 1)] = end


def coefficients(land):
    return jnp.where(land[...] == 1, sea_coef, land_coef).astype(F32)


def shares_of_sea(rows, count, blocks, sea, land):
    vmem = pl.BlockSpec(memory_space=pltpu.VMEM)
    return pl.pallas_call(
        functools.partial(share_kernel, rows, count, blocks),
        out_shape=jax.ShapeDtypeStruct((blocks, rows, count + 2 * HALO), F32),
        in_specs=[vmem, vmem],
        out_specs=vmem,
        compiler_params=pltpu.CompilerParams(vmem_limit_bytes=VMEM_LIMIT // 4),
        name="shares_of_sea",
    )(sea, land)


def windows_kernel(rows, count, width, blocks, scal, got, land, air, west, east, *refs):
    scal = Place(scal)
    own, ring_sea, cap_coef = refs[:3]
    wide, held, sems = refs[-3:]
    edges = list(zip(refs[3:-3], (rows - ROW0, 0)))
    copies = []
    for n, (ref, first) in enumerate(edges):
        some = pl.ds(first, ROW0)
        for m, (source, offset, size) in enumerate(
            ((west, 0, HALO), (air, HALO, count), (east, HALO + count, HALO))
        ):
            copies.append(
                pltpu.make_async_copy(
                    source.at[some], ref.at[:, pl.ds(offset, size)], sems.at[3 * n + m]
                )
            )
    for copy in copies:
        copy.start()
    per = rows // blocks
    for j in range(blocks):
        columns = slice(j * width + HALO, j * width + HALO + count)
        for i in range(blocks):
            wide[per * i : per * (i + 1), columns] = got[i, per * j : per * (j + 1), 0:count]
    rest = width - HALO - count
    for j in range(blocks):
        before = ((j - 1) % blocks) * width + count
        after = ((j + 1) % blocks) * width + HALO
        end = j * width + HALO + count
        wide[:, j * width : j * width + HALO] = wide[:, before : before + HALO]
        wide[:, end : end + rest] = wide[:, after : after + rest]
    block = scal[2]
    own[0] = wide[:, pl.ds(pl.multiple_of(block * width, 128), width)]
    before, after = lax.rem(block + blocks - 1, blocks), lax.rem(block + 1, blocks)
    own[1, :, 0:HALO] = got[before, :, count + HALO : count + 2 * HALO]
    own[1, :, HALO : HALO + count] = coefficients(land)
    own[1, :, HALO + count : 2 * HALO + count] = got[after, :, count : count + HALO]
    if rest > HALO:
        own[1, :, 2 * HALO + count :] = jnp.zeros((rows, rest - HALO), F32)
    for ref, first in edges:
        base = count + 2 * HALO
        for n in range(2):
            for r in range(ROW0):
                for o in range(width // 128):
                    at = base + n * (width // 128) + o
                    ref[r, at : at + 1, :] = own[n, first + r : first + r + 1, pl.ds(128 * o, 128)]

    @pl.when(scal[1] == 1)
    def _():
        @pl.loop(0, 24)
        def _(q):
            r = jnp.where(scal[0] == 1, rows - 1 - q, q)
            ring_sea[pl.ds(q, 1), :] = wide[pl.ds(r, 1), :]

        @pl.loop(0, NPOLE)
        def _(q):
            r = jnp.where(scal[0] == 1, rows - 1 - q, q)
            held[pl.ds(q, 1), :] = own[1, pl.ds(r, 1), :]

        for o in range(width // 128):
            cap_coef[NPOLE * o : NPOLE * (o + 1), :] = held[:, 128 * o : 128 * (o + 1)]

    for copy in copies:
        copy.wait()


def edge_extent(count, width):
    inner = count + 2 * HALO
    return round_up(inner, 8), round_up(inner, 8) + 8


def windows(rows, count, width, blocks, fast, scal, got, land, air, west, east):
    any_spec = pl.BlockSpec(memory_space=pl.ANY)
    edges = [jax.ShapeDtypeStruct((ROW0, edge_extent(count, width)[1], 128), F32)] * 2
    vmem = pl.BlockSpec(memory_space=pltpu.VMEM)
    shape = jax.ShapeDtypeStruct
    return pl.pallas_call(
        functools.partial(windows_kernel, rows, count, width, blocks),
        out_shape=[
            shape((2, rows, width), F32),
            shape((24, blocks * width), F32),
            shape((NPOLE * (width // 128), 128), F32),
        ]
        + (edges if fast else []),
        in_specs=[pl.BlockSpec(memory_space=pltpu.SMEM), vmem, vmem] + [any_spec] * 3,
        out_specs=[vmem] * (5 if fast else 3),
        scratch_shapes=[
            pltpu.VMEM((rows, blocks * width), F32),
            pltpu.VMEM((NPOLE, width), F32),
            pltpu.SemaphoreType.DMA((6,)),
        ],
        compiler_params=pltpu.CompilerParams(vmem_limit_bytes=VMEM_LIMIT),
        name="windows",
    )(scal, got, land, air, west, east)


def outside_kernel(rows, count, width, fast, steps, scal, *refs):
    scal = Place(scal)
    first, last = steps[0] == 1, steps[-1] == STEPS
    if first:
        (air, west, east, north, south, own, courant, mix), refs = refs[:8], refs[8:]
        (state, *hist_outs, sea_start, coef_out, gather_out), refs = refs[:8], refs[8:]
    else:
        (state, sea_hist_in, flux_hist_in, coef_in, courant, mix), refs = refs[:6], refs[6:]
        (air_out, *hist_outs), refs = refs[:5], refs[5:]
    (buf_a, buf_b, xcat_a, xcat_b, sea, flux, point, more, turn, pad, vcat, edge_seas,
     coef, wedge, side, sea_hist, flux_hist, hist_sems, sems) = refs
    flip, polar = scal[0], scal[1]
    total = rows + 2 * ROW0
    inner = count + 2 * HALO
    lanes = lane_iota((width, 128))
    hist = tuple(zip((wedge, side, sea_hist, flux_hist), hist_outs))

    def hist_copies(n, kinds):
        return [
            pltpu.make_async_copy(hist[k][0].at[n], hist[k][1].at[n], hist_sems.at[4 * n + k])
            for k in kinds
        ]

    def base_of(q):
        return pl.multiple_of(8 + (q + ROW0) * width, 8)

    def q_of(r):
        return jnp.where(flip == 1, rows - 1 - r, r)

    def low_row(step):
        return jnp.where(polar == 1, NPOLE + step - 1, step - STEPS)

    def row_range(body, step, *sizes, meanwhile=lambda: None):
        hi = rows - 1 + STEPS - step
        ref, extent, sem = sizes

        @pl.loop(low_row(step), hi + 1)
        def _(q):
            body(q).start()

        meanwhile()
        for kind, count_rows in ((1, hi + 1 - NPOLE - step + 1), (0, hi + 1 + STEPS - step)):
            @pl.when(polar == kind)
            def _(count_rows=count_rows):
                whole = ref.at[pl.ds(0, count_rows * extent)]
                pltpu.make_async_copy(whole, whole, sem).wait()

    def begin():
        mixing(mix, vcat)
        beyond = 8 + total * width
        for ref in (buf_a, buf_b):
            ref[0:8, :] = jnp.zeros((8, 128), F32)
            ref[pl.ds(beyond, BEYOND * width + 8), :] = jnp.zeros((BEYOND * width + 8, 128), F32)
        pad[...] = jnp.zeros_like(pad)

    if first:
        needed = jnp.where(polar == 1, NPOLE - 1, -ROW0)
        at, after = edge_extent(count, width)
        for n, ref in enumerate((north, south)):
            pltpu.make_async_copy(
                ref.at[:, pl.ds(at, 8)], edge_seas.at[n], sems.at[2 + n]
            ).start()
        if fast:
            @pl.loop(0, rows)
            def _(r):
                @pl.when(q_of(r) >= needed)
                def _():
                    base = base_of(q_of(r))
                    for ref, offset, size in (
                        (west, 0, HALO), (air, HALO, count), (east, HALO + count, HALO)
                    ):
                        pltpu.make_async_copy(
                            ref.at[r], buf_a.at[pl.ds(base + offset, size)], sems.at[0]
                        ).start()

            @pl.loop(0, ROW0)
            def _(r):
                for ref, place in ((north, r - ROW0), (south, r + rows)):
                    @pl.when(q_of(place) >= needed)
                    def _(ref=ref, place=place):
                        pltpu.make_async_copy(
                            ref.at[r, pl.ds(0, inner)],
                            buf_a.at[pl.ds(base_of(q_of(place)), inner)],
                            sems.at[0],
                        ).start()

            if inner < width:
                @pl.loop(0, total)
                def _(e):
                    buf_a[pl.ds(base_of(e - ROW0) + inner, width - inner), :] = jnp.zeros(
                        (width - inner, 128), F32
                    )

            extents = ((1, (rows + ROW0 - NPOLE + 1) * inner), (0, total * inner))
        else:
            @pl.loop(0, total)
            def _(e):
                pltpu.make_async_copy(
                    air.at[e], buf_a.at[pl.ds(base_of(q_of(e - ROW0)), width)], sems.at[0]
                ).start()

            extents = ((1, total * width), (0, total * width))
        begin()
        for n, ref in enumerate((north, south)):
            pltpu.make_async_copy(
                ref.at[:, pl.ds(at, 8)], edge_seas.at[n], sems.at[2 + n]
            ).wait()
        chunks = width // 128
        for n, ref in ((0, sea), (1, coef)):
            turn[...] = jnp.zeros_like(turn)

            @pl.loop(0, rows)
            def _(r):
                turn[pl.ds(q_of(r) + ROW0, 1), :] = own[n, pl.ds(r, 1), :]

            for m, place in ((0, -ROW0), (1, rows)):
                @pl.loop(0, ROW0)
                def _(r, m=m, place=place):
                    pieces = [
                        edge_seas[m, r, pl.ds(n * chunks + o, 1), :] for o in range(chunks)
                    ]
                    turn[pl.ds(q_of(r + place) + ROW0, 1), :] = jnp.concatenate(pieces, axis=1)

            ref[...] = jnp.transpose(turn[...])
        sea_start[...] = sea[...]
        coef_out[...] = coef[...]
        for kind, extent in extents:
            @pl.when(polar == kind)
            def _(extent=extent):
                whole = buf_a.at[pl.ds(0, extent)]
                pltpu.make_async_copy(whole, whole, sems.at[0]).wait()
    else:
        small = [
            pltpu.make_async_copy(source, target, sems.at[1 + n])
            for n, (source, target) in enumerate(
                ((sea_hist_in.at[SPLIT - 1], sea), (flux_hist_in.at[SPLIT - 1], flux),
                 (coef_in, coef))
            )
        ]
        for copy in small:
            copy.start()
        row_range(
            lambda q: pltpu.make_async_copy(
                state.at[q + ROW0], buf_a.at[pl.ds(base_of(q), width)], sems.at[0]
            ),
            steps[0] - 1, buf_a, width, sems.at[0], meanwhile=begin,
        )
        for copy in small:
            copy.wait()

    def with_flux(y, q):
        gain = air_gain * pltpu.roll(flux[...], 128 - (q + ROW0), 1)
        return y + jnp.where(lanes == 0, gain, 0.0)

    xcats = (xcat_a, xcat_b)
    cour = winds(courant)
    src, dst = buf_a, buf_b
    for n, step in enumerate(steps):
        lo = low_row(step)
        hi = rows - 1 + STEPS - step
        pairs = jnp.where(polar == 1, (hi - NPOLE - step + 3) // 2, (hi + 1 + STEPS - step) // 2)
        if step > 1:
            gain = air_gain * flux[...]
            pad[pl.ds(8, width), :] = gain
            more[...] = (
                (1.0 - 4.0 * diffusion_rate) * gain
                + diffusion_rate * (pltpu.roll(gain, 1, 1) + pltpu.roll(gain, 127, 1))
                + cour[2] * pad[pl.ds(9, width), :]
                + cour[3] * pad[pl.ds(7, width), :]
            )
        point[...] = jnp.zeros_like(point)

        def load(q, slot, src=src, step=step):
            for n in range(2):
                base = base_of(q + n)
                shared = (more, lax.rem(128 - (q + n + ROW0), 128)) if step > 1 else None
                advance(width, src, base, src, base - width, src, base + width, cour[:2],
                        xcats[slot], shared, n * width)

        def finish(q, slot, between, dst=dst):
            mixed = dot(xcats[slot][...], vcat[...])
            between()
            tops = []
            for n in range(2):
                row = slice(n * width, (n + 1) * width)
                y = mixed[row, :128] + mixed[row, 128:]
                dst[pl.ds(base_of(q + n), width), :] = y
                tops.append(pltpu.roll(jnp.where(lanes == 0, y, 0.0), q + n + ROW0, 1))
            point[...] += tops[0] + tops[1]

        two_at_a_time(lo, pairs // 2, load, finish, None, 2)

        @pl.when(lax.rem(pairs, 2) == 1)
        def _(finish=finish, lo=lo, pairs=pairs):
            finish(lo + 2 * (pairs - 1), 0, lambda: None)

        total_flux = jnp.where(lanes >= lo + ROW0, coef[...] * (sea[...] - point[...]), 0.0)
        flux[...] = total_flux
        new_sea = sea_next(width, polar, rows, sea[...], total_flux, pad)
        sea[...] = new_sea
        sea_hist[n] = new_sea
        flux_hist[n] = total_flux
        for copy in hist_copies(n, (2, 3)):
            copy.start()
        if step <= WEDGE:
            @pl.when(polar == 1)
            def _(dst=dst, step=step, n=n):
                for ref, q in ((wedge, NPOLE + step - 1), (side, NPOLE + step)):
                    ref[n] = with_flux(dst[pl.ds(base_of(q), width), :], q)
                for copy in hist_copies(n, (0, 1)):
                    copy.start()
        src, dst = dst, src

    if first:
        state_rows = row_range(
            lambda q: pltpu.make_async_copy(
                src.at[pl.ds(base_of(q), width)], state.at[q + ROW0], sems.at[1]
            ),
            steps[-1], src, width, sems.at[1],
        )
        for n in range(len(steps)):
            for copy in hist_copies(n, (2, 3)):
                copy.wait()
        turned = jnp.transpose(flux_hist[0])[NPOLE + ROW0 : NPOLE + ROW0 + 8]
        for o in range(width // 128):
            gather_out[8 * o : 8 * o + 8, :] = turned[:, 128 * o : 128 * o + 128]
    else:
        for n in range(len(steps)):
            for copy in hist_copies(n, (2, 3)):
                copy.wait()
        start, extent = (HALO, count) if fast else (0, width)
        first_row = jnp.where(polar == 1, NPOLE + WEDGE, 0)

        @pl.loop(first_row, rows)
        def _(q):
            row = pl.ds(base_of(q), width)
            src[row, :] = with_flux(src[row, :], q)
            pltpu.make_async_copy(
                src.at[pl.ds(base_of(q) + start, extent)], air_out.at[q_of(q)], sems.at[1]
            ).start()

        for kind, count_rows in ((1, rows - NPOLE - WEDGE), (0, rows)):
            @pl.when(polar == kind)
            def _(count_rows=count_rows):
                whole = src.at[pl.ds(0, count_rows * extent)]
                pltpu.make_async_copy(whole, whole, sems.at[1]).wait()

    @pl.when(polar == 1)
    def _():
        for n, step in enumerate(steps):
            if step <= WEDGE:
                for copy in hist_copies(n, (0, 1)):
                    copy.wait()


def outside_steps(rows, count, width, fast, steps, scal, big, small):
    levels = 128
    any_spec = pl.BlockSpec(memory_space=pl.ANY)
    vmem = pl.BlockSpec(memory_space=pltpu.VMEM)
    total = rows + 2 * ROW0
    shape = jax.ShapeDtypeStruct
    square = shape((width, 128), F32)
    hist = [shape((len(steps), width, 128), F32)] * 4
    if steps[0] == 1:
        out_shape = [shape((total, width, levels), F32)] + hist + [square, square]
        out_shape.append(shape((width // 16, 128), F32))
    else:
        out_shape = [shape((rows, count if fast else width, levels), F32)] + hist
    return pl.pallas_call(
        functools.partial(outside_kernel, rows, count, width, fast, steps),
        out_shape=out_shape,
        in_specs=[pl.BlockSpec(memory_space=pltpu.SMEM)]
        + [any_spec] * len(big)
        + [vmem] * len(small),
        out_specs=[any_spec] * 5 + [vmem] * (len(out_shape) - 5),
        scratch_shapes=[
            pltpu.VMEM(((total + BEYOND) * width + 16, levels), F32),
            pltpu.VMEM(((total + BEYOND) * width + 16, levels), F32),
            pltpu.VMEM((2 * width, 2 * levels), BF16),
            pltpu.VMEM((2 * width, 2 * levels), BF16),
            pltpu.VMEM((width, 128), F32),
            pltpu.VMEM((width, 128), F32),
            pltpu.VMEM((width, 128), F32),
            pltpu.VMEM((width, 128), F32),
            pltpu.VMEM((128, width), F32),
            pltpu.VMEM((width + 16, 128), F32),
            pltpu.VMEM((256, 256), BF16),
            pltpu.VMEM((2, ROW0, 8, 128), F32),
            pltpu.VMEM((width, 128), F32),
        ]
        + [pltpu.VMEM((len(steps), width, 128), F32)] * 4
        + [
            pltpu.SemaphoreType.DMA((4 * len(steps),)),
            pltpu.SemaphoreType.DMA((4,)),
        ],
        compiler_params=pltpu.CompilerParams(vmem_limit_bytes=VMEM_LIMIT),
        cost_estimate=pl.CostEstimate(
            flops=len(steps) * rows * width * levels * levels * 4,
            bytes_accessed=rows * width * levels * 10,
            transcendentals=0,
        ),
        name="outside_steps",
    )(scal, *big, *small)


def cap_kernel(rows, count, width, blocks, fast, steps, parts, scal, *refs):
    scal = Place(scal)
    last = steps[-1] == STEPS
    wedge_steps = [step + 1 for step in steps if step < STEPS]
    spec_in, refs = refs[:parts], refs[parts:]
    hists, refs = refs[: 4 * len(cap_hists(steps))], refs[4 * len(cap_hists(steps)) :]
    names = ["free", "t_high", "t_low", "rotate", "coef", "sea", "sea_ring"]
    if steps[0] > 1:
        names += ["gathered", "flux", "ring_flux", "wedge"]
    if last:
        names += list(range(blocks // 2))
    loads = dict(zip(names, refs[: len(names)]))
    refs = refs[len(names) :]
    small_in, refs = refs[:3], refs[3:]
    if last:
        refs = refs[1:]
        (air_out, sea_out), refs = refs[:2], refs[2:]
    else:
        (spec_out, wedge_out, sea_out, flux_out, sea_ring_out, ring_out, gather_to), refs = (
            refs[:7], refs[7:])
    (spec_a, spec_b, cur, prev, xcat, kcat_a, kcat_b, point, sea, flux, pad,
     ring, sea_ring, shares, t_high, t_low, stencil, coef, coef_ring, gathered, sea_hist,
     flux_hist, side, turn, free_top, free_row, vcat, weight, courant, mix, load_sems, row_sems) = refs[:32]
    if last:
        back, free_late, sems = refs[32:]
    else:
        gather_out, store_sems = refs[32:]
    flip, polar, block = scal[0], scal[1], scal[2]
    lanes = lane_iota((width, 128))
    own = pl.ds(pl.multiple_of(block * width, 128), width)

    def hist(kind, step):
        half = 0 if step <= SPLIT else 1
        return hists[4 * cap_hists(steps).index(half) + kind].at[step - 1 - SPLIT * half]

    def own_dot(x):
        return table_dot(t_high[own, :], t_low[own, :], x)

    def wedge_step(step):
        at = wedge_steps.index(step)
        pending = flux_hist[at]
        for j in range(step - 1):
            base = 8 + j * width
            if j == step - 2:
                south_ref, south = side.at[at], 0
            else:
                south_ref, south = cur, base + width
            advance(width, cur, base, prev, 0, south_ref, south, winds(courant)[:2], xcat)
            prev[...] = cur[pl.ds(base, width), :]
            mixed = dot(xcat[...], vcat[...])
            y = mixed[:, :128] + mixed[:, 128:]
            lane = NPOLE + j + ROW0
            out = exchange(y, lane, sea[...], coef[...])
            cur[pl.ds(base, width), :] = y + air_gain * out
            pending += pltpu.roll(out, lane, 1)
        return pending

    def cap_step(step, src, dst, slot):
        count_rows = CAP - step
        if step > 1:
            ready("gathered", "sea_ring", "ring_flux")
        if step > 1:
            for j in range(blocks):
                ring[pl.ds(NPOLE, 8), pl.ds(j * width, width)] = gathered[
                    j, pl.ds(8 * slot, 8), :
                ]
            old, at = sea_ring[...], ring[...]
            place = lax.broadcasted_iota(jnp.int32, old.shape, 0)
            up = jnp.where(place == 0, 0.0, pltpu.roll(old, 1, 0))
            down = pltpu.roll(old, old.shape[0] - 1, 0)
            ring_width = blocks * width
            around = up + down + pltpu.roll(old, 1, 1) + pltpu.roll(old, ring_width - 1, 1)
            sea_ring[...] = old - ocean_gain * at + ocean_diffusion * (around - 4.0 * old)
            spot = lane_iota(at.shape) % width
            at = jnp.where((spot >= HALO) & (spot < HALO + count), at, 0.0)
            high, low = two_parts(at)
            ready("t_high", "t_low", "rotate", "weight")
            both = dot(jnp.concatenate([high, low], axis=0), t_high[...])
            sums = both[:24] + both[24:] + dot(high, t_low[...])
            sums = sums * (air_gain * weight[0:1, :])
            sums = jnp.concatenate([sums, jnp.zeros((104, NK), F32)], axis=0)
            moved = jnp.transpose(sums)
            swapped = jnp.concatenate([moved[128:], moved[:128]], axis=0)
            beside = pltpu.roll(moved, 1, 1) + pltpu.roll(moved, 127, 1)
            top = jnp.broadcast_to(courant[0:1, 0:1], (1, 128))
            shares[...] = (
                stencil[0] * moved + diffusion_rate * beside + (stencil[2] * top) * swapped
            )
            stencil[1] = stencil[2] * courant[0:1, :]

        point[...] = jnp.zeros_like(point)
        kcats = (kcat_a, kcat_b)
        first = lane_iota((128, 128)) == 0

        def load(q, slot):
            cut = scal[3 + q]
            for o, other in ((0, 128), (128, 0)):
                more = pltpu.roll(shares[pl.ds(o, 128), :], lax.rem(128 - q, 128), 1)
                x = jnp.where(first, more, 0.0)
                if step > 2:
                    here = src[q + 1, pl.ds(o, 128), :]
                    swapped = src[q + 1, pl.ds(other, 128), :]
                    around = src[q, pl.ds(o, 128), :] + src[q + 2, pl.ds(o, 128), :]
                    x += (
                        stencil[0, pl.ds(o, 128), :] * here
                        + diffusion_rate * around
                        + stencil[1, pl.ds(o, 128), :] * swapped
                    )
                x = jnp.where(lax.broadcasted_iota(jnp.int32, x.shape, 0) <= cut, x, 0.0)
                high, low = two_parts(x)
                kcats[slot][pl.ds(o, 128), 0:128] = high
                kcats[slot][pl.ds(o, 128), 128:256] = low

        streamed = step == steps[0] and step > 1

        def finish(q, slot, between):
            mixed = dot(kcats[slot][...], vcat[...])
            between()
            y = mixed[:, :128] + mixed[:, 128:]
            dst[q + 1] = y
            point[...] += pltpu.roll(jnp.where(lane_iota(y.shape) == 0, y, 0.0), q, 1)

        pairs = (count_rows + 1) // 2
        if streamed:
            spec_row(0).wait()
            spec_row(1).wait()

        def arrive(n):
            spec_row(2 * n + 2).wait()
            spec_row(2 * n + 3).wait()

        if step > 1:
            two_at_a_time(0, pairs, load, finish, arrive if streamed else None)
        if streamed:
            for q in range(2 * pairs + 2, CAP):
                spec_row(q).wait()
        if step == steps[-1] and not last:
            store(dst.at[pl.ds(1, CAP)], spec_out)
        ready("free")
        top = pltpu.roll(free_top[...], (128 - NPOLE * (step - 1)) % 128, 1)
        point[...] += jnp.where(lane_iota((NK, 128)) < NPOLE, top, 0.0)

        ready("t_high", "t_low", "sea_ring", "coef_ring", "coef", "sea", "flux", "hist")
        at_rows = jnp.transpose(point[...])[:NPOLE]
        high, low = two_parts(at_rows)
        both = dot_nt(jnp.concatenate([high, low], axis=0), t_high[...])
        surface = both[:NPOLE] + both[NPOLE:] + dot_nt(high, t_low[...])
        ring[0:NPOLE, :] = coef_ring[...] * (sea_ring[0:NPOLE, :] - surface)

        here = pltpu.roll(own_dot(point[...]), ROW0, 1)
        in_cap = (lanes >= ROW0) & (lanes < ROW0 + NPOLE)
        total = jnp.where(in_cap, coef[...] * (sea[...] - here), flux[...])
        flux[...] = total
        if step < STEPS:
            edge = pltpu.roll(total, 128 - (ROW0 + NPOLE - 1), 1)
            row = free_row[slot] if step == 1 else dst[NPOLE] + free_row[slot]
            prev[...] = own_dot(row) + air_gain * jnp.where(lanes == 0, edge, 0.0)
        new = sea_next(width, polar, rows, sea[...], total, pad)
        sea[...] = jnp.where(lanes >= ROW0 + NPOLE + step - 1, sea_hist[slot], new)

    copies = {}
    order = []
    stores = []

    def store(source, target):
        copy = pltpu.make_async_copy(source, target, store_sems.at[len(stores)])
        stores.append(copy)
        copy.start()

    def fetch(name, source, target):
        copy = pltpu.make_async_copy(source, target, load_sems.at[len(order)])
        order.append(copy)
        copies.setdefault(name, []).append(copy)
        copy.start()

    def ready(*wanted):
        for name in wanted:
            for copy in copies.pop(name, ()):
                copy.wait()

    def spec_row(q):
        return pltpu.make_async_copy(spec_in[0].at[q], spec_a.at[q + 1], row_sems.at[q])

    @pl.when(polar == 1)
    def _():
        for n, (source, target) in enumerate(zip(small_in, (weight, courant, mix))):
            fetch(("weight", "courant", "mix")[n], source, target)
        if steps[0] > 1:
            fetch("gathered", loads["gathered"], gathered)
            fetch("sea_ring", loads["sea_ring"], sea_ring)
            fetch("ring_flux", loads["ring_flux"], ring.at[pl.ds(0, NPOLE)])
        fetch("t_high", loads["t_high"], t_high)
        fetch("t_low", loads["t_low"], t_low)
        fetch("rotate", loads["rotate"].at[0], stencil.at[0])
        fetch("rotate", loads["rotate"].at[1], stencil.at[2])
        if steps[0] > 1:
            @pl.loop(0, CAP)
            def _(q):
                spec_row(q).start()

        part = NK // blocks
        some = part // 2
        rows_15 = [step for step in steps if step < STEPS]
        for i in range(blocks):
            owner = (i % 2) * (blocks // 2) + i // 2
            for n in range(2):
                at = pl.ds(KMAX * n + n + some * owner, some)
                take = pl.ds(some * n, some)
                fetch("free", loads["free"].at[i, take], free_top.at[at])
                for slot, step in enumerate(rows_15):
                    take = pl.ds(part * step + some * n, some)
                    fetch("free", loads["free"].at[i, take], free_row.at[slot, at])
        if last:
            side_y, place_z = lax.rem(block, 2), block // 2
            for z in range(blocks // 2):
                for y in range(2):
                    owner = (blocks // 2) * jnp.bitwise_xor(side_y, y) + jnp.bitwise_xor(place_z, z)
                    for n in range(2):
                        at = pl.multiple_of((KMAX + 1) * n + some * owner, some)
                        fetch(
                            "late",
                            loads[z].at[y, :, pl.ds(some * n, some)],
                            free_late.at[:, pl.ds(at, some)],
                        )
        if steps[0] == 1:
            fetch("sea_ring", loads["sea_ring"], sea_ring)
            for i in range(blocks):
                for o in range(width // 128):
                    fetch(
                        "gathered",
                        loads["free"].at[i, pl.ds(STEPS * part + 8 * o, 8)],
                        gathered.at[i, pl.ds(8, 8), pl.ds(128 * o, 128)],
                    )
        for i in range(blocks):
            for o in range(width // 128):
                at = STEPS * (NK // blocks) + width // 16 + NPOLE * o
                fetch(
                    "coef_ring",
                    loads["free"].at[i, pl.ds(at, NPOLE)],
                    coef_ring.at[:, pl.ds(i * width + 128 * o, 128)],
                )
        fetch("coef", loads["coef"], coef)
        fetch("sea", loads["sea"], sea)
        fetch("flux", loads["flux"] if steps[0] > 1 else hist(3, 1), flux)
        for n, step in enumerate(steps):
            fetch("hist", hist(2, step), sea_hist.at[n])
        for n, step in enumerate(wedge_steps):
            fetch("hist", hist(3, step), flux_hist.at[n])
            fetch("hist", hist(1, step - 1), side.at[n])
            row = pl.ds(8 + (step - 2) * width, width)
            fetch("hist", hist(0, step - 1), cur.at[row])
        kept = steps[0] - 1
        for j in range(kept):
            fetch("hist", loads["wedge"].at[j], cur.at[pl.ds(8 + j * width, width)])
        ready("mix", "courant")
        mixing(mix, vcat)
        for ref in (spec_a, spec_b):
            ref[0] = jnp.zeros((NK, 128), F32)
            for beyond in range(CAP + 1, CAP + 4):
                ref[beyond] = jnp.zeros((NK, 128), F32)
        cur[0:8, :] = jnp.zeros((8, 128), F32)
        pad[...] = jnp.zeros_like(pad)

        src, dst = spec_a, spec_b
        for n, step in enumerate(steps):
            cap_step(step, src, dst, n)
            src, dst = dst, src
            if step < STEPS:
                pending = wedge_step(step + 1)
                flux[...] = pending
                if not last:
                    turned = jnp.transpose(pending)[NPOLE + ROW0 : NPOLE + ROW0 + 8]
                    for to in range(blocks):
                        gather_out[to, pl.ds(8 * n, 8), :] = turned
        ready(*list(copies))
        if last:
            start, extent = (HALO, count) if fast else (0, width)

            def send(ref, offset, q):
                r = jnp.where(flip == 1, rows - 1 - q, q)
                return pltpu.make_async_copy(
                    ref.at[pl.ds(offset + start, extent)], air_out.at[r], sems.at[q]
                )

            for j in range(WEDGE):
                send(cur, 8 + j * width, NPOLE + j).start()

            @pl.loop(0, NPOLE // 2)
            def _(pair):
                parts_of = [two_parts(src[2 * pair + n + 1] + free_late[2 * pair + n])
                            for n in range(2)]
                highs = jnp.concatenate([high for high, _ in parts_of], axis=1)
                crossed = dot(t_low[own, :], highs)
                for n, (high, low) in enumerate(parts_of):
                    q = 2 * pair + n
                    both = dot(t_high[own, :], jnp.concatenate([high, low], axis=1))
                    y = both[:, :128] + both[:, 128:] + crossed[:, 128 * n : 128 * n + 128]
                    edge = pltpu.roll(flux[...], lax.rem(128 - ROW0 - q, 128), 1)
                    back[q] = y + air_gain * jnp.where(lanes == 0, edge, 0.0)
                    send(back.at[q], 0, q).start()

            @pl.loop(0, NPOLE)
            def _(q):
                send(back.at[q], 0, q).wait()

            for j in range(WEDGE):
                send(cur, 8 + j * width, NPOLE + j).wait()
        else:
            for j in range(len(wedge_steps) + kept):
                store(cur.at[pl.ds(8 + j * width, width)], wedge_out.at[j])
            for source, target in (
                (sea, sea_out), (flux, flux_out), (sea_ring, sea_ring_out),
                (ring.at[pl.ds(0, NPOLE)], ring_out), (gather_out, gather_to),
            ):
                store(source, target)
            for copy in stores:
                copy.wait()

    if last:
        @pl.when(polar == 0)
        def _():
            copy = pltpu.make_async_copy(hist(2, STEPS), sea, load_sems.at[0])
            copy.start()
            copy.wait()

        turn[...] = jnp.transpose(pltpu.roll(sea[...], width - HALO, 0))

        @pl.loop(0, rows)
        def _(q):
            r = jnp.where(flip == 1, rows - 1 - q, q)
            sea_out[pl.ds(r, 1), :] = turn[pl.ds(q + ROW0, 1), pl.ds(0, count)]


def cap_hists(steps):
    return ([0] if steps[0] <= SPLIT + 1 else []) + ([1] if steps[-1] + 1 > SPLIT else [])


def cap_steps(rows, count, width, blocks, fast, steps, scal, spec, big, small, air):
    levels = 128
    ring_width = blocks * width
    last = steps[-1] == STEPS
    any_spec = pl.BlockSpec(memory_space=pl.ANY)
    vmem = pl.BlockSpec(memory_space=pltpu.VMEM)
    shape = jax.ShapeDtypeStruct
    square = pltpu.VMEM((width, 128), F32)
    aliases = {}
    extra = []
    if last:
        out_shape = [
            shape((rows, count if fast else width, levels), F32),
            shape((rows, count), F32),
        ]
        out_specs = [any_spec, vmem]
        extra = [
            pltpu.VMEM((NPOLE, width, levels), F32),
            pltpu.VMEM((NPOLE, NK, levels), F32),
            pltpu.SemaphoreType.DMA((NPOLE + WEDGE,)),
        ]
        aliases = {1 + len(spec) + len(big) + len(small): 0}
    else:
        out_shape = [
            shape((CAP, NK, levels), F32),
            shape((steps[-1], width, levels), F32),
            shape((width, 128), F32),
            shape((width, 128), F32),
            shape((24, ring_width), F32),
            shape((NPOLE, ring_width), F32),
            shape((blocks, 16, width), F32),
        ]
        out_specs = [any_spec] * 7
        extra = [pltpu.VMEM((blocks, 16, width), F32), pltpu.SemaphoreType.DMA((16,))]
    return pl.pallas_call(
        functools.partial(cap_kernel, rows, count, width, blocks, fast, steps, len(spec)),
        out_shape=out_shape,
        in_specs=[pl.BlockSpec(memory_space=pltpu.SMEM)]
        + [any_spec] * (len(spec) + len(big))
        + [any_spec] * (len(small) + len(air)),
        out_specs=out_specs,
        scratch_shapes=[
            pltpu.VMEM((CAP + 4, NK, levels), F32),
            pltpu.VMEM((CAP + 4, NK, levels), F32),
            pltpu.VMEM((WEDGE * width + 16, levels), F32),
            square,
            pltpu.VMEM((width, 2 * levels), BF16),
            pltpu.VMEM((NK, 2 * levels), BF16),
            pltpu.VMEM((NK, 2 * levels), BF16),
            pltpu.VMEM((NK, 128), F32),
            square,
            square,
            pltpu.VMEM((width + 16, 128), F32),
            pltpu.VMEM((24, ring_width), F32),
            pltpu.VMEM((24, ring_width), F32),
            pltpu.VMEM((NK, 128), F32),
            pltpu.VMEM((ring_width, NK), BF16),
            pltpu.VMEM((ring_width, NK), BF16),
            pltpu.VMEM((3, NK, levels), F32),
            square,
            pltpu.VMEM((NPOLE, ring_width), F32),
            pltpu.VMEM((blocks, 16, width), F32),
            pltpu.VMEM((2, width, 128), F32),
            pltpu.VMEM((2, width, 128), F32),
            pltpu.VMEM((2, width, 128), F32),
            pltpu.VMEM((128, width), F32),
            pltpu.VMEM((NK, 128), F32),
            pltpu.VMEM((2, NK, 128), F32),
            pltpu.VMEM((256, 256), BF16),
            pltpu.VMEM((8, NK), F32),
            pltpu.VMEM((1, 128), F32),
            pltpu.VMEM((128, 128), F32),
            pltpu.SemaphoreType.DMA((13 * blocks + 32,)),
            pltpu.SemaphoreType.DMA((CAP,)),
        ]
        + extra,
        input_output_aliases=aliases,
        compiler_params=pltpu.CompilerParams(vmem_limit_bytes=VMEM_LIMIT),
        cost_estimate=pl.CostEstimate(
            flops=len(steps) * CAP * NK * levels * levels * 4,
            bytes_accessed=20_000_000,
            transcendentals=0,
        ),
        name="cap_steps",
    )(scal, *spec, *big, *small, *air)


def shift(x, axis, by, wrap):
    size = lax.axis_size(axis)
    pairs = [(i, (i + by) % size) for i in range(size) if wrap or 0 <= i + by < size]
    return lax.ppermute(x, axis, pairs)


def between_caps(x, by):
    size, bands = lax.axis_size("lon"), lax.axis_size("lat")
    pairs = [(b * size + i, b * size + (i ^ by)) for b in (0, bands - 1) for i in range(size)]
    return lax.ppermute(x, ("lat", "lon"), pairs)


def spread(copies):
    return lax.all_to_all(copies, "lon", split_axis=0, concat_axis=0, tiled=True)


def local(air_temp, sea_temp, land_sea, courant, vertical_mix, cutoffs):
    rows, count, levels = air_temp.shape
    blocks = lax.axis_size("lon")
    nlon = blocks * count
    width = round_up(count + 2 * HALO, 128)
    depth = round_up(count, 128)
    fast = count % 8 == 0
    scal = cutoffs

    window, forward, weight = tables(blocks, count, width, depth)
    t_high, t_low = (jnp.asarray(part) for part in window)
    rotate = rotations(nlon)
    rotate_owned = jnp.asarray(rotate[:, owner_order(blocks)])
    rotate = jnp.asarray(rotate)
    weights = jnp.asarray(np.tile(weight.astype(np.float32), (8, 1)))
    courant = courant.reshape(1, levels)

    west = shift(air_temp[:, count - HALO :], "lon", 1, True)
    east = shift(air_temp[:, :HALO], "lon", -1, True)
    mine = shares_of_sea(rows, count, blocks, sea_temp, land_sea)
    half = blocks // 2
    keep, send = start_spectra(blocks, scal, air_temp, jnp.asarray(forward))
    mine, west, east = lax.optimization_barrier((mine, west, east))
    got = spread(mine)

    taken = between_caps(send, 1)
    half_sum = [keep[j] + taken[j] for j in range(half)]

    outs = windows(
        rows, count, width, blocks, fast, scal, got, land_sea, air_temp, west, east
    )
    own_window, sea_ring, cap_coef = outs[:3]
    if fast:
        last_rows, first_rows = outs[3:]
    else:
        def edge(part):
            extra = own_window[:, part].transpose(1, 0, 2).reshape(ROW0, -1, levels)
            at, after = edge_extent(count, width)
            row = jnp.concatenate([west[part], air_temp[part], east[part]], 1)
            row = jnp.pad(row, ((0, 0), (0, at - row.shape[1]), (0, 0)))
            extra = jnp.pad(extra, ((0, 0), (0, after - at - extra.shape[1]), (0, 0)))
            return jnp.concatenate([row, extra], 1)

        last_rows, first_rows = edge(slice(rows - ROW0, rows)), edge(slice(0, ROW0))
    north = shift(last_rows, "lat", 1, False)
    south = shift(first_rows, "lat", -1, False)

    if fast:
        air = air_temp
    else:
        middle = jnp.concatenate([west, air_temp, east], 1)
        inner = count + 2 * HALO
        air = jnp.concatenate([north[:, :inner], middle, south[:, :inner]], 0)
        air = jnp.pad(air, ((0, 0), (0, width - count - 2 * HALO), (0, 0)))
    half_sum, own_window = lax.optimization_barrier((half_sum, own_window))
    parts = [between_caps(half_sum[j], 2 * j) for j in range(1, half)]
    outs = outside_steps(
        rows, count, width, fast, tuple(range(1, SPLIT + 1)), scal, (air, west, east, north, south),
        (own_window, courant, vertical_mix),
    )
    state, early, sea, coef, gathered = outs[0], tuple(outs[1:5]), outs[5], outs[6], outs[7]
    parts, state = lax.optimization_barrier((parts, state))
    gathered, late_free = free_steps(
        blocks, scal, (half_sum[0], *parts), rotate_owned, courant, vertical_mix, gathered,
        cap_coef,
    )
    gathered, state = lax.optimization_barrier((gathered, state))
    late_pair = jnp.stack([late_free, between_caps(late_free, 1)])
    free = spread(gathered)
    outs = outside_steps(
        rows, count, width, fast, tuple(range(SPLIT + 1, STEPS + 1)), scal,
        (state, early[2], early[3], coef), (courant, vertical_mix),
    )
    air, late = outs[0], tuple(outs[1:5])
    free, air, late = lax.optimization_barrier((free, air, late))

    more, spec = (), ()
    for steps in ((1, 2), (3, 4), (5, 6)):
        hists = sum(((early, late)[h] for h in cap_hists(steps)), ())
        big = hists + (free, t_high, t_low, rotate, coef, sea, sea_ring) + more
        if steps[-1] == STEPS:
            big += tuple(late_free)
        outs = cap_steps(
            rows, count, width, blocks, fast, steps, scal, spec, big,
            (weights, courant, vertical_mix), (air,) if steps[-1] == STEPS else (),
        )
        if steps[-1] < STEPS:
            spec, wedge, sea, flux, sea_ring, ring_flux, mine = outs
            if steps[0] == 1:
                late_pair, mine = lax.optimization_barrier((late_pair, mine))
                late_free = [late_pair] + [
                    between_caps(late_pair, 2 * j) for j in range(1, half)
                ]
            gathered = spread(mine)
            spec, more = (spec,), (gathered, flux, ring_flux, wedge)
    air, sea = outs
    if not fast:
        air = air[:, HALO : HALO + count]
    sea = lax.all_to_all(sea, "lon", split_axis=0, concat_axis=1, tiled=True)
    return air, sea


def solution(mesh):
    placed = (P("lat", "lon", None), P(("lat", "lon"), None), P("lat", "lon"), P(), P(), P())
    return jax.shard_map(
        local,
        mesh=mesh,
        in_specs=placed,
        out_specs=(P("lat", "lon", None), P(("lat", "lon"), None)),
        check_vma=False,
    )
```
